512 devices in a mesh: ctx: 64 (over z_lo, y, core), ch: 8 (over x, z_hi).
Axes of the slice: x: 4, y: 4, z: 16 (z_hi: 2, z_lo: 8; z = z_hi * 8 + z_lo), core: 2. Of those that a mesh axis runs over, the one named last changes fastest.
Arguments:
- gate_input: bfloat16 [16384, 4096], P('ctx', 'ch'), may hold values from -6 to 6
- key_input: bfloat16 [16384, 4096], P('ctx', 'ch'), may hold values from -6 to 6
- value_input: bfloat16 [16384, 4096], P('ctx', 'ch'), may hold values from -6 to 6
- out_grad: bfloat16 [16384, 4096], P(('ctx', 'ch')), may hold values from -6 to 6
- filter_taps: bfloat16 [768, 4096], P(None, 'ch'), may hold values from -6 to 6
Outputs:
- gate_grad: bfloat16 [16384, 4096], P('ctx', 'ch')
- key_grad: bfloat16 [16384, 4096], P('ctx', 'ch')
- value_grad: bfloat16 [16384, 4096], P('ctx', 'ch')
- filter_grad: float32 [768, 4096], P('ctx', 'ch')
The draws below stay inside these ranges and needn't reach their ends.
All inputs are finite; a program needn't handle non-finite values.
Results may differ from the reference program's by a relative error of at most 0.012.
Values may be sent and summed in bfloat16 or wider, within the bound.
No kernel may reach another device: no remote copies, remote signals or barrier semaphores. Data moves between devices by JAX's collectives and lax.ppermute only.
A program may use at most 64 MiB of HBM per device.

```python
import jax
import jax.numpy as jnp
from jax import lax

CW = 4096
FILTER_LEN = 768
TOKENS = 16384


def level_of(stream_key, dims, split, least, largest):
    def one(axis_at, blocks):
        heights = jax.random.uniform(jax.random.fold_in(jax.random.fold_in(stream_key, 6), axis_at), (blocks,), jnp.float32, least / len(split), largest / len(split))
        return jnp.repeat(jnp.exp(heights), dims[axis_at] // blocks).reshape((-1,) + (1,) * (len(dims) - axis_at - 1))

    factor_of = one(*split[0])
    for cut in split[1:]:
        factor_of = factor_of * one(*cut)
    return factor_of


def noise(rng, shape, spread, most, split=(), held_as=jnp.bfloat16):
    gain = level_of(rng, shape, split, -0.22, 0.18) if split else 1.0
    drawn = jax.random.normal(rng, shape, jnp.float32) * spread * gain
    return jnp.minimum(jnp.maximum(drawn, -most), most).astype(held_as)


def setup_inputs(seed: int = 0) -> dict:
    keys = jax.random.split(jax.random.key(seed), 6)
    return {
        "gate_input": noise(keys[0], (TOKENS, CW), 1.0, 6.0, ((0, 64), (1, 8))),
        "key_input": noise(keys[1], (TOKENS, CW), 1.0, 6.0, ((0, 64), (1, 8))),
        "value_input": noise(keys[2], (TOKENS, CW), 1.0, 6.0, ((0, 64), (1, 8))),
        "out_grad": noise(keys[3], (TOKENS, CW), 1.0, 6.0, ((0, 512),)),
        "filter_taps": noise(keys[4], (FILTER_LEN, CW), 1.0, 6.0, ((1, 8),)),
    }


def block_transforms(blocks):
    mixed_block, grad_block, taps_block = blocks
    total = TOKENS + FILTER_LEN
    length = 1 << (total - 1).bit_length()
    mixed_f = jnp.fft.rfft(mixed_block, length, axis=0)
    grad_f = jnp.fft.rfft(grad_block, length, axis=0)
    taps_f = jnp.fft.rfft(taps_block, length, axis=0)
    conv_out = jnp.fft.irfft(mixed_f * taps_f, length, axis=0)[:TOKENS]
    grad_mixed = jnp.fft.irfft(grad_f * jnp.conj(taps_f), length, axis=0)[:TOKENS]
    lag_grad = jnp.fft.irfft(grad_f * jnp.conj(mixed_f), length, axis=0)[:FILTER_LEN]
    return conv_out, grad_mixed, lag_grad


def split_blocks(array, width):
    return array.reshape(array.shape[0], CW // width, width).transpose(1, 0, 2)


def join_blocks(array):
    return array.transpose(1, 0, 2).reshape(array.shape[1], CW)


def reference(gate_input, key_input, value_input, out_grad, filter_taps):
    mixed_in = (key_input.astype(jnp.float32) * value_input.astype(jnp.float32)).astype(jnp.bfloat16)
    grad_conv = (out_grad.astype(jnp.float32) * gate_input.astype(jnp.float32)).astype(jnp.bfloat16)
    scale = 1.0 / (FILTER_LEN ** 0.5)
    taps = filter_taps.astype(jnp.float32) * scale
    width = min(CW, 256)
    conv_out, grad_mixed, lag_grad = lax.map(
        block_transforms,
        (split_blocks(mixed_in.astype(jnp.float32), width),
         split_blocks(grad_conv.astype(jnp.float32), width),
         split_blocks(taps, width)))
    conv_out = join_blocks(conv_out)
    grad_mixed = join_blocks(grad_mixed)
    lag_grad = join_blocks(lag_grad)
    gate_grad = (out_grad.astype(jnp.float32) * conv_out).astype(jnp.bfloat16)
    key_grad = (grad_mixed * value_input.astype(jnp.float32)).astype(jnp.bfloat16)
    value_grad = (grad_mixed * key_input.astype(jnp.float32)).astype(jnp.bfloat16)
    filter_grad = lag_grad * scale
    return gate_grad, key_grad, value_grad, filter_grad
```

```python
import functools
import math

import jax
import jax.numpy as jnp
import ml_dtypes
import numpy as np
from jax import lax
from jax.experimental import pallas as pl
from jax.experimental.pallas import tpu as pltpu
from jax.sharding import Mesh, PartitionSpec as P

BF16 = jnp.bfloat16
F32 = jnp.float32
AXES = ("z", "yh", "yl", "c", "x", "zh")
SIZES = (8, 2, 2, 2, 4, 2)
CTX = ("z", "yh", "yl", "c")
GROUP = ("yl", "c")
RUNS = ("z", "yh")
CH = ("x", "zh")

BLOCK = 256
PERIOD = 1024
LANES = 128
BLOCKS = 4
BINS = 128
STEPS = PERIOD // 2 // BINS
ROWS = 2 * BINS


def make_tables():
    freq = np.arange(PERIOD // 2)[:, None]
    place = np.arange(PERIOD)[None, :]
    angle = math.pi / PERIOD * ((2 * freq + 1) * place % (2 * PERIOD)).astype(np.float64)
    both = np.stack([np.cos(angle), -np.sin(angle)])
    both = both.reshape(2, STEPS, BINS, PERIOD).transpose(1, 0, 2, 3).reshape(PERIOD, PERIOD)
    return both.astype(ml_dtypes.bfloat16), np.ascontiguousarray(both.T).astype(ml_dtypes.bfloat16)


def dot(a, b):
    return jnp.dot(a, b, preferred_element_type=F32)


def spread(part):
    return jnp.concatenate([part] * BLOCKS, axis=1)


def fill_windows(windows, source):
    for block in range(BLOCKS):
        windows[:, block * LANES : (block + 1) * LANES] = source[
            block * BLOCK : block * BLOCK + PERIOD, :
        ]


def conv_kernel(scale, forward, inverse, mixed, taps, conv, spectrum, response, windows, total):
    step = pl.program_id(0)

    @pl.when(step == 0)
    def _():
        fill_windows(windows, mixed)

    resp = dot(forward[:, : taps.shape[0]], taps[...])
    response[...] = resp
    spec = dot(forward[...], windows[...])
    spectrum[...] = spec
    f_re, f_im = spread(resp[:BINS]), spread(resp[BINS:])
    x_re, x_im = spec[:BINS], spec[BINS:]
    y = jnp.concatenate([f_re * x_re - f_im * x_im, f_re * x_im + f_im * x_re]).astype(BF16)
    part = dot(inverse[...], y)

    @pl.when(step == 0)
    def _():
        total[...] = part

    @pl.when(step > 0)
    def _():
        total[...] += part

    @pl.when(step == STEPS - 1)
    def _():
        for block in range(BLOCKS):
            conv[block * BLOCK : (block + 1) * BLOCK, :] = (
                total[:, block * LANES : (block + 1) * LANES] * scale
            )


def cross_kernel(scale, forward, inverse, grad, spectrum, lag_grad, windows, total):
    step = pl.program_id(0)

    @pl.when(step == 0)
    def _():
        for block in range(BLOCKS):
            windows[:, block * LANES : (block + 1) * LANES] = grad[
                block * BLOCK : (block + 1) * BLOCK, :
            ]

    spec = dot(forward[...], windows[...])
    g_re, g_im = spec[:BINS], spec[BINS:]
    x_re, x_im = spectrum[:BINS], spectrum[BINS:]
    re = g_re * x_re + g_im * x_im
    im = g_im * x_re - g_re * x_im
    re = sum(re[:, b * LANES : (b + 1) * LANES] for b in range(BLOCKS))
    im = sum(im[:, b * LANES : (b + 1) * LANES] for b in range(BLOCKS))
    part = dot(inverse[...], jnp.concatenate([re, im]).astype(BF16))

    @pl.when(step == 0)
    def _():
        total[...] = part

    @pl.when(step > 0)
    def _():
        total[...] += part

    @pl.when(step == STEPS - 1)
    def _():
        lag_grad[...] = (total[...] * scale).astype(BF16)


def back_kernel(scale, forward, inverse, grad, response, back, windows, total):
    step = pl.program_id(0)

    @pl.when(step == 0)
    def _():
        fill_windows(windows, grad)

    spec = dot(forward[...], windows[...])
    f_re, f_im = spread(response[:BINS]), spread(response[BINS:])
    g_re, g_im = spec[:BINS], spec[BINS:]
    y = jnp.concatenate([f_re * g_re + f_im * g_im, f_re * g_im - f_im * g_re]).astype(BF16)
    part = dot(inverse[...], y)

    @pl.when(step == 0)
    def _():
        total[...] = part

    @pl.when(step > 0)
    def _():
        total[...] += part

    @pl.when(step == STEPS - 1)
    def _():
        for block in range(BLOCKS):
            back[block * BLOCK : (block + 1) * BLOCK, :] = (
                total[:, block * LANES : (block + 1) * LANES] * scale
            ).astype(BF16)


def whole(shape):
    return pl.BlockSpec(shape, lambda step: (0,) * len(shape))


def call(kernel, in_specs, out_specs, out_shape, scratch, macs, moved):
    return pl.pallas_call(
        kernel,
        grid=(STEPS,),
        in_specs=in_specs,
        out_specs=out_specs,
        out_shape=out_shape,
        scratch_shapes=scratch,
        compiler_params=pltpu.CompilerParams(
            dimension_semantics=("arbitrary",), vmem_limit_bytes=24 * 1024 * 1024
        ),
        cost_estimate=pl.CostEstimate(flops=2 * macs, bytes_accessed=moved, transcendentals=0),
    )


def shift(value, steps):
    count = lax.axis_size(RUNS)
    first, last = max(0, -steps), min(count, count - steps)
    return lax.ppermute(value, RUNS, [(i, i + steps) for i in range(first, last)])


def exchange(value, axes):
    return lax.all_to_all(value, axes, split_axis=0, concat_axis=0, tiled=True)


def body(forward, inverse, gate_input, key_input, value_input, out_grad, filter_taps):
    lags = filter_taps.shape[0]
    tokens = BLOCKS * BLOCK
    wide = BLOCKS * LANES
    norm = 2.0 / PERIOD / lags**0.5
    held = out_grad.shape[0]
    pieces = out_grad.reshape(held, -1, BLOCKS, LANES).transpose(2, 1, 0, 3)
    cotangent = exchange(pieces.reshape(-1, held, LANES), GROUP + CH).reshape(tokens, LANES)
    by_quarter = lambda a: a.reshape(BLOCK, BLOCKS, LANES).transpose(1, 0, 2)
    mixed = (key_input.astype(F32) * value_input.astype(F32)).astype(BF16)
    mixed = exchange(by_quarter(mixed), GROUP).reshape(tokens, LANES)
    gate = exchange(by_quarter(gate_input), GROUP).reshape(tokens, LANES)
    mixed_window = jnp.concatenate([shift(mixed[tokens - lags :], 1), mixed])
    quarter = lax.axis_index(GROUP)
    taps = lax.dynamic_slice_in_dim(filter_taps, quarter * LANES, LANES, 1)

    conv, spectrum, response = call(
        functools.partial(conv_kernel, norm),
        [
            pl.BlockSpec((ROWS, PERIOD), lambda step: (step, 0)),
            pl.BlockSpec((BLOCK, ROWS), lambda step: (lags // BLOCK, step)),
            whole((tokens + lags, LANES)),
            whole((lags, LANES)),
        ],
        [
            whole((tokens, LANES)),
            pl.BlockSpec((ROWS, wide), lambda step: (step, 0)),
            pl.BlockSpec((ROWS, LANES), lambda step: (step, 0)),
        ],
        [
            jax.ShapeDtypeStruct((tokens, LANES), F32),
            jax.ShapeDtypeStruct((PERIOD, wide), F32),
            jax.ShapeDtypeStruct((PERIOD, LANES), F32),
        ],
        [pltpu.VMEM((PERIOD, wide), BF16), pltpu.VMEM((BLOCK, wide), F32)],
        PERIOD * (PERIOD * wide + lags * LANES + BLOCK * wide),
        6_000_000,
    )(forward, inverse, mixed_window, taps)

    grad = (cotangent.astype(F32) * gate.astype(F32)).astype(BF16)
    grad_window = jnp.concatenate([grad, shift(grad[:lags], -1)])

    lag_grad = call(
        functools.partial(cross_kernel, norm),
        [
            pl.BlockSpec((ROWS, BLOCK), lambda step: (step, lags // BLOCK)),
            pl.BlockSpec((lags, ROWS), lambda step: (0, step)),
            whole((tokens, LANES)),
            pl.BlockSpec((ROWS, wide), lambda step: (step, 0)),
        ],
        whole((lags, LANES)),
        jax.ShapeDtypeStruct((lags, LANES), BF16),
        [pltpu.VMEM((BLOCK, wide), BF16), pltpu.VMEM((lags, LANES), F32)],
        PERIOD * (BLOCK * wide + lags * LANES),
        4_000_000,
    )(forward, inverse, grad, spectrum)
    share = lags // lax.axis_size(CTX)
    parts = exchange(lag_grad.reshape(-1, share, LANES), CTX)
    filter_grad = parts.reshape(-1, BLOCKS, share, LANES).astype(F32).sum(0)
    filter_grad = filter_grad.transpose(1, 0, 2).reshape(share, wide)

    back = call(
        functools.partial(back_kernel, norm),
        [
            pl.BlockSpec((ROWS, PERIOD), lambda step: (step, 0)),
            pl.BlockSpec((BLOCK, ROWS), lambda step: (0, step)),
            whole((tokens + lags, LANES)),
            pl.BlockSpec((ROWS, LANES), lambda step: (step, 0)),
        ],
        whole((tokens, LANES)),
        jax.ShapeDtypeStruct((tokens, LANES), BF16),
        [pltpu.VMEM((PERIOD, wide), BF16), pltpu.VMEM((BLOCK, wide), F32)],
        PERIOD * (PERIOD * wide + BLOCK * wide),
        4_000_000,
    )(forward, inverse, grad_window, response)

    gate_part = (cotangent.astype(F32) * conv).astype(BF16)
    by_token = lambda a: (
        exchange(a.reshape(BLOCKS, BLOCK, LANES), GROUP).transpose(1, 0, 2).reshape(BLOCK, wide)
    )
    gate_grad = by_token(gate_part)
    grad_mixed = by_token(back).astype(F32)
    key_grad = (grad_mixed * value_input.astype(F32)).astype(BF16)
    value_grad = (grad_mixed * key_input.astype(F32)).astype(BF16)
    return gate_grad, key_grad, value_grad, filter_grad


def solution(mesh):
    split = Mesh(mesh.devices.reshape(SIZES), AXES)
    spans = P(CTX, CH)
    mapped = jax.shard_map(
        body,
        mesh=split,
        in_specs=(P(), P(), spans, spans, spans, P(CTX + CH, None), P(None, CH)),
        out_specs=(spans, spans, spans, spans),
        check_vma=False,
    )
    forward, inverse = make_tables()

    def run(gate_input, key_input, value_input, out_grad, filter_taps):
        return mapped(
            forward, inverse, gate_input, key_input, value_input, out_grad, filter_taps
        )

    return run
```

```python
import functools
import math

import jax
import jax.numpy as jnp
import ml_dtypes
import numpy as np
from jax import lax
from jax.experimental import pallas as pl
from jax.experimental.pallas import tpu as pltpu
from jax.sharding import Mesh, PartitionSpec as P

BF16 = jnp.bfloat16
F32 = jnp.float32
AXES = ("z", "yh", "yl", "c", "x", "zh")
SIZES = (8, 2, 2, 2, 4, 2)
CTX = ("z", "yh", "yl", "c")
GROUP = ("yl", "c")
RUNS = ("z", "yh")
CH = ("x", "zh")

BLOCK = 256
PERIOD = 1024
LANES = 128
BLOCKS = 4
TOKENS = BLOCKS * BLOCK
WIDE = BLOCKS * LANES
BINS = 128
STEPS = PERIOD // 2 // BINS
ROWS = 2 * BINS
SLOT = 16
MIB = 1024 * 1024


def make_tables(lags, share):
    freq = np.arange(PERIOD // 2)[:, None]
    place = np.arange(PERIOD)[None, :]
    angle = math.pi / PERIOD * ((2 * freq + 1) * place % (2 * PERIOD)).astype(np.float64)
    both = np.stack([np.cos(angle), -np.sin(angle)])
    both = both.reshape(2, STEPS, BINS, PERIOD).transpose(1, 0, 2, 3).reshape(PERIOD, PERIOD)
    by_slot = np.zeros((lags // share, SLOT, PERIOD))
    by_slot[:, :share] = both.T[:lags].reshape(lags // share, share, PERIOD)
    tables = both, both.T, by_slot.reshape(-1, PERIOD)
    return tuple(np.ascontiguousarray(t).astype(ml_dtypes.bfloat16) for t in tables)


def dot(a, b):
    return jnp.dot(a, b, preferred_element_type=F32)


def lane_block(index):
    return slice(index * LANES, (index + 1) * LANES)


def lanes_at(index):
    return pl.ds(pl.multiple_of(index * LANES, LANES), LANES)


def token_block(index):
    return slice(index * BLOCK, (index + 1) * BLOCK)


def spread(part):
    return jnp.concatenate([part] * BLOCKS, axis=1)


def accumulate(step, total, part):
    @pl.when(step == 0)
    def _():
        total[...] = part

    @pl.when(step > 0)
    def _():
        total[...] += part


def prep_kernel(place, key, value, gate, out_grad, *outs):
    ships, pieces = outs[:BLOCKS], outs[BLOCKS]
    for hop, ship in enumerate(ships):
        at = (slice(None), lanes_at(place[0] ^ hop))
        ship[:BLOCK, :] = (key[at].astype(F32) * value[at].astype(F32)).astype(BF16)
        ship[BLOCK:, :] = gate[at]
    count = pieces.shape[0]
    for piece in range(count):
        target = piece % BLOCKS * (count // BLOCKS) + piece // BLOCKS
        pieces[target] = out_grad[:, lane_block(piece)]


def join_kernel(place, *refs):
    ships, (mixed, tail, gate) = refs[:BLOCKS], refs[BLOCKS:]
    skipped = TOKENS - tail.shape[0]
    for hop, ship in enumerate(ships):
        block = place[0] ^ hop
        at = pl.multiple_of(block * BLOCK, BLOCK)
        mixed[pl.ds(at, BLOCK), :] = ship[:BLOCK, :]
        gate[pl.ds(at, BLOCK), :] = ship[BLOCK:, :]

    tail[...] = mixed[skipped:, :]


def conv_kernel(scale, forward, inverse, halo, mixed, taps, conv, spectrum, response, windows, total):
    step = pl.program_id(0)
    lags = taps.shape[0]

    @pl.when(step == 0)
    def _():
        for block in range(BLOCKS):
            early = lags - block * BLOCK
            if early:
                windows[:early, lane_block(block)] = halo[block * BLOCK :, :]
            windows[early:, lane_block(block)] = mixed[: (block + 1) * BLOCK, :]

    resp = dot(forward[:, :lags], taps[...])
    response[...] = resp
    spec = dot(forward[...], windows[...])
    spectrum[...] = spec
    f_re, f_im = spread(resp[:BINS]), spread(resp[BINS:])
    x_re, x_im = spec[:BINS], spec[BINS:]
    y = jnp.concatenate([f_re * x_re - f_im * x_im, f_re * x_im + f_im * x_re]).astype(BF16)
    accumulate(step, total, dot(inverse[...], y))

    @pl.when(step == STEPS - 1)
    def _():
        for block in range(BLOCKS):
            conv[token_block(block), :] = total[:, lane_block(block)] * scale


def cross_kernel(
    scale, forward, inverse, cotangent, gate, spectrum, grad, head, lag_grad, windows, total
):
    step = pl.program_id(0)

    @pl.when(step == 0)
    def _():
        product = (cotangent[...].astype(F32) * gate[...].astype(F32)).astype(BF16)
        grad[...] = product
        head[...] = product[: head.shape[0]]
        for block in range(BLOCKS):
            windows[:, lane_block(block)] = product[token_block(block)]

    spec = dot(forward[...], windows[...])
    g_re, g_im = spec[:BINS], spec[BINS:]
    x_re, x_im = spectrum[:BINS], spectrum[BINS:]
    re = g_re * x_re + g_im * x_im
    im = g_im * x_re - g_re * x_im
    re = sum(re[:, lane_block(b)] for b in range(BLOCKS))
    im = sum(im[:, lane_block(b)] for b in range(BLOCKS))
    accumulate(step, total, dot(inverse[...], jnp.concatenate([re, im]).astype(BF16)))

    @pl.when(step == STEPS - 1)
    def _():
        lag_grad[...] = (total[...] * scale).astype(BF16)


def back_kernel(
    scale, place, forward, inverse, grad, halo, response, conv, cotangent, *refs
):
    outs, (windows, total) = refs[:BLOCKS], refs[BLOCKS:]
    step = pl.program_id(0)

    @pl.when(step == 0)
    def _():
        for block in range(BLOCKS):
            own = min(PERIOD, TOKENS - block * BLOCK)
            windows[:own, lane_block(block)] = grad[block * BLOCK : block * BLOCK + own, :]
            if own < PERIOD:
                windows[own:, lane_block(block)] = halo[: PERIOD - own, :]
        for hop, out in enumerate(outs):
            at = pl.ds(pl.multiple_of((place[0] ^ hop) * BLOCK, BLOCK), BLOCK)
            out[:BLOCK, :] = (cotangent[at, :].astype(F32) * conv[at, :]).astype(BF16)

    spec = dot(forward[...], windows[...])
    f_re, f_im = spread(response[:BINS]), spread(response[BINS:])
    g_re, g_im = spec[:BINS], spec[BINS:]
    y = jnp.concatenate([f_re * g_re + f_im * g_im, f_re * g_im - f_im * g_re]).astype(BF16)
    accumulate(step, total, dot(inverse[...], y))

    @pl.when(step == STEPS - 1)
    def _():
        for hop, out in enumerate(outs):
            out[BLOCK:, :] = (total[:, lanes_at(place[0] ^ hop)] * scale).astype(BF16)


def final_kernel(place, *refs):
    ships, (key, value, gate_grad, key_grad, value_grad) = refs[:BLOCKS], refs[BLOCKS:]
    for hop, ship in enumerate(ships):
        at = (slice(None), lanes_at(place[0] ^ hop))
        gate_grad[at] = ship[:BLOCK, :]
        back = ship[BLOCK:, :].astype(F32)
        key_grad[at] = (back * value[at].astype(F32)).astype(BF16)
        value_grad[at] = (back * key[at].astype(F32)).astype(BF16)


def sum_kernel(parts, out):
    for block in range(BLOCKS):
        total = parts[block].astype(F32)
        for source in range(1, parts.shape[0] // BLOCKS):
            total += parts[source * BLOCKS + block].astype(F32)
        out[:, lane_block(block)] = total[: out.shape[0]]


def whole(shape):
    return pl.BlockSpec(shape, lambda *_: (0,) * len(shape))


def shaped(shape, dtype=BF16):
    return jax.ShapeDtypeStruct(shape, dtype)


def call(kernel, in_specs, out_specs, out_shape, scratch=(), steps=1, macs=0, moved=0):
    return pl.pallas_call(
        kernel,
        grid=(steps,),
        in_specs=in_specs,
        out_specs=out_specs,
        out_shape=out_shape,
        scratch_shapes=scratch,
        compiler_params=pltpu.CompilerParams(
            dimension_semantics=("arbitrary",), vmem_limit_bytes=VMEM_LIMIT
        ),
        cost_estimate=pl.CostEstimate(flops=2 * macs, bytes_accessed=moved, transcendentals=0),
    )


VMEM_LIMIT = 56 * MIB


def shift(value, steps):
    count = lax.axis_size(RUNS)
    first, last = max(0, -steps), min(count, count - steps)
    return lax.ppermute(value, RUNS, [(i, i + steps) for i in range(first, last)])


def swap(ships):
    return [ships[0]] + [
        lax.ppermute(ships[hop], GROUP, [(i, i ^ hop) for i in range(BLOCKS)])
        for hop in range(1, BLOCKS)
    ]


def exchange(value, axes):
    return lax.all_to_all(value, axes, split_axis=0, concat_axis=0, tiled=True)


def body(forward, inverse, slotted, gate_input, key_input, value_input, out_grad, filter_taps):
    lags = filter_taps.shape[0]
    held, channels = out_grad.shape
    share = lags // lax.axis_size(CTX)
    norm = 2.0 / PERIOD / lags**0.5
    local = (BLOCK, WIDE)
    ship = (2 * BLOCK, LANES)
    pieces = (channels // LANES, held, LANES)
    flat = (TOKENS, LANES)
    reach = (lags, LANES)
    scalar = pl.BlockSpec(memory_space=pltpu.SMEM)
    place = lax.axis_index(GROUP).reshape(1)

    *ships, cotangent = call(
        prep_kernel,
        [scalar] + [whole(local)] * 3 + [whole(out_grad.shape)],
        [whole(ship)] * BLOCKS + [whole(pieces)],
        [shaped(ship)] * BLOCKS + [shaped(pieces)],
    )(place, key_input, value_input, gate_input, out_grad)
    cotangent = exchange(cotangent, GROUP + CH).reshape(flat)
    mixed, tail, gate = call(
        join_kernel,
        [scalar] + [whole(ship)] * BLOCKS,
        [whole(flat), whole(reach), whole(flat)],
        [shaped(flat), shaped(reach), shaped(flat)],
    )(place, *swap(ships))
    mixed_halo = shift(tail, 1)
    taps = lax.dynamic_slice_in_dim(filter_taps, lax.axis_index(GROUP) * LANES, LANES, 1)

    table = pl.BlockSpec((ROWS, PERIOD), lambda step: (step, 0))
    bins = pl.BlockSpec((ROWS, WIDE), lambda step: (step, 0))
    narrow_bins = pl.BlockSpec((ROWS, LANES), lambda step: (step, 0))
    conv, spectrum, response = call(
        functools.partial(conv_kernel, norm),
        [
            table,
            pl.BlockSpec((BLOCK, ROWS), lambda step: (lags // BLOCK, step)),
            whole(reach),
            whole(flat),
            whole(reach),
        ],
        [whole(flat), bins, narrow_bins],
        [shaped(flat, F32), shaped((PERIOD, WIDE), F32), shaped((PERIOD, LANES), F32)],
        [pltpu.VMEM((PERIOD, WIDE), BF16), pltpu.VMEM(local, F32)],
        STEPS,
    )(forward, inverse, mixed_halo, mixed, taps)

    grad, head, lag_grad = call(
        functools.partial(cross_kernel, norm),
        [
            pl.BlockSpec((ROWS, BLOCK), lambda step: (step, lags // BLOCK)),
            pl.BlockSpec((slotted.shape[0], ROWS), lambda step: (0, step)),
            whole(flat),
            whole(flat),
            bins,
        ],
        [whole(flat), whole(reach), whole((slotted.shape[0], LANES))],
        [shaped(flat), shaped(reach), shaped((slotted.shape[0], LANES))],
        [pltpu.VMEM(local, BF16), pltpu.VMEM((slotted.shape[0], LANES), F32)],
        STEPS,
    )(forward, slotted, cotangent, gate, spectrum)
    grad_halo = shift(head, -1)
    lag_parts = exchange(lag_grad.reshape(-1, SLOT, LANES), CTX)

    ships = call(
        functools.partial(back_kernel, norm),
        [
            scalar,
            table,
            pl.BlockSpec((BLOCK, ROWS), lambda step: (0, step)),
            whole(flat),
            whole(reach),
            narrow_bins,
            whole(flat),
            whole(flat),
        ],
        [whole(ship)] * BLOCKS,
        [shaped(ship)] * BLOCKS,
        [pltpu.VMEM((PERIOD, WIDE), BF16), pltpu.VMEM(local, F32)],
        STEPS,
    )(place, forward, inverse, grad, grad_halo, response, conv, cotangent)
    gate_grad, key_grad, value_grad = call(
        final_kernel,
        [scalar] + [whole(ship)] * BLOCKS + [whole(local)] * 2,
        [whole(local)] * 3,
        [shaped(local)] * 3,
    )(place, *swap(ships), key_input, value_input)
    filter_grad = call(
        sum_kernel,
        [whole(lag_parts.shape)],
        whole((share, WIDE)),
        shaped((share, WIDE), F32),
    )(lag_parts)
    return gate_grad, key_grad, value_grad, filter_grad


def solution(mesh):
    split = Mesh(mesh.devices.reshape(SIZES), AXES)
    spans = P(CTX, CH)
    mapped = jax.shard_map(
        body,
        mesh=split,
        in_specs=(P(), P(), P(), spans, spans, spans, P(CTX + CH, None), P(None, CH)),
        out_specs=(spans, spans, spans, spans),
        check_vma=False,
    )

    def run(gate_input, key_input, value_input, out_grad, filter_taps):
        lags = filter_taps.shape[0]
        tables = make_tables(lags, lags // math.prod(SIZES[:4]))
        return mapped(*tables, gate_input, key_input, value_input, out_grad, filter_taps)

    return run
```

```python
import functools
import math

import jax
import jax.numpy as jnp
import ml_dtypes
import numpy as np
from jax import lax
from jax.experimental import pallas as pl
from jax.experimental.pallas import tpu as pltpu
from jax.sharding import Mesh, PartitionSpec as P

BF16 = jnp.bfloat16
F32 = jnp.float32
AXES = ("chip", "core", "ch")
CORES = 2
CTX = ("chip", "core")

PERIOD = 1024
REACH = 3
BINS = 128
STEPS = PERIOD // 2 // BINS
ROWS = 2 * BINS
SLOT = 16
LANES = 128
MIB = 1024 * 1024


def make_tables(lags, share):
    freq = np.arange(PERIOD // 2)[:, None]
    place = np.arange(PERIOD)[None, :]
    angle = math.pi / PERIOD * ((2 * freq + 1) * place % (2 * PERIOD)).astype(np.float64)
    both = np.stack([np.cos(angle), -np.sin(angle)])
    both = both.reshape(2, STEPS, BINS, PERIOD).transpose(1, 0, 2, 3).reshape(PERIOD, PERIOD)
    by_slot = np.zeros((CORES, lags // share // CORES, SLOT, PERIOD))
    by_slot[:, :, :share] = (
        both.T[:lags].reshape(-1, CORES, share, PERIOD).transpose(1, 0, 2, 3)
    )
    tables = both, both.T, by_slot.reshape(-1, PERIOD)
    return tuple(np.ascontiguousarray(t).astype(ml_dtypes.bfloat16) for t in tables)


def dot(a, b):
    return jnp.dot(a, b, preferred_element_type=F32)


def product(a, b):
    return (a[...].astype(F32) * b[...].astype(F32)).astype(BF16)


def lane_block(index):
    return slice(index * LANES, (index + 1) * LANES)


def spectrum(table, spans):
    rows = spans[0].shape[0]
    return sum(
        dot(table[:, i * rows : (i + 1) * rows], span[...]) for i, span in enumerate(spans)
    )


def halves(spec):
    return spec[:BINS], spec[BINS:]


def accumulate(step, total, part):
    @pl.when(step == 0)
    def _():
        total[...] = part

    @pl.when(step > 0)
    def _():
        total[...] += part


def prep_kernel(key, value, out_grad, mixed, pieces):
    mixed[...] = product(key, value)
    width = pieces.shape[2]
    for piece in range(pieces.shape[0]):
        pieces[piece] = out_grad[:, piece * width : (piece + 1) * width]


def pack(slot, share):
    rest = SLOT - share
    count = share // rest
    last = slot[:share, count * LANES :]
    return jnp.concatenate(
        [
            jnp.concatenate(
                [slot[:share, lane_block(i)], last[i * rest : (i + 1) * rest]], axis=0
            )
            for i in range(count)
        ],
        axis=1,
    )


def unpack(packed, share):
    rest = SLOT - share
    count = share // rest
    last = jnp.concatenate([packed[share:, lane_block(i)] for i in range(count)], axis=0)
    return jnp.concatenate([packed[:share], last], axis=1)


def cross_kernel(scale, share, core, table, inverse, *refs):
    spans, (cotangent, gate, grad, mine, theirs, total) = refs[: REACH + 1], refs[REACH + 1 :]
    step = pl.program_id(0)

    @pl.when(step == 0)
    def _():
        grad[...] = product(cotangent, gate)

    rows = grad.shape[0]
    x_re, x_im = halves(spectrum(table, spans))
    g_re, g_im = halves(dot(table[:, REACH * rows :], grad[...]))
    y = jnp.concatenate([g_re * x_re + g_im * x_im, g_im * x_re - g_re * x_im]).astype(BF16)
    accumulate(step, total, dot(inverse[...], y))

    @pl.when(step == STEPS - 1)
    def _():
        count = mine.shape[0]
        for out, owner in ((mine, core[0]), (theirs, 1 - core[0])):

            @pl.loop(0, count)
            def _(slot):
                at = pl.multiple_of((owner * count + slot) * SLOT, SLOT)
                out[slot] = pack(total[pl.ds(at, SLOT), :] * scale, share).astype(BF16)


def add_kernel(a, b, out):
    out[...] = (a[...].astype(F32) + b[...].astype(F32)).astype(BF16)


def sum_kernel(parts, out):
    total = parts[0].astype(F32)
    for source in range(1, parts.shape[0]):
        total += parts[source].astype(F32)
    out[...] = unpack(total, out.shape[0])


def rest_kernel(scale, table, first, last, taps, *refs):
    early, late = refs[: REACH + 1], refs[REACH + 1 : 2 * REACH + 2]
    cotangent, key, value, gate_grad, key_grad, value_grad, conv, back = refs[2 * REACH + 2 :]
    step = pl.program_id(0)
    f_re, f_im = halves(dot(table[:, : taps.shape[0]], taps[...]))
    x_re, x_im = halves(spectrum(table, early))
    y = jnp.concatenate([f_re * x_re - f_im * x_im, f_re * x_im + f_im * x_re]).astype(BF16)
    accumulate(step, conv, dot(last[...], y))
    g_re, g_im = halves(spectrum(table, late))
    y = jnp.concatenate([f_re * g_re + f_im * g_im, f_re * g_im - f_im * g_re]).astype(BF16)
    accumulate(step, back, dot(first[...], y))

    @pl.when(step == STEPS - 1)
    def _():
        gate_grad[...] = (cotangent[...].astype(F32) * (conv[...] * scale)).astype(BF16)
        grad_mixed = back[...] * scale
        key_grad[...] = (grad_mixed * value[...].astype(F32)).astype(BF16)
        value_grad[...] = (grad_mixed * key[...].astype(F32)).astype(BF16)


def whole(shape):
    return pl.BlockSpec(shape, lambda *_: (0,) * len(shape))


def shaped(shape, dtype=BF16):
    return jax.ShapeDtypeStruct(shape, dtype)


def call(kernel, in_specs, out_specs, out_shape, scratch=(), steps=1):
    return pl.pallas_call(
        kernel,
        grid=(steps,),
        in_specs=in_specs,
        out_specs=out_specs,
        out_shape=out_shape,
        scratch_shapes=scratch,
        compiler_params=pltpu.CompilerParams(
            dimension_semantics=("arbitrary",), vmem_limit_bytes=VMEM_LIMIT
        ),
        cost_estimate=pl.CostEstimate(flops=0, bytes_accessed=0, transcendentals=0),
    )


VMEM_LIMIT = 56 * MIB


def shift(value, steps):
    count = lax.axis_size(CTX)
    first, last = max(0, -steps), min(count, count - steps)
    return lax.ppermute(value, CTX, [(i, i + steps) for i in range(first, last)])


def exchange(value, axes):
    return lax.all_to_all(value, axes, split_axis=0, concat_axis=0, tiled=True)


def body(forward, inverse, slotted, gate_input, key_input, value_input, out_grad, filter_taps):
    lags, width = filter_taps.shape
    held, channels = out_grad.shape
    local = gate_input.shape
    span = local[0]
    chips = lax.axis_size("chip")
    share = lags // chips // CORES
    norm = 2.0 / PERIOD / lags**0.5
    pieces = (channels // width, held, width)
    packed = (chips, SLOT, width * share // SLOT)
    scalar = pl.BlockSpec(memory_space=pltpu.SMEM)

    mixed, cotangent = call(
        prep_kernel,
        [whole(local)] * 2 + [whole(out_grad.shape)],
        [whole(local), whole(pieces)],
        [shaped(local), shaped(pieces)],
    )(key_input, value_input, out_grad)
    early = [shift(mixed, steps) for steps in range(REACH, 0, -1)] + [mixed]
    cotangent = exchange(cotangent, "ch").reshape(local)

    table = pl.BlockSpec((ROWS, PERIOD), lambda step: (step, 0))
    grad, mine, theirs = call(
        functools.partial(cross_kernel, norm, share),
        [scalar, table, pl.BlockSpec((slotted.shape[0], ROWS), lambda step: (0, step))]
        + [whole(local)] * (REACH + 3),
        [whole(local), whole(packed), whole(packed)],
        [shaped(local), shaped(packed), shaped(packed)],
        [pltpu.VMEM((slotted.shape[0], width), F32)],
        STEPS,
    )(lax.axis_index("core").reshape(1), forward, slotted, *early, cotangent, gate_input)
    theirs = lax.ppermute(theirs, "core", [(i, 1 - i) for i in range(CORES)])
    mine = call(add_kernel, [whole(packed)] * 2, whole(packed), shaped(packed))(mine, theirs)
    parts = exchange(mine, "chip")
    filter_grad = call(
        sum_kernel, [whole(packed)], whole((share, width)), shaped((share, width), F32)
    )(parts)

    late = [grad] + [shift(grad, -steps) for steps in range(1, REACH + 1)]
    gate_grad, key_grad, value_grad = call(
        functools.partial(rest_kernel, norm),
        [
            table,
            pl.BlockSpec((span, ROWS), lambda step: (0, step)),
            pl.BlockSpec((span, ROWS), lambda step: (REACH, step)),
            whole((lags, width)),
        ]
        + [whole(local)] * (2 * REACH + 5),
        [whole(local)] * 3,
        [shaped(local)] * 3,
        [pltpu.VMEM(local, F32)] * 2,
        STEPS,
    )(forward, inverse, inverse, filter_taps, *early, *late, cotangent, key_input, value_input)
    return gate_grad, key_grad, value_grad, filter_grad


def solution(mesh):
    count, groups = mesh.devices.shape
    split = Mesh(mesh.devices.reshape(count // CORES, CORES, groups), AXES)
    spans = P(CTX, "ch")
    mapped = jax.shard_map(
        body,
        mesh=split,
        in_specs=(P(), P(), P(), spans, spans, spans, P(CTX + ("ch",), None), P(None, "ch")),
        out_specs=(spans, spans, spans, spans),
        check_vma=False,
    )

    def run(gate_input, key_input, value_input, out_grad, filter_taps):
        lags = filter_taps.shape[0]
        tables = make_tables(lags, lags // count)
        return mapped(*tables, gate_input, key_input, value_input, out_grad, filter_taps)

    return run
```

```python
import functools
import math

import jax
import jax.numpy as jnp
import ml_dtypes
import numpy as np
from jax import lax
from jax.experimental import pallas as pl
from jax.experimental.pallas import tpu as pltpu
from jax.sharding import Mesh, PartitionSpec as P

BF16 = jnp.bfloat16
F32 = jnp.float32
AXES = ("chip", "core", "ch")
CORES = 2
CTX = ("chip", "core")

PERIOD = 1024
REACH = 3
BINS = 128
STEPS = PERIOD // 2 // BINS
ROWS = 2 * BINS
SLOT = 16
LANES = 128
MIB = 1024 * 1024


def make_tables(lags, share):
    freq = np.arange(PERIOD // 2)[:, None]
    place = np.arange(PERIOD)[None, :]
    angle = math.pi / PERIOD * ((2 * freq + 1) * place % (2 * PERIOD)).astype(np.float64)
    both = np.stack([np.cos(angle), -np.sin(angle)])
    both = both.reshape(2, STEPS, BINS, PERIOD).transpose(1, 0, 2, 3).reshape(PERIOD, PERIOD)
    by_slot = np.zeros((CORES, lags // share // CORES, SLOT, PERIOD))
    by_slot[:, :, :share] = (
        both.T[:lags].reshape(-1, CORES, share, PERIOD).transpose(1, 0, 2, 3)
    )
    tables = both, both.T, by_slot.reshape(-1, PERIOD)
    return tuple(np.ascontiguousarray(t).astype(ml_dtypes.bfloat16) for t in tables)


def dot(a, b):
    return jnp.dot(a, b, preferred_element_type=F32)


def product(a, b):
    return (a[...].astype(F32) * b[...].astype(F32)).astype(BF16)


def lane_block(index):
    return slice(index * LANES, (index + 1) * LANES)


def spectrum(table, spans):
    rows = spans[0].shape[0]
    return sum(
        dot(table[:, i * rows : (i + 1) * rows], span[...]) for i, span in enumerate(spans)
    )


def halves(spec):
    return spec[:BINS], spec[BINS:]


def accumulate(step, total, part):
    @pl.when(step == 0)
    def _():
        total[...] = part

    @pl.when(step > 0)
    def _():
        total[...] += part


def prep_kernel(key, value, out_grad, mixed, pieces):
    mixed[...] = product(key, value)
    width = pieces.shape[2]
    for piece in range(pieces.shape[0]):
        pieces[piece] = out_grad[:, piece * width : (piece + 1) * width]


def pack(slot, share):
    rest = SLOT - share
    count = share // rest
    last = slot[:share, count * LANES :]
    return jnp.concatenate(
        [
            jnp.concatenate(
                [slot[:share, lane_block(i)], last[i * rest : (i + 1) * rest]], axis=0
            )
            for i in range(count)
        ],
        axis=1,
    )


def unpack(packed, share):
    rest = SLOT - share
    count = share // rest
    last = jnp.concatenate([packed[share:, lane_block(i)] for i in range(count)], axis=0)
    return jnp.concatenate([packed[:share], last], axis=1)


def conv_kernel(scale, table, last, taps, *refs):
    spans, (conv, spec, total) = refs[: REACH + 1], refs[REACH + 1 :]
    step = pl.program_id(0)
    f_re, f_im = halves(dot(table[:, : taps.shape[0]], taps[...]))
    full = spectrum(table, spans)
    spec[...] = full.astype(BF16)
    x_re, x_im = halves(full)
    y = jnp.concatenate([f_re * x_re - f_im * x_im, f_re * x_im + f_im * x_re]).astype(BF16)
    accumulate(step, total, dot(last[...], y))

    @pl.when(step == STEPS - 1)
    def _():
        conv[...] = total[...] * scale


def cross_kernel(scale, share, core, table, inverse, spec, cotangent, gate, grad, *refs):
    mine, theirs, total = refs
    step = pl.program_id(0)

    @pl.when(step == 0)
    def _():
        grad[...] = product(cotangent, gate)

    x_re, x_im = halves(spec[...].astype(F32))
    g_re, g_im = halves(dot(table[...], grad[...]))
    y = jnp.concatenate([g_re * x_re + g_im * x_im, g_im * x_re - g_re * x_im]).astype(BF16)
    accumulate(step, total, dot(inverse[...], y))

    @pl.when(step == STEPS - 1)
    def _():
        count = mine.shape[0]
        for out, owner in ((mine, core[0]), (theirs, 1 - core[0])):
            for slot in range(count):
                at = pl.multiple_of((owner * count + slot) * SLOT, SLOT)
                out[slot] = pack(total[pl.ds(at, SLOT), :] * scale, share).astype(BF16)


def add_kernel(a, b, out):
    out[...] = (a[...].astype(F32) + b[...].astype(F32)).astype(BF16)


def sum_kernel(parts, out):
    total = parts[0].astype(F32)
    for source in range(1, parts.shape[0]):
        total += parts[source].astype(F32)
    out[...] = unpack(total, out.shape[0])


def back_kernel(scale, table, first, taps, *refs):
    spans = refs[: REACH + 1]
    cotangent, conv, key, value, gate_grad, key_grad, value_grad, total = refs[REACH + 1 :]
    step = pl.program_id(0)
    f_re, f_im = halves(dot(table[:, : taps.shape[0]], taps[...]))
    g_re, g_im = halves(spectrum(table, spans))
    y = jnp.concatenate([f_re * g_re + f_im * g_im, f_re * g_im - f_im * g_re]).astype(BF16)
    accumulate(step, total, dot(first[...], y))

    @pl.when(step == STEPS - 1)
    def _():
        gate_grad[...] = (cotangent[...].astype(F32) * conv[...]).astype(BF16)
        grad_mixed = total[...] * scale
        key_grad[...] = (grad_mixed * value[...].astype(F32)).astype(BF16)
        value_grad[...] = (grad_mixed * key[...].astype(F32)).astype(BF16)


def whole(shape):
    return pl.BlockSpec(shape, lambda *_: (0,) * len(shape))


def shaped(shape, dtype=BF16):
    return jax.ShapeDtypeStruct(shape, dtype)


def call(kernel, in_specs, out_specs, out_shape, scratch=(), steps=1, flops=0):
    return pl.pallas_call(
        kernel,
        grid=(steps,),
        in_specs=in_specs,
        out_specs=out_specs,
        out_shape=out_shape,
        scratch_shapes=scratch,
        compiler_params=pltpu.CompilerParams(
            dimension_semantics=("arbitrary",), vmem_limit_bytes=VMEM_LIMIT
        ),
        cost_estimate=pl.CostEstimate(flops=flops, bytes_accessed=0, transcendentals=0),
    )


VMEM_LIMIT = 56 * MIB
FLOPS = 35_000_000_000


def shift(value, steps):
    count = lax.axis_size(CTX)
    first, last = max(0, -steps), min(count, count - steps)
    return lax.ppermute(value, CTX, [(i, i + steps) for i in range(first, last)])


def exchange(value, axes):
    return lax.all_to_all(value, axes, split_axis=0, concat_axis=0, tiled=True)


def body(forward, inverse, slotted, gate_input, key_input, value_input, out_grad, filter_taps):
    lags, width = filter_taps.shape
    held, channels = out_grad.shape
    local = gate_input.shape
    span = local[0]
    chips = lax.axis_size("chip")
    share = lags // chips // CORES
    norm = 2.0 / PERIOD / lags**0.5
    pieces = (channels // width, held, width)
    packed = (chips, SLOT, width * share // SLOT)
    scalar = pl.BlockSpec(memory_space=pltpu.SMEM)

    mixed, cotangent = call(
        prep_kernel,
        [whole(local)] * 2 + [whole(out_grad.shape)],
        [whole(local), whole(pieces)],
        [shaped(local), shaped(pieces)],
    )(key_input, value_input, out_grad)
    early = [shift(mixed, steps) for steps in range(REACH, 0, -1)] + [mixed]
    cotangent = exchange(cotangent, "ch").reshape(local)

    table = pl.BlockSpec((ROWS, PERIOD), lambda step: (step, 0))
    bins = pl.BlockSpec((ROWS, width), lambda step: (step, 0))
    conv, spec = call(
        functools.partial(conv_kernel, norm),
        [table, pl.BlockSpec((span, ROWS), lambda step: (REACH, step)), whole((lags, width))]
        + [whole(local)] * (REACH + 1),
        [whole(local), bins],
        [shaped(local, F32), shaped((PERIOD, width))],
        [pltpu.VMEM(local, F32)],
        STEPS,
        FLOPS,
    )(forward, inverse, filter_taps, *early)
    grad, mine, theirs = call(
        functools.partial(cross_kernel, norm, share),
        [
            scalar,
            pl.BlockSpec((ROWS, span), lambda step: (step, REACH)),
            pl.BlockSpec((slotted.shape[0], ROWS), lambda step: (0, step)),
            bins,
        ]
        + [whole(local)] * 2,
        [whole(local), whole(packed), whole(packed)],
        [shaped(local), shaped(packed), shaped(packed)],
        [pltpu.VMEM((slotted.shape[0], width), F32)],
        STEPS,
    )(lax.axis_index("core").reshape(1), forward, slotted, spec, cotangent, gate_input)
    theirs = lax.ppermute(theirs, "core", [(i, 1 - i) for i in range(CORES)])
    mine = call(add_kernel, [whole(packed)] * 2, whole(packed), shaped(packed))(mine, theirs)
    parts = exchange(mine, "chip")
    filter_grad = call(
        sum_kernel, [whole(packed)], whole((share, width)), shaped((share, width), F32)
    )(parts)

    late = [grad] + [shift(grad, -steps) for steps in range(1, REACH + 1)]
    gate_grad, key_grad, value_grad = call(
        functools.partial(back_kernel, norm),
        [table, pl.BlockSpec((span, ROWS), lambda step: (0, step)), whole((lags, width))]
        + [whole(local)] * (REACH + 5),
        [whole(local)] * 3,
        [shaped(local)] * 3,
        [pltpu.VMEM(local, F32)],
        STEPS,
        FLOPS,
    )(forward, inverse, filter_taps, *late, cotangent, conv, key_input, value_input)
    return gate_grad, key_grad, value_grad, filter_grad


def solution(mesh):
    count, groups = mesh.devices.shape
    split = Mesh(mesh.devices.reshape(count // CORES, CORES, groups), AXES)
    spans = P(CTX, "ch")
    mapped = jax.shard_map(
        body,
        mesh=split,
        in_specs=(P(), P(), P(), spans, spans, spans, P(CTX + ("ch",), None), P(None, "ch")),
        out_specs=(spans, spans, spans, spans),
        check_vma=False,
    )

    def run(gate_input, key_input, value_input, out_grad, filter_taps):
        lags = filter_taps.shape[0]
        tables = make_tables(lags, lags // count)
        return mapped(*tables, gate_input, key_input, value_input, out_grad, filter_taps)

    return run
```

```python
import functools
import math

import jax
import jax.numpy as jnp
import ml_dtypes
import numpy as np
from jax import lax
from jax.experimental import pallas as pl
from jax.experimental.pallas import tpu as pltpu
from jax.sharding import Mesh, PartitionSpec as P

BF16 = jnp.bfloat16
F32 = jnp.float32
AXES = ("z", "yh", "yl", "c", "x", "zh")
SIZES = (8, 2, 2, 2, 4, 2)
CTX = ("z", "yh", "yl", "c")
GROUP = ("yl", "c")
RUNS = ("z", "yh")
CH = ("x", "zh")

BLOCK = 256
PERIOD = 1024
LANES = 128
BLOCKS = 4
TOKENS = BLOCKS * BLOCK
WIDE = BLOCKS * LANES
BINS = 512
STEPS = PERIOD // 2 // BINS
ROWS = 2 * BINS
SLOT = 16
MIB = 1024 * 1024


def make_tables(lags):
    freq = np.arange(PERIOD // 2)[:, None]
    place = np.arange(PERIOD)[None, :]
    angle = math.pi / PERIOD * ((2 * freq + 1) * place % (2 * PERIOD)).astype(np.float64)
    both = np.stack([np.cos(angle), -np.sin(angle)])
    both = both.reshape(2, STEPS, BINS, PERIOD).transpose(1, 0, 2, 3).reshape(STEPS, ROWS, PERIOD)
    back = both.transpose(0, 2, 1)
    tables = both, both[:, :, lags:], back[:, :BLOCK], back[:, :lags], back[:, lags:]
    return tuple(np.ascontiguousarray(t).astype(ml_dtypes.bfloat16) for t in tables)


def dot(a, b):
    return jnp.dot(a, b, preferred_element_type=F32)


def lane_block(index):
    return slice(index * LANES, (index + 1) * LANES)


def lanes_at(index):
    return pl.ds(pl.multiple_of(index * LANES, LANES), LANES)


def token_block(index):
    return slice(index * BLOCK, (index + 1) * BLOCK)


def spread(part):
    return jnp.concatenate([part] * BLOCKS, axis=1)


def accumulate(step, total, part):
    @pl.when(step == 0)
    def _():
        total[...] = part

    @pl.when(step > 0)
    def _():
        total[...] += part


def prep_kernel(place, key, value, gate, out_grad, *outs):
    ships, pieces = outs[:BLOCKS], outs[BLOCKS]
    for hop, ship in enumerate(ships):
        at = (slice(None), lanes_at(place[0] ^ hop))
        ship[:BLOCK, :] = (key[at].astype(F32) * value[at].astype(F32)).astype(BF16)
        ship[BLOCK:, :] = gate[at]
    count = pieces.shape[0]
    for piece in range(count):
        target = piece % BLOCKS * (count // BLOCKS) + piece // BLOCKS
        pieces[target] = out_grad[:, lane_block(piece)]


def join_kernel(place, *refs):
    ships, (mixed, tail, gate) = refs[:BLOCKS], refs[BLOCKS:]
    skipped = TOKENS - tail.shape[0]
    for hop, ship in enumerate(ships):
        block = place[0] ^ hop
        at = pl.multiple_of(block * BLOCK, BLOCK)
        mixed[pl.ds(at, BLOCK), :] = ship[:BLOCK, :]
        gate[pl.ds(at, BLOCK), :] = ship[BLOCK:, :]

    tail[...] = mixed[skipped:, :]


def conv_kernel(scale, forward, inverse, halo, mixed, taps, conv, spectrum, response, windows, total):
    step = pl.program_id(0)
    lags = taps.shape[0]

    @pl.when(step == 0)
    def _():
        for block in range(BLOCKS):
            early = lags - block * BLOCK
            if early:
                windows[:early, lane_block(block)] = halo[block * BLOCK :, :]
            windows[early:, lane_block(block)] = mixed[: (block + 1) * BLOCK, :]

    resp = dot(forward[:, :lags], taps[...])
    response[...] = resp.astype(BF16)
    spec = dot(forward[...], windows[...])
    spectrum[...] = spec.astype(BF16)
    f_re, f_im = spread(resp[:BINS]), spread(resp[BINS:])
    x_re, x_im = spec[:BINS], spec[BINS:]
    y = jnp.concatenate([f_re * x_re - f_im * x_im, f_re * x_im + f_im * x_re]).astype(BF16)
    accumulate(step, total, dot(inverse[...], y))

    @pl.when(step == STEPS - 1)
    def _():
        for block in range(BLOCKS):
            conv[token_block(block), :] = total[:, lane_block(block)] * scale


def cross_kernel(
    scale, forward, inverse, cotangent, gate, spectrum, grad, head, lag_grad, windows, total
):
    step = pl.program_id(0)

    @pl.when(step == 0)
    def _():
        product = (cotangent[...].astype(F32) * gate[...].astype(F32)).astype(BF16)
        grad[...] = product
        head[...] = product[: head.shape[0]]
        for block in range(BLOCKS):
            windows[:, lane_block(block)] = product[token_block(block)]

    spec = dot(forward[...], windows[...])
    g_re, g_im = spec[:BINS], spec[BINS:]
    full = spectrum[...].astype(F32)
    x_re, x_im = full[:BINS], full[BINS:]
    re = g_re * x_re + g_im * x_im
    im = g_im * x_re - g_re * x_im
    re = sum(re[:, lane_block(b)] for b in range(BLOCKS))
    im = sum(im[:, lane_block(b)] for b in range(BLOCKS))
    lags = inverse.shape[0]
    part = dot(inverse[...], jnp.concatenate([re, im]).astype(BF16))

    @pl.when(step == 0)
    def _():
        total[:lags, :] = part
        total[lags:, :] = jnp.zeros_like(total[lags:, :])

    @pl.when(step > 0)
    def _():
        total[:lags, :] += part

    @pl.when(step == STEPS - 1)
    def _():
        count = lag_grad.shape[0]
        share = lags // count
        for slot in range(count):
            rows = total[slot * share : slot * share + SLOT, :] * scale
            lag_grad[slot] = rows.astype(BF16)


def back_kernel(
    scale, place, forward, inverse, grad, halo, response, conv, cotangent, *refs
):
    outs, (windows, total) = refs[:BLOCKS], refs[BLOCKS:]
    step = pl.program_id(0)

    @pl.when(step == 0)
    def _():
        for block in range(BLOCKS):
            own = min(PERIOD, TOKENS - block * BLOCK)
            windows[:own, lane_block(block)] = grad[block * BLOCK : block * BLOCK + own, :]
            if own < PERIOD:
                windows[own:, lane_block(block)] = halo[: PERIOD - own, :]
        for hop, out in enumerate(outs):
            at = pl.ds(pl.multiple_of((place[0] ^ hop) * BLOCK, BLOCK), BLOCK)
            out[:BLOCK, :] = (cotangent[at, :].astype(F32) * conv[at, :]).astype(BF16)

    spec = dot(forward[...], windows[...])
    resp = response[...].astype(F32)
    f_re, f_im = spread(resp[:BINS]), spread(resp[BINS:])
    g_re, g_im = spec[:BINS], spec[BINS:]
    y = jnp.concatenate([f_re * g_re + f_im * g_im, f_re * g_im - f_im * g_re]).astype(BF16)
    accumulate(step, total, dot(inverse[...], y))

    @pl.when(step == STEPS - 1)
    def _():
        for hop, out in enumerate(outs):
            out[BLOCK:, :] = (total[:, lanes_at(place[0] ^ hop)] * scale).astype(BF16)


def final_kernel(place, *refs):
    ships, (key, value, gate_grad, key_grad, value_grad) = refs[:BLOCKS], refs[BLOCKS:]
    for hop, ship in enumerate(ships):
        at = (slice(None), lanes_at(place[0] ^ hop))
        gate_grad[at] = ship[:BLOCK, :]
        back = ship[BLOCK:, :].astype(F32)
        key_grad[at] = (back * value[at].astype(F32)).astype(BF16)
        value_grad[at] = (back * key[at].astype(F32)).astype(BF16)


def sum_kernel(parts, out):
    for block in range(BLOCKS):
        total = parts[block].astype(F32)
        for source in range(1, parts.shape[0] // BLOCKS):
            total += parts[source * BLOCKS + block].astype(F32)
        out[:, lane_block(block)] = total[: out.shape[0]]


def whole(shape):
    return pl.BlockSpec(shape, lambda *_: (0,) * len(shape))


def shaped(shape, dtype=BF16):
    return jax.ShapeDtypeStruct(shape, dtype)


def call(kernel, in_specs, out_specs, out_shape, scratch=(), steps=1, flops=0):
    return pl.pallas_call(
        kernel,
        grid=(steps,),
        in_specs=in_specs,
        out_specs=out_specs,
        out_shape=out_shape,
        scratch_shapes=scratch,
        compiler_params=pltpu.CompilerParams(
            dimension_semantics=("arbitrary",), vmem_limit_bytes=VMEM_LIMIT
        ),
        cost_estimate=pl.CostEstimate(flops=flops, bytes_accessed=0, transcendentals=0),
    )


VMEM_LIMIT = 56 * MIB
CONV_FLOPS = 6_000_000_000
CROSS_FLOPS = 0
JOIN_FLOPS = 8_000_000_000
BACK_FLOPS = 35_000_000_000


def shift(value, steps):
    count = lax.axis_size(RUNS)
    first, last = max(0, -steps), min(count, count - steps)
    return lax.ppermute(value, RUNS, [(i, i + steps) for i in range(first, last)])


def swap(ships):
    return [ships[0]] + [
        lax.ppermute(ships[hop], GROUP, [(i, i ^ hop) for i in range(BLOCKS)])
        for hop in range(1, BLOCKS)
    ]


def exchange(value, axes):
    return lax.all_to_all(value, axes, split_axis=0, concat_axis=0, tiled=True)


def body(forward, own, first, lagged, last, gate_input, key_input, value_input, out_grad, filter_taps):
    lags = filter_taps.shape[0]
    held, channels = out_grad.shape
    share = lags // lax.axis_size(CTX)
    norm = 2.0 / PERIOD / lags**0.5
    local = (BLOCK, WIDE)
    ship = (2 * BLOCK, LANES)
    pieces = (channels // LANES, held, LANES)
    flat = (TOKENS, LANES)
    reach = (lags, LANES)
    slots = (lags // share, SLOT, LANES)
    scalar = pl.BlockSpec(memory_space=pltpu.SMEM)
    place = lax.axis_index(GROUP).reshape(1)

    *ships, cotangent = call(
        prep_kernel,
        [scalar] + [whole(local)] * 3 + [whole(out_grad.shape)],
        [whole(ship)] * BLOCKS + [whole(pieces)],
        [shaped(ship)] * BLOCKS + [shaped(pieces)],
    )(place, key_input, value_input, gate_input, out_grad)
    cotangent = exchange(cotangent, GROUP + CH).reshape(flat)
    mixed, tail, gate = call(
        join_kernel,
        [scalar] + [whole(ship)] * BLOCKS,
        [whole(flat), whole(reach), whole(flat)],
        [shaped(flat), shaped(reach), shaped(flat)],
        flops=JOIN_FLOPS,
    )(place, *swap(ships))
    mixed_halo = shift(tail, 1)
    taps = lax.dynamic_slice_in_dim(filter_taps, lax.axis_index(GROUP) * LANES, LANES, 1)

    def stepped(*shape):
        return pl.BlockSpec((None,) + shape, lambda step: (step, 0, 0))

    table = stepped(ROWS, PERIOD)
    bins = pl.BlockSpec((ROWS, WIDE), lambda step: (step, 0))
    narrow_bins = pl.BlockSpec((ROWS, LANES), lambda step: (step, 0))
    conv, spectrum, response = call(
        functools.partial(conv_kernel, norm),
        [
            table,
            stepped(BLOCK, ROWS),
            whole(reach),
            whole(flat),
            whole(reach),
        ],
        [whole(flat), bins, narrow_bins],
        [shaped(flat, F32), shaped((PERIOD, WIDE)), shaped((PERIOD, LANES))],
        [pltpu.VMEM((PERIOD, WIDE), BF16), pltpu.VMEM(local, F32)],
        STEPS,
        CONV_FLOPS,
    )(forward, last, mixed_halo, mixed, taps)

    grad, head, lag_grad = call(
        functools.partial(cross_kernel, norm),
        [
            stepped(ROWS, BLOCK),
            stepped(lags, ROWS),
            whole(flat),
            whole(flat),
            bins,
        ],
        [whole(flat), whole(reach), whole(slots)],
        [shaped(flat), shaped(reach), shaped(slots)],
        [pltpu.VMEM(local, BF16), pltpu.VMEM((lags + SLOT, LANES), F32)],
        STEPS,
        CROSS_FLOPS,
    )(own, lagged, cotangent, gate, spectrum)
    grad_halo = shift(head, -1)
    lag_parts = exchange(lag_grad, CTX)

    ships = call(
        functools.partial(back_kernel, norm),
        [
            scalar,
            table,
            stepped(BLOCK, ROWS),
            whole(flat),
            whole(reach),
            narrow_bins,
            whole(flat),
            whole(flat),
        ],
        [whole(ship)] * BLOCKS,
        [shaped(ship)] * BLOCKS,
        [pltpu.VMEM((PERIOD, WIDE), BF16), pltpu.VMEM(local, F32)],
        STEPS,
        BACK_FLOPS,
    )(place, forward, first, grad, grad_halo, response, conv, cotangent)
    gate_grad, key_grad, value_grad = call(
        final_kernel,
        [scalar] + [whole(ship)] * BLOCKS + [whole(local)] * 2,
        [whole(local)] * 3,
        [shaped(local)] * 3,
    )(place, *swap(ships), key_input, value_input)
    filter_grad = call(
        sum_kernel,
        [whole(lag_parts.shape)],
        whole((share, WIDE)),
        shaped((share, WIDE), F32),
    )(lag_parts)
    return gate_grad, key_grad, value_grad, filter_grad


def solution(mesh):
    split = Mesh(mesh.devices.reshape(SIZES), AXES)
    spans = P(CTX, CH)
    mapped = jax.shard_map(
        body,
        mesh=split,
        in_specs=(P(), P(), P(), P(), P(), spans, spans, spans, P(CTX + CH, None), P(None, CH)),
        out_specs=(spans, spans, spans, spans),
        check_vma=False,
    )

    def run(gate_input, key_input, value_input, out_grad, filter_taps):
        lags = filter_taps.shape[0]
        tables = make_tables(lags)
        return mapped(*tables, gate_input, key_input, value_input, out_grad, filter_taps)

    return run
```

```python
import functools
import math

import jax
import jax.numpy as jnp
import ml_dtypes
import numpy as np
from jax import lax
from jax.experimental import pallas as pl
from jax.experimental.pallas import tpu as pltpu
from jax.sharding import Mesh, PartitionSpec as P

BF16 = jnp.bfloat16
F32 = jnp.float32
AXES = ("z", "yh", "yl", "c", "x", "zh")
SIZES = (8, 2, 2, 2, 4, 2)
CTX = ("z", "yh", "yl", "c")
GROUP = ("yl", "c")
RUNS = ("z", "yh")
CH = ("x", "zh")

BLOCK = 256
PERIOD = 1024
LANES = 128
BLOCKS = 4
TOKENS = BLOCKS * BLOCK
WIDE = BLOCKS * LANES
BINS = 512
STEPS = PERIOD // 2 // BINS
ROWS = 2 * BINS
SLOT = 16
MIB = 1024 * 1024


def make_tables(lags):
    freq = np.arange(PERIOD // 2)[:, None]
    place = np.arange(PERIOD)[None, :]
    angle = math.pi / PERIOD * ((2 * freq + 1) * place % (2 * PERIOD)).astype(np.float64)
    both = np.stack([np.cos(angle), -np.sin(angle)])
    both = both.reshape(2, STEPS, BINS, PERIOD).transpose(1, 0, 2, 3).reshape(STEPS, ROWS, PERIOD)
    back = both.transpose(0, 2, 1)
    tables = both, both[:, :, lags:], back[:, :BLOCK], back[:, :lags], back[:, lags:]
    return tuple(np.ascontiguousarray(t).astype(ml_dtypes.bfloat16) for t in tables)


def dot(a, b):
    return jnp.dot(a, b, preferred_element_type=F32)


def lane_block(index):
    return slice(index * LANES, (index + 1) * LANES)


def lanes_at(index):
    return pl.ds(pl.multiple_of(index * LANES, LANES), LANES)


def rows_at(index):
    return pl.ds(pl.multiple_of(index * BLOCK, BLOCK), BLOCK)


def token_block(index):
    return slice(index * BLOCK, (index + 1) * BLOCK)


def spread(part):
    return jnp.concatenate([part] * BLOCKS, axis=1)


def accumulate(step, total, part):
    @pl.when(step == 0)
    def _():
        total[...] = part

    @pl.when(step > 0)
    def _():
        total[...] += part


def prep_kernel(place, key, value, gate, out_grad, mixed, *outs):
    ships, pieces = outs[:BLOCKS], outs[BLOCKS]
    product = (key[...].astype(F32) * value[...].astype(F32)).astype(BF16)
    for block in range(BLOCKS):
        mixed[block] = product[:, lane_block(block)]
    for hop, ship in enumerate(ships):
        ship[...] = gate[:, lanes_at(place[0] ^ hop)]
    count = pieces.shape[0]
    for piece in range(count):
        target = piece % BLOCKS * (count // BLOCKS) + piece // BLOCKS
        pieces[target] = out_grad[:, lane_block(piece)]


def conv_kernel(scale, forward, inverse, halo, mixed, taps, conv, spectrum, response, windows, total):
    step = pl.program_id(0)
    lags = taps.shape[0]

    @pl.when(step == 0)
    def _():
        for block in range(BLOCKS):
            early = lags - block * BLOCK
            if early:
                windows[:early, lane_block(block)] = halo[block * BLOCK :, :]
            windows[early:, lane_block(block)] = mixed[: (block + 1) * BLOCK, :]

    resp = dot(forward[:, :lags], taps[...])
    response[...] = resp.astype(BF16)
    spec = dot(forward[...], windows[...])
    spectrum[...] = spec.astype(BF16)
    f_re, f_im = spread(resp[:BINS]), spread(resp[BINS:])
    x_re, x_im = spec[:BINS], spec[BINS:]
    y = jnp.concatenate([f_re * x_re - f_im * x_im, f_re * x_im + f_im * x_re]).astype(BF16)
    accumulate(step, total, dot(inverse[...], y))

    @pl.when(step == STEPS - 1)
    def _():
        for block in range(BLOCKS):
            conv[token_block(block), :] = total[:, lane_block(block)] * scale


def cross_kernel(scale, place, forward, inverse, cotangent, spectrum, *refs):
    gates, (grad, head, lag_grad, windows, total) = refs[:BLOCKS], refs[BLOCKS:]
    step = pl.program_id(0)

    @pl.when(step == 0)
    def _():
        for hop, gate in enumerate(gates):
            block = place[0] ^ hop
            at = rows_at(block)
            product = (cotangent[at, :].astype(F32) * gate[...].astype(F32)).astype(BF16)
            grad[at, :] = product
            windows[:, lanes_at(block)] = product
        head[...] = grad[: head.shape[0], :]

    spec = dot(forward[...], windows[...])
    g_re, g_im = spec[:BINS], spec[BINS:]
    full = spectrum[...].astype(F32)
    x_re, x_im = full[:BINS], full[BINS:]
    re = g_re * x_re + g_im * x_im
    im = g_im * x_re - g_re * x_im
    re = sum(re[:, lane_block(b)] for b in range(BLOCKS))
    im = sum(im[:, lane_block(b)] for b in range(BLOCKS))
    lags = inverse.shape[0]
    part = dot(inverse[...], jnp.concatenate([re, im]).astype(BF16))

    @pl.when(step == 0)
    def _():
        total[:lags, :] = part
        total[lags:, :] = jnp.zeros_like(total[lags:, :])

    @pl.when(step > 0)
    def _():
        total[:lags, :] += part

    @pl.when(step == STEPS - 1)
    def _():
        count = lag_grad.shape[0]
        share = lags // count
        for slot in range(count):
            rows = total[slot * share : slot * share + SLOT, :] * scale
            lag_grad[slot] = rows.astype(BF16)


def back_kernel(
    scale, place, forward, inverse, grad, halo, response, conv, cotangent, *refs
):
    outs, (windows, total) = refs[:BLOCKS], refs[BLOCKS:]
    step = pl.program_id(0)

    @pl.when(step == 0)
    def _():
        for block in range(BLOCKS):
            own = min(PERIOD, TOKENS - block * BLOCK)
            windows[:own, lane_block(block)] = grad[block * BLOCK : block * BLOCK + own, :]
            if own < PERIOD:
                windows[own:, lane_block(block)] = halo[: PERIOD - own, :]
        for hop, out in enumerate(outs):
            at = rows_at(place[0] ^ hop)
            out[:BLOCK, :] = (cotangent[at, :].astype(F32) * conv[at, :]).astype(BF16)

    spec = dot(forward[...], windows[...])
    resp = response[...].astype(F32)
    f_re, f_im = spread(resp[:BINS]), spread(resp[BINS:])
    g_re, g_im = spec[:BINS], spec[BINS:]
    y = jnp.concatenate([f_re * g_re + f_im * g_im, f_re * g_im - f_im * g_re]).astype(BF16)
    accumulate(step, total, dot(inverse[...], y))

    @pl.when(step == STEPS - 1)
    def _():
        for hop, out in enumerate(outs):
            out[BLOCK:, :] = (total[:, lanes_at(place[0] ^ hop)] * scale).astype(BF16)


def final_kernel(place, *refs):
    ships, (key, value, parts, gate_grad, key_grad, value_grad, lag_grad) = (
        refs[:BLOCKS],
        refs[BLOCKS:],
    )
    for hop, ship in enumerate(ships):
        at = (slice(None), lanes_at(place[0] ^ hop))
        gate_grad[at] = ship[:BLOCK, :]
        back = ship[BLOCK:, :].astype(F32)
        key_grad[at] = (back * value[at].astype(F32)).astype(BF16)
        value_grad[at] = (back * key[at].astype(F32)).astype(BF16)
    for block in range(BLOCKS):
        total = parts[block].astype(F32)
        for source in range(1, parts.shape[0] // BLOCKS):
            total += parts[source * BLOCKS + block].astype(F32)
        lag_grad[:, lane_block(block)] = total[: lag_grad.shape[0]]


def whole(shape):
    return pl.BlockSpec(shape, lambda *_: (0,) * len(shape))


def shaped(shape, dtype=BF16):
    return jax.ShapeDtypeStruct(shape, dtype)


def call(kernel, in_specs, out_specs, out_shape, scratch=(), steps=1, flops=0, limit=None):
    return pl.pallas_call(
        kernel,
        grid=(steps,),
        in_specs=in_specs,
        out_specs=out_specs,
        out_shape=out_shape,
        scratch_shapes=scratch,
        compiler_params=pltpu.CompilerParams(
            dimension_semantics=("arbitrary",), vmem_limit_bytes=limit or VMEM_LIMIT
        ),
        cost_estimate=pl.CostEstimate(flops=flops, bytes_accessed=0, transcendentals=0),
    )


VMEM_LIMIT = 56 * MIB
FINAL_LIMIT = 16 * MIB
CONV_FLOPS = 24_000_000_000
CROSS_FLOPS = 0
BACK_FLOPS = 35_000_000_000


def shift(value, steps):
    count = lax.axis_size(RUNS)
    first, last = max(0, -steps), min(count, count - steps)
    return lax.ppermute(value, RUNS, [(i, i + steps) for i in range(first, last)])


def swap(ships):
    return [ships[0]] + [
        lax.ppermute(ships[hop], GROUP, [(i, i ^ hop) for i in range(BLOCKS)])
        for hop in range(1, BLOCKS)
    ]


def exchange(value, axes):
    return lax.all_to_all(value, axes, split_axis=0, concat_axis=0, tiled=True)


def body(forward, own, first, lagged, last, gate_input, key_input, value_input, out_grad, filter_taps):
    lags = filter_taps.shape[0]
    held, channels = out_grad.shape
    share = lags // lax.axis_size(CTX)
    norm = 2.0 / PERIOD / lags**0.5
    local = (BLOCK, WIDE)
    ship = (2 * BLOCK, LANES)
    pieces = (channels // LANES, held, LANES)
    flat = (TOKENS, LANES)
    reach = (lags, LANES)
    slots = (lags // share, SLOT, LANES)
    scalar = pl.BlockSpec(memory_space=pltpu.SMEM)
    place = lax.axis_index(GROUP).reshape(1)

    part = (BLOCK, LANES)
    by_block = (BLOCKS, BLOCK, LANES)
    mixed, *gates, cotangent = call(
        prep_kernel,
        [scalar] + [whole(local)] * 3 + [whole(out_grad.shape)],
        [whole(by_block)] + [whole(part)] * BLOCKS + [whole(pieces)],
        [shaped(by_block)] + [shaped(part)] * BLOCKS + [shaped(pieces)],
    )(place, key_input, value_input, gate_input, out_grad)
    mixed = exchange(mixed, GROUP).reshape(flat)
    mixed_halo = shift(mixed[TOKENS - lags :], 1)
    cotangent = exchange(cotangent, GROUP + CH).reshape(flat)
    gates = swap(gates)
    taps = lax.dynamic_slice_in_dim(filter_taps, lax.axis_index(GROUP) * LANES, LANES, 1)

    def stepped(*shape):
        return pl.BlockSpec((None,) + shape, lambda step: (step, 0, 0))

    table = stepped(ROWS, PERIOD)
    bins = pl.BlockSpec((ROWS, WIDE), lambda step: (step, 0))
    narrow_bins = pl.BlockSpec((ROWS, LANES), lambda step: (step, 0))
    conv, spectrum, response = call(
        functools.partial(conv_kernel, norm),
        [
            table,
            stepped(BLOCK, ROWS),
            whole(reach),
            whole(flat),
            whole(reach),
        ],
        [whole(flat), bins, narrow_bins],
        [shaped(flat, F32), shaped((PERIOD, WIDE)), shaped((PERIOD, LANES))],
        [pltpu.VMEM((PERIOD, WIDE), BF16), pltpu.VMEM(local, F32)],
        STEPS,
        CONV_FLOPS,
    )(forward, last, mixed_halo, mixed, taps)

    grad, head, lag_grad = call(
        functools.partial(cross_kernel, norm),
        [
            scalar,
            stepped(ROWS, BLOCK),
            stepped(lags, ROWS),
            whole(flat),
            bins,
        ]
        + [whole(part)] * BLOCKS,
        [whole(flat), whole(reach), whole(slots)],
        [shaped(flat), shaped(reach), shaped(slots)],
        [pltpu.VMEM(local, BF16), pltpu.VMEM((lags + SLOT, LANES), F32)],
        STEPS,
        CROSS_FLOPS,
    )(place, own, lagged, cotangent, spectrum, *gates)
    grad_halo = shift(head, -1)
    lag_parts = exchange(lag_grad, CTX)

    ships = call(
        functools.partial(back_kernel, norm),
        [
            scalar,
            table,
            stepped(BLOCK, ROWS),
            whole(flat),
            whole(reach),
            narrow_bins,
            whole(flat),
            whole(flat),
        ],
        [whole(ship)] * BLOCKS,
        [shaped(ship)] * BLOCKS,
        [pltpu.VMEM((PERIOD, WIDE), BF16), pltpu.VMEM(local, F32)],
        STEPS,
        BACK_FLOPS,
    )(place, forward, first, grad, grad_halo, response, conv, cotangent)
    gate_grad, key_grad, value_grad, filter_grad = call(
        final_kernel,
        [scalar] + [whole(ship)] * BLOCKS + [whole(local)] * 2 + [whole(slots)],
        [whole(local)] * 3 + [whole((share, WIDE))],
        [shaped(local)] * 3 + [shaped((share, WIDE), F32)],
        limit=FINAL_LIMIT,
    )(place, *swap(ships), key_input, value_input, lag_parts)
    return gate_grad, key_grad, value_grad, filter_grad


def solution(mesh):
    split = Mesh(mesh.devices.reshape(SIZES), AXES)
    spans = P(CTX, CH)
    mapped = jax.shard_map(
        body,
        mesh=split,
        in_specs=(P(), P(), P(), P(), P(), spans, spans, spans, P(CTX + CH, None), P(None, CH)),
        out_specs=(spans, spans, spans, spans),
        check_vma=False,
    )

    def run(gate_input, key_input, value_input, out_grad, filter_taps):
        lags = filter_taps.shape[0]
        tables = make_tables(lags)
        return mapped(*tables, gate_input, key_input, value_input, out_grad, filter_taps)

    return run
```

```python
import functools
import math

import jax
import jax.numpy as jnp
import ml_dtypes
import numpy as np
from jax import lax
from jax.experimental import pallas as pl
from jax.experimental.pallas import tpu as pltpu
from jax.sharding import Mesh, PartitionSpec as P

BF16 = jnp.bfloat16
F32 = jnp.float32
AXES = ("z", "yh", "yl", "c", "x", "zh")
SIZES = (8, 2, 2, 2, 4, 2)
CTX = ("z", "yh", "yl", "c")
GROUP = ("yl", "c")
RUNS = ("z", "yh")
CH = ("x", "zh")

BLOCK = 256
PERIOD = 1024
LANES = 128
BLOCKS = 4
TOKENS = BLOCKS * BLOCK
WIDE = BLOCKS * LANES
BINS = 512
STEPS = PERIOD // 2 // BINS
ROWS = 2 * BINS
SLOT = 16
MIB = 1024 * 1024


def make_tables(lags):
    freq = np.arange(PERIOD // 2)[:, None]
    place = np.arange(PERIOD)[None, :]
    angle = math.pi / PERIOD * ((2 * freq + 1) * place % (2 * PERIOD)).astype(np.float64)
    both = np.stack([np.cos(angle), -np.sin(angle)])
    both = both.reshape(2, STEPS, BINS, PERIOD).transpose(1, 0, 2, 3).reshape(STEPS, ROWS, PERIOD)
    back = both.transpose(0, 2, 1)
    tables = both, both[:, :, lags:], back[:, :BLOCK], back[:, :lags], back[:, lags:]
    return tuple(np.ascontiguousarray(t).astype(ml_dtypes.bfloat16) for t in tables)


def dot(a, b):
    return jnp.dot(a, b, preferred_element_type=F32)


def lane_block(index):
    return slice(index * LANES, (index + 1) * LANES)


def lanes_at(index):
    return pl.ds(pl.multiple_of(index * LANES, LANES), LANES)


def rows_at(index):
    return pl.ds(pl.multiple_of(index * BLOCK, BLOCK), BLOCK)


def token_block(index):
    return slice(index * BLOCK, (index + 1) * BLOCK)


def spread(part):
    return jnp.concatenate([part] * BLOCKS, axis=1)


def accumulate(step, total, part):
    @pl.when(step == 0)
    def _():
        total[...] = part

    @pl.when(step > 0)
    def _():
        total[...] += part


def prep_kernel(place, key, value, out_grad, *outs):
    ships, pieces = outs[:BLOCKS], outs[BLOCKS]
    for hop, ship in enumerate(ships):
        at = (slice(None), lanes_at(place[0] ^ hop))
        ship[...] = (key[at].astype(F32) * value[at].astype(F32)).astype(BF16)
    for piece in range(pieces.shape[0]):
        pieces[piece] = out_grad[:, piece * WIDE : (piece + 1) * WIDE]


def join_kernel(place, *refs):
    ships, (mixed, tail) = refs[:BLOCKS], refs[BLOCKS:]
    for hop, ship in enumerate(ships):
        mixed[rows_at(place[0] ^ hop), :] = ship[...]
    tail[...] = mixed[TOKENS - tail.shape[0] :, :]


def grad_kernel(cotangent, gate, grad):
    product = (cotangent[...].astype(F32) * gate[...].astype(F32)).astype(BF16)
    for block in range(BLOCKS):
        grad[block] = product[:, lane_block(block)]


def conv_kernel(
    scale, place, forward, inverse, halo, mixed, taps, conv, spectrum, response, windows, total
):
    step = pl.program_id(0)
    lags = taps.shape[0]

    @pl.when(step == 0)
    def _():
        for block in range(BLOCKS):
            early = lags - block * BLOCK
            if early:
                windows[:early, lane_block(block)] = halo[block * BLOCK :, :]
            windows[early:, lane_block(block)] = mixed[: (block + 1) * BLOCK, :]

    resp = dot(forward[:, :lags], taps[...])
    response[...] = resp.astype(BF16)
    spec = dot(forward[...], windows[...])
    spectrum[...] = spec.astype(BF16)
    f_re, f_im = spread(resp[:BINS]), spread(resp[BINS:])
    x_re, x_im = spec[:BINS], spec[BINS:]
    y = jnp.concatenate([f_re * x_re - f_im * x_im, f_re * x_im + f_im * x_re]).astype(BF16)
    accumulate(step, total, dot(inverse[...], y))

    @pl.when(step == STEPS - 1)
    def _():
        for block in range(BLOCKS):
            conv[token_block(block), :] = (total[:, lane_block(block)] * scale).astype(BF16)


def cross_kernel(scale, forward, inverse, grad, spectrum, head, lag_grad, windows, total):
    step = pl.program_id(0)

    @pl.when(step == 0)
    def _():
        head[...] = grad[: head.shape[0], :]
        for block in range(BLOCKS):
            windows[:, lane_block(block)] = grad[token_block(block), :]

    spec = dot(forward[...], windows[...])
    g_re, g_im = spec[:BINS], spec[BINS:]
    full = spectrum[...].astype(F32)
    x_re, x_im = full[:BINS], full[BINS:]
    re = g_re * x_re + g_im * x_im
    im = g_im * x_re - g_re * x_im
    re = sum(re[:, lane_block(b)] for b in range(BLOCKS))
    im = sum(im[:, lane_block(b)] for b in range(BLOCKS))
    lags = inverse.shape[0]
    part = dot(inverse[...], jnp.concatenate([re, im]).astype(BF16))

    @pl.when(step == 0)
    def _():
        total[:lags, :] = part
        total[lags:, :] = jnp.zeros_like(total[lags:, :])

    @pl.when(step > 0)
    def _():
        total[:lags, :] += part

    @pl.when(step == STEPS - 1)
    def _():
        count = lag_grad.shape[0]
        share = lags // count
        for slot in range(count):
            rows = total[slot * share : slot * share + SLOT, :] * scale
            lag_grad[slot] = rows.astype(BF16)


def back_kernel(scale, place, forward, inverse, grad, halo, response, conv, *refs):
    outs, (windows, total) = refs[:BLOCKS], refs[BLOCKS:]
    step = pl.program_id(0)

    @pl.when(step == 0)
    def _():
        for block in range(BLOCKS):
            own = min(PERIOD, TOKENS - block * BLOCK)
            windows[:own, lane_block(block)] = grad[block * BLOCK : block * BLOCK + own, :]
            if own < PERIOD:
                windows[own:, lane_block(block)] = halo[: PERIOD - own, :]
        for hop, out in enumerate(outs):
            out[:BLOCK, :] = conv[rows_at(place[0] ^ hop), :]

    spec = dot(forward[...], windows[...])
    resp = response[...].astype(F32)
    f_re, f_im = spread(resp[:BINS]), spread(resp[BINS:])
    g_re, g_im = spec[:BINS], spec[BINS:]
    y = jnp.concatenate([f_re * g_re + f_im * g_im, f_re * g_im - f_im * g_re]).astype(BF16)
    accumulate(step, total, dot(inverse[...], y))

    @pl.when(step == STEPS - 1)
    def _():
        for hop, out in enumerate(outs):
            out[BLOCK:, :] = (total[:, lanes_at(place[0] ^ hop)] * scale).astype(BF16)


def final_kernel(place, *refs):
    ships, refs = refs[:BLOCKS], refs[BLOCKS:]
    cotangent, key, value, parts, gate_grad, key_grad, value_grad, lag_grad = refs
    for hop, ship in enumerate(ships):
        at = (slice(None), lanes_at(place[0] ^ hop))
        conv, back = ship[:BLOCK, :].astype(F32), ship[BLOCK:, :].astype(F32)
        gate_grad[at] = (cotangent[at].astype(F32) * conv).astype(BF16)
        key_grad[at] = (back * value[at].astype(F32)).astype(BF16)
        value_grad[at] = (back * key[at].astype(F32)).astype(BF16)
    for block in range(BLOCKS):
        total = parts[block].astype(F32)
        for source in range(1, parts.shape[0] // BLOCKS):
            total += parts[source * BLOCKS + block].astype(F32)
        lag_grad[:, lane_block(block)] = total[: lag_grad.shape[0]]


def whole(shape):
    return pl.BlockSpec(shape, lambda *_: (0,) * len(shape))


def shaped(shape, dtype=BF16):
    return jax.ShapeDtypeStruct(shape, dtype)


def call(kernel, in_specs, out_specs, out_shape, scratch=(), steps=1, flops=0, limit=None, scalars=0):
    return pl.pallas_call(
        kernel,
        grid_spec=pltpu.PrefetchScalarGridSpec(
            num_scalar_prefetch=scalars,
            grid=(steps,),
            in_specs=in_specs,
            out_specs=out_specs,
            scratch_shapes=scratch,
        ),
        out_shape=out_shape,
        compiler_params=pltpu.CompilerParams(
            dimension_semantics=("arbitrary",), vmem_limit_bytes=limit or VMEM_LIMIT
        ),
        cost_estimate=pl.CostEstimate(flops=flops, bytes_accessed=0, transcendentals=0),
    )


VMEM_LIMIT = 56 * MIB
FINAL_LIMIT = 16 * MIB
CONV_FLOPS = 24_000_000_000
CROSS_FLOPS = 0
JOIN_FLOPS = 0
BACK_FLOPS = 35_000_000_000


def shift(value, steps):
    count = lax.axis_size(RUNS)
    first, last = max(0, -steps), min(count, count - steps)
    return lax.ppermute(value, RUNS, [(i, i + steps) for i in range(first, last)])


def swap(ships):
    return [ships[0]] + [
        lax.ppermute(ships[hop], GROUP, [(i, i ^ hop) for i in range(BLOCKS)])
        for hop in range(1, BLOCKS)
    ]


def exchange(value, axes):
    return lax.all_to_all(value, axes, split_axis=0, concat_axis=0, tiled=True)


def body(forward, own, first, lagged, last, gate_input, key_input, value_input, out_grad, filter_taps):
    lags = filter_taps.shape[0]
    held, channels = out_grad.shape
    share = lags // lax.axis_size(CTX)
    norm = 2.0 / PERIOD / lags**0.5
    local = (BLOCK, WIDE)
    ship = (2 * BLOCK, LANES)
    pieces = (channels // WIDE, held, WIDE)
    flat = (TOKENS, LANES)
    reach = (lags, LANES)
    slots = (lags // share, SLOT, LANES)
    scalar = pl.BlockSpec(memory_space=pltpu.SMEM)
    place = lax.axis_index(GROUP).reshape(1)

    part = (BLOCK, LANES)
    by_block = (BLOCKS, BLOCK, LANES)
    *ships, cotangent = call(
        prep_kernel,
        [scalar] + [whole(local)] * 2 + [whole(out_grad.shape)],
        [whole(part)] * BLOCKS + [whole(pieces)],
        [shaped(part)] * BLOCKS + [shaped(pieces)],
    )(place, key_input, value_input, out_grad)
    cotangent = exchange(cotangent, CH).reshape(local)
    mixed, tail = call(
        join_kernel,
        [scalar] + [whole(part)] * BLOCKS,
        [whole(flat), whole(reach)],
        [shaped(flat), shaped(reach)],
        flops=JOIN_FLOPS,
    )(place, *swap(ships))
    mixed_halo = shift(tail, 1)
    grad = call(grad_kernel, [whole(local)] * 2, whole(by_block), shaped(by_block))(
        cotangent, gate_input
    )
    grad = exchange(grad, GROUP).reshape(flat)

    def stepped(*shape):
        return pl.BlockSpec((None,) + shape, lambda step, *_: (step, 0, 0))

    table = stepped(ROWS, PERIOD)
    bins = pl.BlockSpec((ROWS, WIDE), lambda step, *_: (step, 0))
    narrow_bins = pl.BlockSpec((ROWS, LANES), lambda step, *_: (step, 0))
    conv, spectrum, response = call(
        functools.partial(conv_kernel, norm),
        [
            table,
            stepped(BLOCK, ROWS),
            whole(reach),
            whole(flat),
            pl.BlockSpec(reach, lambda step, place: (0, place[0])),
        ],
        [whole(flat), bins, narrow_bins],
        [shaped(flat), shaped((PERIOD, WIDE)), shaped((PERIOD, LANES))],
        [pltpu.VMEM((PERIOD, WIDE), BF16), pltpu.VMEM(local, F32)],
        STEPS,
        CONV_FLOPS,
        scalars=1,
    )(place, forward, last, mixed_halo, mixed, filter_taps)

    head, lag_grad = call(
        functools.partial(cross_kernel, norm),
        [stepped(ROWS, BLOCK), stepped(lags, ROWS), whole(flat), bins],
        [whole(reach), whole(slots)],
        [shaped(reach), shaped(slots)],
        [pltpu.VMEM(local, BF16), pltpu.VMEM((lags + SLOT, LANES), F32)],
        STEPS,
        CROSS_FLOPS,
    )(own, lagged, grad, spectrum)
    grad_halo = shift(head, -1)
    lag_parts = exchange(lag_grad, CTX)

    ships = call(
        functools.partial(back_kernel, norm),
        [
            scalar,
            table,
            stepped(BLOCK, ROWS),
            whole(flat),
            whole(reach),
            narrow_bins,
            whole(flat),
        ],
        [whole(ship)] * BLOCKS,
        [shaped(ship)] * BLOCKS,
        [pltpu.VMEM((PERIOD, WIDE), BF16), pltpu.VMEM(local, F32)],
        STEPS,
        BACK_FLOPS,
    )(place, forward, first, grad, grad_halo, response, conv)
    gate_grad, key_grad, value_grad, filter_grad = call(
        final_kernel,
        [scalar] + [whole(ship)] * BLOCKS + [whole(local)] * 3 + [whole(slots)],
        [whole(local)] * 3 + [whole((share, WIDE))],
        [shaped(local)] * 3 + [shaped((share, WIDE), F32)],
        limit=FINAL_LIMIT,
    )(place, *swap(ships), cotangent, key_input, value_input, lag_parts)
    return gate_grad, key_grad, value_grad, filter_grad


def solution(mesh):
    split = Mesh(mesh.devices.reshape(SIZES), AXES)
    spans = P(CTX, CH)
    mapped = jax.shard_map(
        body,
        mesh=split,
        in_specs=(P(), P(), P(), P(), P(), spans, spans, spans, P(CTX + CH, None), P(None, CH)),
        out_specs=(spans, spans, spans, spans),
        check_vma=False,
    )

    def run(gate_input, key_input, value_input, out_grad, filter_taps):
        lags = filter_taps.shape[0]
        tables = make_tables(lags)
        return mapped(*tables, gate_input, key_input, value_input, out_grad, filter_taps)

    return run
```

```python
import functools
import math

import jax
import jax.numpy as jnp
import ml_dtypes
import numpy as np
from jax import lax
from jax.experimental import pallas as pl
from jax.experimental.pallas import tpu as pltpu
from jax.sharding import Mesh, PartitionSpec as P

BF16 = jnp.bfloat16
F32 = jnp.float32
AXES = ("z", "yh", "yl", "c", "x", "zh")
SIZES = (8, 2, 2, 2, 4, 2)
CTX = ("z", "yh", "yl", "c")
GROUP = ("yl", "c")
RUNS = ("z", "yh")
CH = ("x", "zh")

BLOCK = 256
PERIOD = 1024
LANES = 128
BLOCKS = 4
TOKENS = BLOCKS * BLOCK
WIDE = BLOCKS * LANES
BINS = 128
STEPS = PERIOD // 2 // BINS
ROWS = 2 * BINS
SLOT = 16
MIB = 1024 * 1024


def make_tables(lags):
    freq = np.arange(PERIOD // 2)[:, None]
    place = np.arange(PERIOD)[None, :]
    angle = math.pi / PERIOD * ((2 * freq + 1) * place % (2 * PERIOD)).astype(np.float64)
    both = np.stack([np.cos(angle), -np.sin(angle)])
    both = both.reshape(2, STEPS, BINS, PERIOD).transpose(1, 0, 2, 3).reshape(STEPS, ROWS, PERIOD)
    back = both.transpose(0, 2, 1)
    tables = both, both[:, :, lags:], back[:, :BLOCK], back[:, :lags], back[:, lags:]
    return tuple(np.ascontiguousarray(t).astype(ml_dtypes.bfloat16) for t in tables)


def dot(a, b):
    return jnp.dot(a, b, preferred_element_type=F32)


def lane_block(index):
    return slice(index * LANES, (index + 1) * LANES)


def lanes_at(index):
    return pl.ds(pl.multiple_of(index * LANES, LANES), LANES)


def rows_at(index):
    return pl.ds(pl.multiple_of(index * BLOCK, BLOCK), BLOCK)


def token_block(index):
    return slice(index * BLOCK, (index + 1) * BLOCK)


def spread(part):
    return jnp.concatenate([part] * BLOCKS, axis=1)


def start(source, target, sem):
    copy = pltpu.make_async_copy(source, target, sem)
    copy.start()
    return copy


def wait(copies):
    for copy in copies:
        copy.wait()


def start_chunks(sources, targets, sems):
    return [
        [
            start(source.at[chunk], target.at[chunk], sems.at[number, chunk])
            for number, (source, target) in enumerate(zip(sources, targets))
        ]
        for chunk in range(STEPS)
    ]


def prep_kernel(place, key, value, out_grad, *outs):
    ships, pieces = outs[:BLOCKS], outs[BLOCKS]
    for hop, ship in enumerate(ships):
        at = (slice(None), lanes_at(place[0] ^ hop))
        ship[...] = (key[at].astype(F32) * value[at].astype(F32)).astype(BF16)
    for piece in range(pieces.shape[0]):
        pieces[piece] = out_grad[:, piece * WIDE : (piece + 1) * WIDE]


def join_kernel(place, *refs):
    ships, (mixed, tail) = refs[:BLOCKS], refs[BLOCKS:]
    for hop, ship in enumerate(ships):
        mixed[rows_at(place[0] ^ hop), :] = ship[...]
    tail[...] = mixed[TOKENS - tail.shape[0] :, :]


def conv_kernel(
    scale,
    place,
    forward,
    inverse,
    halo,
    mixed,
    taps,
    conv,
    spectrum,
    response,
    table,
    back,
    windows,
    filt,
    spec_out,
    sems,
    small_sems,
    out_sems,
):
    lags = halo.shape[0]
    copies = [start(taps.at[:, lanes_at(place[0])], filt, small_sems.at[0])]
    for block in range(BLOCKS):
        early = lags - block * BLOCK
        target = windows.at[early:, lane_block(block)]
        copies.append(start(mixed.at[: (block + 1) * BLOCK], target, small_sems.at[1 + block]))
    for block in range(BLOCKS - 1):
        early = lags - block * BLOCK
        target = windows.at[:early, lane_block(block)]
        sem = small_sems.at[1 + BLOCKS + block]
        copies.append(start(halo.at[block * BLOCK :], target, sem))
    chunks = start_chunks((forward, inverse), (table, back), sems)
    wait(copies)
    outs = []
    for chunk in range(STEPS):
        wait(chunks[chunk])
        resp = dot(table[chunk, :, :lags], filt[...])
        response[chunk] = resp.astype(BF16)
        spec = dot(table[chunk], windows[...])
        spec_out[chunk] = spec.astype(BF16)
        outs.append(start(spec_out.at[chunk], spectrum.at[chunk], out_sems.at[chunk]))
        f_re, f_im = spread(resp[:BINS]), spread(resp[BINS:])
        x_re, x_im = spec[:BINS], spec[BINS:]
        y = jnp.concatenate([f_re * x_re - f_im * x_im, f_re * x_im + f_im * x_re])
        part = dot(back[chunk], y.astype(BF16))
        total = total + part if chunk else part
    for block in range(BLOCKS):
        conv[token_block(block), :] = (total[:, lane_block(block)] * scale).astype(BF16)
    wait(outs)


def cross_kernel(
    scale,
    forward,
    inverse,
    grad,
    spectrum,
    head,
    lag_grad,
    table,
    back,
    spec_in,
    windows,
    total,
    sems,
    small_sems,
):
    lags = head.shape[0]
    copies = [
        start(grad.at[token_block(b)], windows.at[:, lane_block(b)], small_sems.at[b])
        for b in range(BLOCKS)
    ]
    chunks = start_chunks((forward, spectrum, inverse), (table, spec_in, back), sems)
    wait(copies)
    for block in range(lags // BLOCK):
        head[token_block(block), :] = windows[:, lane_block(block)]
    for chunk in range(STEPS):
        wait(chunks[chunk])
        spec = dot(table[chunk], windows[...])
        g_re, g_im = spec[:BINS], spec[BINS:]
        full = spec_in[chunk].astype(F32)
        x_re, x_im = full[:BINS], full[BINS:]
        re = g_re * x_re + g_im * x_im
        im = g_im * x_re - g_re * x_im
        re = sum(re[:, lane_block(b)] for b in range(BLOCKS))
        im = sum(im[:, lane_block(b)] for b in range(BLOCKS))
        part = dot(back[chunk], jnp.concatenate([re, im]).astype(BF16))
        whole_part = whole_part + part if chunk else part
    total[:lags, :] = whole_part * scale
    total[lags:, :] = jnp.zeros_like(total[lags:, :])
    count = lag_grad.shape[0]
    share = lags // count
    for slot in range(count):
        lag_grad[slot] = total[slot * share : slot * share + SLOT, :].astype(BF16)


def back_kernel(scale, place, forward, inverse, grad, halo, response, conv, *refs):
    outs, (table, back, filt, windows, sems, small_sems) = refs[:BLOCKS], refs[BLOCKS:]
    copies = []
    for block in range(BLOCKS):
        own = min(PERIOD, TOKENS - block * BLOCK)
        source = grad.at[block * BLOCK : block * BLOCK + own]
        target = windows.at[:own, lane_block(block)]
        copies.append(start(source, target, small_sems.at[block]))
        if own < PERIOD:
            target = windows.at[own:, lane_block(block)]
            sem = small_sems.at[BLOCKS + block]
            copies.append(start(halo.at[: PERIOD - own], target, sem))
    chunks = start_chunks((forward, response, inverse), (table, filt, back), sems)
    moved = [
        start(conv.at[rows_at(place[0] ^ hop)], out.at[:BLOCK], small_sems.at[2 * BLOCKS + hop])
        for hop, out in enumerate(outs)
    ]
    wait(copies)
    for chunk in range(STEPS):
        wait(chunks[chunk])
        spec = dot(table[chunk], windows[...])
        resp = filt[chunk].astype(F32)
        f_re, f_im = spread(resp[:BINS]), spread(resp[BINS:])
        g_re, g_im = spec[:BINS], spec[BINS:]
        y = jnp.concatenate([f_re * g_re + f_im * g_im, f_re * g_im - f_im * g_re])
        part = dot(back[chunk], y.astype(BF16))
        total = total + part if chunk else part
    windows[:BLOCK, :] = (total * scale).astype(BF16)
    for hop, out in enumerate(outs):
        out[BLOCK:, :] = windows[:BLOCK, lanes_at(place[0] ^ hop)]
    wait(moved)


def final_kernel(place, *refs):
    ships, refs = refs[:BLOCKS], refs[BLOCKS:]
    cotangent, key, value, parts, gate_grad, key_grad, value_grad, lag_grad = refs
    for hop, ship in enumerate(ships):
        at = (slice(None), lanes_at(place[0] ^ hop))
        conv, back = ship[:BLOCK, :].astype(F32), ship[BLOCK:, :].astype(F32)
        gate_grad[at] = (cotangent[at].astype(F32) * conv).astype(BF16)
        key_grad[at] = (back * value[at].astype(F32)).astype(BF16)
        value_grad[at] = (back * key[at].astype(F32)).astype(BF16)
    for block in range(BLOCKS):
        total = parts[block].astype(F32)
        for source in range(1, parts.shape[0] // BLOCKS):
            total += parts[source * BLOCKS + block].astype(F32)
        lag_grad[:, lane_block(block)] = total[: lag_grad.shape[0]]


def whole(shape):
    return pl.BlockSpec(shape, lambda *_: (0,) * len(shape))


def shaped(shape, dtype=BF16):
    return jax.ShapeDtypeStruct(shape, dtype)


def call(kernel, in_specs, out_specs, out_shape, scratch=(), flops=0, limit=None, scalars=0):
    return pl.pallas_call(
        kernel,
        grid_spec=pltpu.PrefetchScalarGridSpec(
            num_scalar_prefetch=scalars,
            grid=(1,),
            in_specs=in_specs,
            out_specs=out_specs,
            scratch_shapes=scratch,
        ),
        out_shape=out_shape,
        compiler_params=pltpu.CompilerParams(
            dimension_semantics=("arbitrary",), vmem_limit_bytes=limit or VMEM_LIMIT
        ),
        cost_estimate=pl.CostEstimate(flops=flops, bytes_accessed=0, transcendentals=0),
    )


VMEM_LIMIT = 56 * MIB
FINAL_LIMIT = 16 * MIB
CONV_FLOPS = 24_000_000_000
CROSS_FLOPS = 0
JOIN_FLOPS = 0
BACK_FLOPS = 35_000_000_000


def shift(value, steps):
    count = lax.axis_size(RUNS)
    first, last = max(0, -steps), min(count, count - steps)
    return lax.ppermute(value, RUNS, [(i, i + steps) for i in range(first, last)])


def swap(ships):
    return [ships[0]] + [
        lax.ppermute(ships[hop], GROUP, [(i, i ^ hop) for i in range(BLOCKS)])
        for hop in range(1, BLOCKS)
    ]


def exchange(value, axes):
    return lax.all_to_all(value, axes, split_axis=0, concat_axis=0, tiled=True)


def body(forward, own, first, lagged, last, gate_input, key_input, value_input, out_grad, filter_taps):
    lags = filter_taps.shape[0]
    held, channels = out_grad.shape
    share = lags // lax.axis_size(CTX)
    norm = 2.0 / PERIOD / lags**0.5
    local = (BLOCK, WIDE)
    ship = (2 * BLOCK, LANES)
    pieces = (channels // WIDE, held, WIDE)
    flat = (TOKENS, LANES)
    reach = (lags, LANES)
    slots = (lags // share, SLOT, LANES)
    scalar = pl.BlockSpec(memory_space=pltpu.SMEM)
    anywhere = pl.BlockSpec(memory_space=pl.ANY)
    place = lax.axis_index(GROUP).reshape(1)

    part = (BLOCK, LANES)
    by_block = (BLOCKS, BLOCK, LANES)
    *ships, cotangent = call(
        prep_kernel,
        [scalar] + [whole(local)] * 2 + [whole(out_grad.shape)],
        [whole(part)] * BLOCKS + [whole(pieces)],
        [shaped(part)] * BLOCKS + [shaped(pieces)],
    )(place, key_input, value_input, out_grad)
    cotangent = exchange(cotangent, CH).reshape(local)
    mixed, tail = call(
        join_kernel,
        [scalar] + [whole(part)] * BLOCKS,
        [whole(flat), whole(reach)],
        [shaped(flat), shaped(reach)],
        flops=JOIN_FLOPS,
    )(place, *swap(ships))
    mixed_halo = shift(tail, 1)
    grad = (cotangent.astype(F32) * gate_input.astype(F32)).astype(BF16)
    grad = exchange(grad.reshape(BLOCK, BLOCKS, LANES).transpose(1, 0, 2), GROUP).reshape(flat)

    table = pltpu.VMEM((STEPS, ROWS, PERIOD), BF16)
    narrow = pltpu.VMEM((STEPS, ROWS, BLOCK), BF16)
    by_bins = (STEPS, ROWS, WIDE)
    filt_bins = (STEPS, ROWS, LANES)
    windows = pltpu.VMEM((PERIOD, WIDE), BF16)
    dma = pltpu.SemaphoreType.DMA
    conv, spectrum, response = call(
        functools.partial(conv_kernel, norm),
        [anywhere] * 5,
        [whole(flat), anywhere, whole(filt_bins)],
        [shaped(flat), shaped(by_bins), shaped(filt_bins)],
        [
            table,
            narrow,
            windows,
            pltpu.VMEM(reach, BF16),
            pltpu.VMEM(by_bins, BF16),
            dma((2, STEPS)),
            dma((2 * BLOCKS,)),
            dma((STEPS,)),
        ],
        CONV_FLOPS,
        scalars=1,
    )(place, forward, last, mixed_halo, mixed, filter_taps)
    head, lag_grad = call(
        functools.partial(cross_kernel, norm),
        [anywhere] * 4,
        [whole(reach), whole(slots)],
        [shaped(reach), shaped(slots)],
        [
            narrow,
            pltpu.VMEM((STEPS, lags, ROWS), BF16),
            pltpu.VMEM(by_bins, BF16),
            pltpu.VMEM(local, BF16),
            pltpu.VMEM((lags + SLOT, LANES), F32),
            dma((3, STEPS)),
            dma((BLOCKS,)),
        ],
        CROSS_FLOPS,
    )(own, lagged, grad, spectrum)
    grad_halo = shift(head, -1)
    lag_parts = exchange(lag_grad, CTX)

    ships = call(
        functools.partial(back_kernel, norm),
        [scalar] + [anywhere] * 6,
        [whole(ship)] * BLOCKS,
        [shaped(ship)] * BLOCKS,
        [
            table,
            narrow,
            pltpu.VMEM(filt_bins, BF16),
            windows,
            dma((3, STEPS)),
            dma((3 * BLOCKS,)),
        ],
        BACK_FLOPS,
    )(place, forward, first, grad, grad_halo, response, conv)
    gate_grad, key_grad, value_grad, filter_grad = call(
        final_kernel,
        [scalar] + [whole(ship)] * BLOCKS + [whole(local)] * 3 + [whole(slots)],
        [whole(local)] * 3 + [whole((share, WIDE))],
        [shaped(local)] * 3 + [shaped((share, WIDE), F32)],
        limit=FINAL_LIMIT,
    )(place, *swap(ships), cotangent, key_input, value_input, lag_parts)
    return gate_grad, key_grad, value_grad, filter_grad


def solution(mesh):
    split = Mesh(mesh.devices.reshape(SIZES), AXES)
    spans = P(CTX, CH)
    mapped = jax.shard_map(
        body,
        mesh=split,
        in_specs=(P(), P(), P(), P(), P(), spans, spans, spans, P(CTX + CH, None), P(None, CH)),
        out_specs=(spans, spans, spans, spans),
        check_vma=False,
    )

    def run(gate_input, key_input, value_input, out_grad, filter_taps):
        lags = filter_taps.shape[0]
        tables = make_tables(lags)
        return mapped(*tables, gate_input, key_input, value_input, out_grad, filter_taps)

    return run
```

```python
import functools
import math

import jax
import jax.numpy as jnp
import ml_dtypes
import numpy as np
from jax import lax
from jax.experimental import pallas as pl
from jax.experimental.pallas import tpu as pltpu
from jax.sharding import Mesh, PartitionSpec as P

BF16 = jnp.bfloat16
F32 = jnp.float32
AXES = ("z", "yh", "yl", "c", "x", "zh")
SIZES = (8, 2, 2, 2, 4, 2)
CTX = ("z", "yh", "yl", "c")
GROUP = ("yl", "c")
RUNS = ("z", "yh")
CH = ("x", "zh")

BLOCK = 256
PERIOD = 1024
LANES = 128
BLOCKS = 4
TOKENS = BLOCKS * BLOCK
WIDE = BLOCKS * LANES
BINS = 512
STEPS = PERIOD // 2 // BINS
ROWS = 2 * BINS
SLOT = 16
MIB = 1024 * 1024


def make_tables(lags):
    freq = np.arange(PERIOD // 2)[:, None]
    place = np.arange(PERIOD)[None, :]
    angle = math.pi / PERIOD * ((2 * freq + 1) * place % (2 * PERIOD)).astype(np.float64)
    both = np.stack([np.cos(angle), -np.sin(angle)])
    both = both.reshape(2, STEPS, BINS, PERIOD).transpose(1, 0, 2, 3).reshape(STEPS, ROWS, PERIOD)
    back = both.transpose(0, 2, 1)
    tables = both, both[:, :, lags:], back[:, :BLOCK], back[:, :lags], back[:, lags:]
    return tuple(np.ascontiguousarray(t).astype(ml_dtypes.bfloat16) for t in tables)


def dot(a, b):
    return jnp.dot(a, b, preferred_element_type=F32)


def lane_block(index):
    return slice(index * LANES, (index + 1) * LANES)


def lanes_at(index):
    return pl.ds(pl.multiple_of(index * LANES, LANES), LANES)


def rows_at(index):
    return pl.ds(pl.multiple_of(index * BLOCK, BLOCK), BLOCK)


def token_block(index):
    return slice(index * BLOCK, (index + 1) * BLOCK)


def spread(part):
    return jnp.concatenate([part] * BLOCKS, axis=1)


def accumulate(step, total, part):
    @pl.when(step == 0)
    def _():
        total[...] = part

    @pl.when(step > 0)
    def _():
        total[...] += part


def prep_kernel(place, key, value, out_grad, *outs):
    ships, pieces = outs[:BLOCKS], outs[BLOCKS]
    for hop, ship in enumerate(ships):
        at = (slice(None), lanes_at(place[0] ^ hop))
        ship[...] = (key[at].astype(F32) * value[at].astype(F32)).astype(BF16)
    for piece in range(pieces.shape[0]):
        pieces[piece] = out_grad[:, piece * WIDE : (piece + 1) * WIDE]


def join_kernel(place, *refs):
    ships, (mixed, tail) = refs[:BLOCKS], refs[BLOCKS:]
    for hop, ship in enumerate(ships):
        mixed[rows_at(place[0] ^ hop), :] = ship[...]
    tail[...] = mixed[TOKENS - tail.shape[0] :, :]


def conv_kernel(
    scale, place, forward, inverse, halo, mixed, taps, conv, spectrum, response, windows, total
):
    step = pl.program_id(0)
    lags = taps.shape[0]

    @pl.when(step == 0)
    def _():
        for block in range(BLOCKS):
            early = lags - block * BLOCK
            if early:
                windows[:early, lane_block(block)] = halo[block * BLOCK :, :]
            windows[early:, lane_block(block)] = mixed[: (block + 1) * BLOCK, :]

    resp = dot(forward[:, :lags], taps[...])
    response[...] = resp.astype(BF16)
    spec = dot(forward[...], windows[...])
    spectrum[...] = spec.astype(BF16)
    f_re, f_im = spread(resp[:BINS]), spread(resp[BINS:])
    x_re, x_im = spec[:BINS], spec[BINS:]
    y = jnp.concatenate([f_re * x_re - f_im * x_im, f_re * x_im + f_im * x_re]).astype(BF16)
    accumulate(step, total, dot(inverse[...], y))

    @pl.when(step == STEPS - 1)
    def _():
        for block in range(BLOCKS):
            conv[token_block(block), :] = (total[:, lane_block(block)] * scale).astype(BF16)


def cross_kernel(scale, forward, inverse, grad, spectrum, head, lag_grad, windows, total):
    step = pl.program_id(0)

    @pl.when(step == 0)
    def _():
        head[...] = grad[: head.shape[0], :]
        for block in range(BLOCKS):
            windows[:, lane_block(block)] = grad[token_block(block), :]

    spec = dot(forward[...], windows[...])
    g_re, g_im = spec[:BINS], spec[BINS:]
    full = spectrum[...].astype(F32)
    x_re, x_im = full[:BINS], full[BINS:]
    re = g_re * x_re + g_im * x_im
    im = g_im * x_re - g_re * x_im
    re = sum(re[:, lane_block(b)] for b in range(BLOCKS))
    im = sum(im[:, lane_block(b)] for b in range(BLOCKS))
    lags = inverse.shape[0]
    part = dot(inverse[...], jnp.concatenate([re, im]).astype(BF16))

    @pl.when(step == 0)
    def _():
        total[:lags, :] = part
        total[lags:, :] = jnp.zeros_like(total[lags:, :])

    @pl.when(step > 0)
    def _():
        total[:lags, :] += part

    @pl.when(step == STEPS - 1)
    def _():
        count = lag_grad.shape[0]
        share = lags // count
        for slot in range(count):
            rows = total[slot * share : slot * share + SLOT, :] * scale
            lag_grad[slot] = rows.astype(BF16)


def back_kernel(scale, place, forward, inverse, grad, halo, response, conv, *refs):
    outs, (windows, total) = refs[:BLOCKS], refs[BLOCKS:]
    step = pl.program_id(0)

    @pl.when(step == 0)
    def _():
        for block in range(BLOCKS):
            own = min(PERIOD, TOKENS - block * BLOCK)
            windows[:own, lane_block(block)] = grad[block * BLOCK : block * BLOCK + own, :]
            if own < PERIOD:
                windows[own:, lane_block(block)] = halo[: PERIOD - own, :]
        for hop, out in enumerate(outs):
            out[:BLOCK, :] = conv[rows_at(place[0] ^ hop), :]

    spec = dot(forward[...], windows[...])
    resp = response[...].astype(F32)
    f_re, f_im = spread(resp[:BINS]), spread(resp[BINS:])
    g_re, g_im = spec[:BINS], spec[BINS:]
    y = jnp.concatenate([f_re * g_re + f_im * g_im, f_re * g_im - f_im * g_re]).astype(BF16)
    accumulate(step, total, dot(inverse[...], y))

    @pl.when(step == STEPS - 1)
    def _():
        for hop, out in enumerate(outs):
            out[BLOCK:, :] = (total[:, lanes_at(place[0] ^ hop)] * scale).astype(BF16)


def final_kernel(place, *refs):
    ships, refs = refs[:BLOCKS], refs[BLOCKS:]
    cotangent, key, value, parts, gate_grad, key_grad, value_grad, lag_grad = refs
    for hop, ship in enumerate(ships):
        at = (slice(None), lanes_at(place[0] ^ hop))
        conv, back = ship[:BLOCK, :].astype(F32), ship[BLOCK:, :].astype(F32)
        gate_grad[at] = (cotangent[at].astype(F32) * conv).astype(BF16)
        key_grad[at] = (back * value[at].astype(F32)).astype(BF16)
        value_grad[at] = (back * key[at].astype(F32)).astype(BF16)
    for block in range(BLOCKS):
        total = parts[block].astype(F32)
        for source in range(1, parts.shape[0] // BLOCKS):
            total += parts[source * BLOCKS + block].astype(F32)
        lag_grad[:, lane_block(block)] = total[: lag_grad.shape[0]]


def whole(shape):
    return pl.BlockSpec(shape, lambda *_: (0,) * len(shape))


def shaped(shape, dtype=BF16):
    return jax.ShapeDtypeStruct(shape, dtype)


def call(kernel, in_specs, out_specs, out_shape, scratch=(), steps=1, flops=0, limit=None, scalars=0):
    return pl.pallas_call(
        kernel,
        grid_spec=pltpu.PrefetchScalarGridSpec(
            num_scalar_prefetch=scalars,
            grid=(steps,),
            in_specs=in_specs,
            out_specs=out_specs,
            scratch_shapes=scratch,
        ),
        out_shape=out_shape,
        compiler_params=pltpu.CompilerParams(
            dimension_semantics=("arbitrary",), vmem_limit_bytes=limit or VMEM_LIMIT
        ),
        cost_estimate=pl.CostEstimate(flops=flops, bytes_accessed=0, transcendentals=0),
    )


VMEM_LIMIT = 52 * MIB
FINAL_LIMIT = 16 * MIB
PREP_LIMIT = 56 * MIB
CONV_FLOPS = 24_000_000_000
CROSS_FLOPS = 0
JOIN_FLOPS = 0
BACK_FLOPS = 35_000_000_000


def shift(value, steps):
    count = lax.axis_size(RUNS)
    first, last = max(0, -steps), min(count, count - steps)
    return lax.ppermute(value, RUNS, [(i, i + steps) for i in range(first, last)])


def swap(ships):
    return [ships[0]] + [
        lax.ppermute(ships[hop], GROUP, [(i, i ^ hop) for i in range(BLOCKS)])
        for hop in range(1, BLOCKS)
    ]


def exchange(value, axes):
    return lax.all_to_all(value, axes, split_axis=0, concat_axis=0, tiled=True)


def body(forward, own, first, lagged, last, gate_input, key_input, value_input, out_grad, filter_taps):
    lags = filter_taps.shape[0]
    held, channels = out_grad.shape
    share = lags // lax.axis_size(CTX)
    norm = 2.0 / PERIOD / lags**0.5
    local = (BLOCK, WIDE)
    ship = (2 * BLOCK, LANES)
    pieces = (channels // WIDE, held, WIDE)
    flat = (TOKENS, LANES)
    reach = (lags, LANES)
    slots = (lags // share, SLOT, LANES)
    scalar = pl.BlockSpec(memory_space=pltpu.SMEM)
    place = lax.axis_index(GROUP).reshape(1)

    part = (BLOCK, LANES)
    by_block = (BLOCKS, BLOCK, LANES)
    *ships, cotangent = call(
        prep_kernel,
        [scalar] + [whole(local)] * 2 + [whole(out_grad.shape)],
        [whole(part)] * BLOCKS + [whole(pieces)],
        [shaped(part)] * BLOCKS + [shaped(pieces)],
        limit=PREP_LIMIT,
    )(place, key_input, value_input, out_grad)
    cotangent = exchange(cotangent, CH).reshape(local)
    mixed, tail = call(
        join_kernel,
        [scalar] + [whole(part)] * BLOCKS,
        [whole(flat), whole(reach)],
        [shaped(flat), shaped(reach)],
        flops=JOIN_FLOPS,
    )(place, *swap(ships))
    mixed_halo = shift(tail, 1)
    grad = (cotangent.astype(F32) * gate_input.astype(F32)).astype(BF16)
    grad = exchange(grad.reshape(BLOCK, BLOCKS, LANES).transpose(1, 0, 2), GROUP).reshape(flat)

    def stepped(*shape):
        return pl.BlockSpec((None,) + shape, lambda step, *_: (step, 0, 0))

    table = stepped(ROWS, PERIOD)
    bins = pl.BlockSpec((ROWS, WIDE), lambda step, *_: (step, 0))
    narrow_bins = pl.BlockSpec((ROWS, LANES), lambda step, *_: (step, 0))
    conv, spectrum, response = call(
        functools.partial(conv_kernel, norm),
        [
            table,
            stepped(BLOCK, ROWS),
            whole(reach),
            whole(flat),
            pl.BlockSpec(reach, lambda step, place: (0, place[0])),
        ],
        [whole(flat), bins, narrow_bins],
        [shaped(flat), shaped((PERIOD, WIDE)), shaped((PERIOD, LANES))],
        [pltpu.VMEM((PERIOD, WIDE), BF16), pltpu.VMEM(local, F32)],
        STEPS,
        CONV_FLOPS,
        scalars=1,
    )(place, forward, last, mixed_halo, mixed, filter_taps)

    head, lag_grad = call(
        functools.partial(cross_kernel, norm),
        [stepped(ROWS, BLOCK), stepped(lags, ROWS), whole(flat), bins],
        [whole(reach), whole(slots)],
        [shaped(reach), shaped(slots)],
        [pltpu.VMEM(local, BF16), pltpu.VMEM((lags + SLOT, LANES), F32)],
        STEPS,
        CROSS_FLOPS,
    )(own, lagged, grad, spectrum)
    grad_halo = shift(head, -1)
    lag_parts = exchange(lag_grad, CTX)

    ships = call(
        functools.partial(back_kernel, norm),
        [
            scalar,
            table,
            stepped(BLOCK, ROWS),
            whole(flat),
            whole(reach),
            narrow_bins,
            whole(flat),
        ],
        [whole(ship)] * BLOCKS,
        [shaped(ship)] * BLOCKS,
        [pltpu.VMEM((PERIOD, WIDE), BF16), pltpu.VMEM(local, F32)],
        STEPS,
        BACK_FLOPS,
    )(place, forward, first, grad, grad_halo, response, conv)
    gate_grad, key_grad, value_grad, filter_grad = call(
        final_kernel,
        [scalar] + [whole(ship)] * BLOCKS + [whole(local)] * 3 + [whole(slots)],
        [whole(local)] * 3 + [whole((share, WIDE))],
        [shaped(local)] * 3 + [shaped((share, WIDE), F32)],
        limit=FINAL_LIMIT,
    )(place, *swap(ships), cotangent, key_input, value_input, lag_parts)
    return gate_grad, key_grad, value_grad, filter_grad


def solution(mesh):
    split = Mesh(mesh.devices.reshape(SIZES), AXES)
    spans = P(CTX, CH)
    mapped = jax.shard_map(
        body,
        mesh=split,
        in_specs=(P(), P(), P(), P(), P(), spans, spans, spans, P(CTX + CH, None), P(None, CH)),
        out_specs=(spans, spans, spans, spans),
        check_vma=False,
    )

    def run(gate_input, key_input, value_input, out_grad, filter_taps):
        lags = filter_taps.shape[0]
        tables = make_tables(lags)
        return mapped(*tables, gate_input, key_input, value_input, out_grad, filter_taps)

    return run
```

```python
import functools
import math

import jax
import jax.numpy as jnp
import ml_dtypes
import numpy as np
from jax import lax
from jax.experimental import pallas as pl
from jax.experimental.pallas import tpu as pltpu
from jax.sharding import Mesh, PartitionSpec as P

BF16 = jnp.bfloat16
F32 = jnp.float32
AXES = ("z", "yh", "yl", "c", "x", "zh")
SIZES = (8, 2, 2, 2, 4, 2)
CTX = ("z", "yh", "yl", "c")
GROUP = ("yl", "c")
RUNS = ("z", "yh")
CH = ("x", "zh")

BLOCK = 256
PERIOD = 1024
LANES = 128
BLOCKS = 4
TOKENS = BLOCKS * BLOCK
WIDE = BLOCKS * LANES
BINS = 128
STEPS = 4
ROWS = 2 * BINS
SLOT = 16
MIB = 1024 * 1024


def make_tables():
    freq = np.arange(PERIOD // 2)[:, None]
    place = np.arange(BLOCK)[None, :]
    angle = math.pi / PERIOD * ((2 * freq + 1) * place % (2 * PERIOD)).astype(np.float64)
    both = np.stack([np.cos(angle), -np.sin(angle)]).reshape(2, BINS, STEPS, BLOCK)
    both = both.transpose(2, 0, 1, 3).reshape(STEPS, ROWS, BLOCK)
    tables = both, both.transpose(0, 2, 1)
    return tuple(np.ascontiguousarray(t).astype(ml_dtypes.bfloat16) for t in tables)


def turn(spec, chunk, block):
    re, im = spec
    eighths = (2 * chunk + 1) * block % 8
    half = math.sqrt(0.5)
    if eighths == 0:
        return re, im
    if eighths == 1:
        return (re + im) * half, (im - re) * half
    if eighths == 2:
        return im, -re
    if eighths == 3:
        return (im - re) * half, (re + im) * -half
    if eighths == 4:
        return -re, -im
    if eighths == 5:
        return (re + im) * -half, (re - im) * half
    if eighths == 6:
        return -im, re
    return (re - im) * half, (re + im) * half


def add(specs):
    return sum(re for re, _ in specs), sum(im for _, im in specs)


def times(a, b):
    return a[0] * b[0] - a[1] * b[1], a[0] * b[1] + a[1] * b[0]


def times_conj(a, b):
    return a[0] * b[0] + a[1] * b[1], a[1] * b[0] - a[0] * b[1]


def transform(table, blocks, chunk, first=0):
    flat = dot(table, blocks)
    count = blocks.shape[1] // LANES
    parts = [flat[:, lane_block(i)] for i in range(count)]
    return [turn((p[:BINS], p[BINS:]), chunk, first + i) for i, p in enumerate(parts)]


def stacked(specs):
    return jnp.concatenate([jnp.concatenate(spec, axis=0) for spec in specs], axis=1).astype(BF16)


def fill(blocks, *sources):
    at = 0
    for source in sources:
        for block in range(source.shape[0] // BLOCK):
            blocks[:, lane_block(at)] = source[token_block(block), :]
            at += 1


def dot(a, b):
    return jnp.dot(a, b, preferred_element_type=F32)


def lane_block(index):
    return slice(index * LANES, (index + 1) * LANES)


def lanes_at(index):
    return pl.ds(pl.multiple_of(index * LANES, LANES), LANES)


def rows_at(index):
    return pl.ds(pl.multiple_of(index * BLOCK, BLOCK), BLOCK)


def token_block(index):
    return slice(index * BLOCK, (index + 1) * BLOCK)


def prep_kernel(place, key, value, out_grad, *outs):
    ships, pieces = outs[:BLOCKS], outs[BLOCKS]
    for hop, ship in enumerate(ships):
        at = (slice(None), lanes_at(place[0] ^ hop))
        ship[...] = (key[at].astype(F32) * value[at].astype(F32)).astype(BF16)
    for piece in range(pieces.shape[0]):
        pieces[piece] = out_grad[:, piece * WIDE : (piece + 1) * WIDE]


def join_kernel(place, *refs):
    ships, (mixed, tail) = refs[:BLOCKS], refs[BLOCKS:]
    for hop, ship in enumerate(ships):
        mixed[rows_at(place[0] ^ hop), :] = ship[...]
    tail[...] = mixed[TOKENS - tail.shape[0] :, :]


def conv_kernel(scale, place, table, back, halo, mixed, taps, conv, spectrum, response, blocks, filt):
    reach = taps.shape[0] // BLOCK
    fill(blocks, halo, mixed)
    fill(filt, taps)
    for chunk in range(STEPS):
        resp = add(transform(table[chunk], filt[...], chunk))
        response[chunk] = stacked([resp])
        specs = transform(table[chunk], blocks[...], chunk)
        specs = [add(specs[b : b + reach + 1]) for b in range(BLOCKS)]
        spectrum[chunk] = stacked(specs)
        y = [turn(times(resp, spec), chunk, -(b + reach)) for b, spec in enumerate(specs)]
        part = dot(back[chunk], stacked(y))
        total = total + part if chunk else part
    for block in range(BLOCKS):
        conv[token_block(block), :] = (total[:, lane_block(block)] * scale).astype(BF16)


def cross_kernel(scale, table, back, grad, spectrum, head, lag_grad, blocks, total):
    lags = head.shape[0]
    reach = lags // BLOCK
    head[...] = grad[:lags, :]
    fill(blocks, grad)
    for chunk in range(STEPS):
        specs = transform(table[chunk], blocks[...], chunk, reach)
        terms = []
        for block, spec in enumerate(specs):
            held = spectrum[chunk, :, lane_block(block)].astype(F32)
            terms.append(times_conj(spec, (held[:BINS], held[BINS:])))
        term = add(terms)
        part = dot(back[chunk], stacked([turn(term, chunk, -j) for j in range(reach)]))
        summed = summed + part if chunk else part
    for j in range(reach):
        total[token_block(j), :] = summed[:, lane_block(j)] * scale
    total[lags:, :] = jnp.zeros_like(total[lags:, :])
    count = lag_grad.shape[0]
    share = lags // count
    for slot in range(count):
        lag_grad[slot] = total[slot * share : slot * share + SLOT, :].astype(BF16)


def back_kernel(scale, place, table, back, grad, halo, response, conv, *refs):
    outs, (blocks,) = refs[:BLOCKS], refs[BLOCKS:]
    reach = halo.shape[0] // BLOCK
    fill(blocks, grad, halo)
    for chunk in range(STEPS):
        held = response[chunk].astype(F32)
        resp = held[:BINS], held[BINS:]
        specs = transform(table[chunk], blocks[...], chunk)
        specs = [add(specs[b : b + reach + 1]) for b in range(BLOCKS)]
        y = [turn(times_conj(spec, resp), chunk, -b) for b, spec in enumerate(specs)]
        part = dot(back[chunk], stacked(y))
        total = total + part if chunk else part
    blocks[:, :WIDE] = (total * scale).astype(BF16)
    for hop, out in enumerate(outs):
        out[:BLOCK, :] = conv[rows_at(place[0] ^ hop), :]
        out[BLOCK:, :] = blocks[:, lanes_at(place[0] ^ hop)]


def final_kernel(place, *refs):
    ships, refs = refs[:BLOCKS], refs[BLOCKS:]
    cotangent, key, value, parts, gate_grad, key_grad, value_grad, lag_grad = refs
    for hop, ship in enumerate(ships):
        at = (slice(None), lanes_at(place[0] ^ hop))
        conv, back = ship[:BLOCK, :].astype(F32), ship[BLOCK:, :].astype(F32)
        gate_grad[at] = (cotangent[at].astype(F32) * conv).astype(BF16)
        key_grad[at] = (back * value[at].astype(F32)).astype(BF16)
        value_grad[at] = (back * key[at].astype(F32)).astype(BF16)
    for block in range(BLOCKS):
        total = parts[block].astype(F32)
        for source in range(1, parts.shape[0] // BLOCKS):
            total += parts[source * BLOCKS + block].astype(F32)
        lag_grad[:, lane_block(block)] = total[: lag_grad.shape[0]]


def whole(shape):
    return pl.BlockSpec(shape, lambda *_: (0,) * len(shape))


def shaped(shape, dtype=BF16):
    return jax.ShapeDtypeStruct(shape, dtype)


def call(kernel, in_specs, out_specs, out_shape, scratch=(), flops=0, limit=None, scalars=0):
    return pl.pallas_call(
        kernel,
        grid_spec=pltpu.PrefetchScalarGridSpec(
            num_scalar_prefetch=scalars,
            grid=(1,),
            in_specs=in_specs,
            out_specs=out_specs,
            scratch_shapes=scratch,
        ),
        out_shape=out_shape,
        compiler_params=pltpu.CompilerParams(
            dimension_semantics=("arbitrary",), vmem_limit_bytes=limit or VMEM_LIMIT
        ),
        cost_estimate=pl.CostEstimate(flops=flops, bytes_accessed=0, transcendentals=0),
    )


VMEM_LIMIT = 52 * MIB
FINAL_LIMIT = 16 * MIB
PREP_LIMIT = 56 * MIB
CONV_FLOPS = 24_000_000_000
CROSS_FLOPS = 0
JOIN_FLOPS = 0
BACK_FLOPS = 35_000_000_000


def shift(value, steps):
    count = lax.axis_size(RUNS)
    first, last = max(0, -steps), min(count, count - steps)
    return lax.ppermute(value, RUNS, [(i, i + steps) for i in range(first, last)])


def swap(ships):
    return [ships[0]] + [
        lax.ppermute(ships[hop], GROUP, [(i, i ^ hop) for i in range(BLOCKS)])
        for hop in range(1, BLOCKS)
    ]


def exchange(value, axes):
    return lax.all_to_all(value, axes, split_axis=0, concat_axis=0, tiled=True)


def body(forward, inverse, gate_input, key_input, value_input, out_grad, filter_taps):
    lags = filter_taps.shape[0]
    held, channels = out_grad.shape
    share = lags // lax.axis_size(CTX)
    norm = 2.0 / PERIOD / lags**0.5
    local = (BLOCK, WIDE)
    ship = (2 * BLOCK, LANES)
    pieces = (channels // WIDE, held, WIDE)
    flat = (TOKENS, LANES)
    reach = (lags, LANES)
    slots = (lags // share, SLOT, LANES)
    scalar = pl.BlockSpec(memory_space=pltpu.SMEM)
    place = lax.axis_index(GROUP).reshape(1)

    part = (BLOCK, LANES)
    by_block = (BLOCKS, BLOCK, LANES)
    *ships, cotangent = call(
        prep_kernel,
        [scalar] + [whole(local)] * 2 + [whole(out_grad.shape)],
        [whole(part)] * BLOCKS + [whole(pieces)],
        [shaped(part)] * BLOCKS + [shaped(pieces)],
        limit=PREP_LIMIT,
    )(place, key_input, value_input, out_grad)
    cotangent = exchange(cotangent, CH).reshape(local)
    mixed, tail = call(
        join_kernel,
        [scalar] + [whole(part)] * BLOCKS,
        [whole(flat), whole(reach)],
        [shaped(flat), shaped(reach)],
        flops=JOIN_FLOPS,
    )(place, *swap(ships))
    mixed_halo = shift(tail, 1)
    grad = (cotangent.astype(F32) * gate_input.astype(F32)).astype(BF16)
    grad = exchange(grad.reshape(BLOCK, BLOCKS, LANES).transpose(1, 0, 2), GROUP).reshape(flat)

    table = whole(forward.shape)
    by_bins = (STEPS, ROWS, WIDE)
    filt_bins = (STEPS, ROWS, LANES)
    seven = pltpu.VMEM((BLOCK, WIDE + lags // BLOCK * LANES), BF16)
    conv, spectrum, response = call(
        functools.partial(conv_kernel, norm),
        [
            table,
            table,
            whole(reach),
            whole(flat),
            pl.BlockSpec(reach, lambda step, place: (0, place[0])),
        ],
        [whole(flat), whole(by_bins), whole(filt_bins)],
        [shaped(flat), shaped(by_bins), shaped(filt_bins)],
        [seven, pltpu.VMEM((BLOCK, lags // BLOCK * LANES), BF16)],
        CONV_FLOPS,
        scalars=1,
    )(place, forward, inverse, mixed_halo, mixed, filter_taps)
    head, lag_grad = call(
        functools.partial(cross_kernel, norm),
        [table, table, whole(flat), whole(by_bins)],
        [whole(reach), whole(slots)],
        [shaped(reach), shaped(slots)],
        [pltpu.VMEM(local, BF16), pltpu.VMEM((lags + SLOT, LANES), F32)],
        CROSS_FLOPS,
    )(forward, inverse, grad, spectrum)
    grad_halo = shift(head, -1)
    lag_parts = exchange(lag_grad, CTX)

    ships = call(
        functools.partial(back_kernel, norm),
        [
            scalar,
            table,
            table,
            whole(flat),
            whole(reach),
            whole(filt_bins),
            whole(flat),
        ],
        [whole(ship)] * BLOCKS,
        [shaped(ship)] * BLOCKS,
        [seven],
        BACK_FLOPS,
    )(place, forward, inverse, grad, grad_halo, response, conv)
    gate_grad, key_grad, value_grad, filter_grad = call(
        final_kernel,
        [scalar] + [whole(ship)] * BLOCKS + [whole(local)] * 3 + [whole(slots)],
        [whole(local)] * 3 + [whole((share, WIDE))],
        [shaped(local)] * 3 + [shaped((share, WIDE), F32)],
        limit=FINAL_LIMIT,
    )(place, *swap(ships), cotangent, key_input, value_input, lag_parts)
    return gate_grad, key_grad, value_grad, filter_grad


def solution(mesh):
    split = Mesh(mesh.devices.reshape(SIZES), AXES)
    spans = P(CTX, CH)
    mapped = jax.shard_map(
        body,
        mesh=split,
        in_specs=(P(), P(), spans, spans, spans, P(CTX + CH, None), P(None, CH)),
        out_specs=(spans, spans, spans, spans),
        check_vma=False,
    )

    def run(gate_input, key_input, value_input, out_grad, filter_taps):
        return mapped(*make_tables(), gate_input, key_input, value_input, out_grad, filter_taps)

    return run
```

```python
import functools
import math

import jax
import jax.numpy as jnp
import ml_dtypes
import numpy as np
from jax import lax
from jax.experimental import pallas as pl
from jax.experimental.pallas import tpu as pltpu
from jax.sharding import Mesh, PartitionSpec as P

BF16 = jnp.bfloat16
F32 = jnp.float32
AXES = ("z", "yh", "yl", "c", "x", "zh")
SIZES = (8, 2, 2, 2, 4, 2)
CTX = ("z", "yh", "yl", "c")
GROUP = ("yl", "c")
RUNS = ("z", "yh")
CH = ("x", "zh")

BLOCK = 256
PERIOD = 1024
LANES = 128
BLOCKS = 4
TOKENS = BLOCKS * BLOCK
WIDE = BLOCKS * LANES
BINS = 128
STEPS = 4
ROWS = 2 * BINS
SLOT = 16
MIB = 1024 * 1024


def make_tables():
    freq = np.arange(PERIOD // 2)[:, None]
    place = np.arange(BLOCK)[None, :]
    angle = math.pi / PERIOD * ((2 * freq + 1) * place % (2 * PERIOD)).astype(np.float64)
    both = np.stack([np.cos(angle), -np.sin(angle)]).reshape(2, BINS, STEPS, BLOCK)
    both = both.transpose(2, 0, 1, 3).reshape(STEPS, ROWS, BLOCK)
    tables = both, both.transpose(0, 2, 1)
    return tuple(np.ascontiguousarray(t).astype(ml_dtypes.bfloat16) for t in tables)


def turn(spec, chunk, block):
    re, im = spec
    eighths = (2 * chunk + 1) * block % 8
    half = math.sqrt(0.5)
    if eighths == 0:
        return re, im
    if eighths == 1:
        return (re + im) * half, (im - re) * half
    if eighths == 2:
        return im, -re
    if eighths == 3:
        return (im - re) * half, (re + im) * -half
    if eighths == 4:
        return -re, -im
    if eighths == 5:
        return (re + im) * -half, (re - im) * half
    if eighths == 6:
        return -im, re
    return (re - im) * half, (re + im) * half


def add(specs):
    return sum(re for re, _ in specs), sum(im for _, im in specs)


def times(a, b):
    return a[0] * b[0] - a[1] * b[1], a[0] * b[1] + a[1] * b[0]


def times_conj(a, b):
    return a[0] * b[0] + a[1] * b[1], a[1] * b[0] - a[0] * b[1]


def transform(table, blocks, chunk, first=0):
    flat = dot(table, blocks)
    count = blocks.shape[1] // LANES
    parts = [flat[:, lane_block(i)] for i in range(count)]
    return [turn((p[:BINS], p[BINS:]), chunk, first + i) for i, p in enumerate(parts)]


def stacked(specs):
    return jnp.concatenate([jnp.concatenate(spec, axis=0) for spec in specs], axis=1).astype(BF16)


def fill(blocks, *sources):
    at = 0
    for source in sources:
        for block in range(source.shape[0] // BLOCK):
            blocks[:, lane_block(at)] = source[token_block(block), :]
            at += 1


def dot(a, b):
    return jnp.dot(a, b, preferred_element_type=F32)


def lane_block(index):
    return slice(index * LANES, (index + 1) * LANES)


def lanes_at(index):
    return pl.ds(pl.multiple_of(index * LANES, LANES), LANES)


def rows_at(index):
    return pl.ds(pl.multiple_of(index * BLOCK, BLOCK), BLOCK)


def token_block(index):
    return slice(index * BLOCK, (index + 1) * BLOCK)


def at_hops(kept, near, far):
    return [kept, near.at[0], far.at[0], far.at[1]]


def out_hops(kept, near, far):
    return [kept, near.at[0], far, near.at[1]]


def prep_kernel(place, key, value, out_grad, kept, near, far, pieces):
    for hop, ship in enumerate(out_hops(kept, near, far)):
        at = (slice(None), lanes_at(place[0] ^ hop))
        ship[...] = (key[at].astype(F32) * value[at].astype(F32)).astype(BF16)
    for piece in range(pieces.shape[0]):
        pieces[piece] = out_grad[:, piece * WIDE : (piece + 1) * WIDE]


def pick_kernel(far, near, out):
    out[0] = far[...]
    out[1] = near[1]


def join_kernel(place, kept, near, far, mixed, tail):
    for hop, ship in enumerate(at_hops(kept, near, far)):
        mixed[rows_at(place[0] ^ hop), :] = ship[...]
    tail[...] = mixed[TOKENS - tail.shape[0] :, :]


def conv_kernel(scale, place, table, back, halo, mixed, taps, conv, spectrum, response, blocks, filt):
    reach = taps.shape[0] // BLOCK
    fill(blocks, halo, mixed)
    fill(filt, taps)
    for chunk in range(STEPS):
        resp = add(transform(table[chunk], filt[...], chunk))
        response[chunk] = stacked([resp])
        specs = transform(table[chunk], blocks[...], chunk)
        specs = [add(specs[b : b + reach + 1]) for b in range(BLOCKS)]
        spectrum[chunk] = stacked(specs)
        y = [turn(times(resp, spec), chunk, -(b + reach)) for b, spec in enumerate(specs)]
        part = dot(back[chunk], stacked(y))
        total = total + part if chunk else part
    for block in range(BLOCKS):
        conv[token_block(block), :] = (total[:, lane_block(block)] * scale).astype(BF16)


def cross_kernel(scale, table, back, grad, spectrum, head, lag_grad, blocks, total):
    lags = head.shape[0]
    reach = lags // BLOCK
    head[...] = grad[:lags, :]
    fill(blocks, grad)
    for chunk in range(STEPS):
        specs = transform(table[chunk], blocks[...], chunk, reach)
        terms = []
        for block, spec in enumerate(specs):
            held = spectrum[chunk, :, lane_block(block)].astype(F32)
            terms.append(times_conj(spec, (held[:BINS], held[BINS:])))
        term = add(terms)
        part = dot(back[chunk], stacked([turn(term, chunk, -j) for j in range(reach)]))
        summed = summed + part if chunk else part
    for j in range(reach):
        total[token_block(j), :] = summed[:, lane_block(j)] * scale
    total[lags:, :] = jnp.zeros_like(total[lags:, :])
    count = lag_grad.shape[0]
    share = lags // count
    for slot in range(count):
        lag_grad[slot] = total[slot * share : slot * share + SLOT, :].astype(BF16)


def back_kernel(
    scale, place, table, back, grad, halo, response, conv, kept, near, far, blocks
):
    reach = halo.shape[0] // BLOCK
    fill(blocks, grad, halo)
    for chunk in range(STEPS):
        held = response[chunk].astype(F32)
        resp = held[:BINS], held[BINS:]
        specs = transform(table[chunk], blocks[...], chunk)
        specs = [add(specs[b : b + reach + 1]) for b in range(BLOCKS)]
        y = [turn(times_conj(spec, resp), chunk, -b) for b, spec in enumerate(specs)]
        part = dot(back[chunk], stacked(y))
        total = total + part if chunk else part
    blocks[:, :WIDE] = (total * scale).astype(BF16)
    for hop, out in enumerate(out_hops(kept, near, far)):
        out[:BLOCK, :] = conv[rows_at(place[0] ^ hop), :]
        out[BLOCK:, :] = blocks[:, lanes_at(place[0] ^ hop)]


def final_kernel(
    place,
    kept,
    near,
    far,
    cotangent,
    key,
    value,
    parts,
    gate_grad,
    key_grad,
    value_grad,
    lag_grad,
):
    for hop, ship in enumerate(at_hops(kept, near, far)):
        at = (slice(None), lanes_at(place[0] ^ hop))
        conv, back = ship[:BLOCK, :].astype(F32), ship[BLOCK:, :].astype(F32)
        gate_grad[at] = (cotangent[at].astype(F32) * conv).astype(BF16)
        key_grad[at] = (back * value[at].astype(F32)).astype(BF16)
        value_grad[at] = (back * key[at].astype(F32)).astype(BF16)
    for block in range(BLOCKS):
        total = parts[block].astype(F32)
        for source in range(1, parts.shape[0] // BLOCKS):
            total += parts[source * BLOCKS + block].astype(F32)
        lag_grad[:, lane_block(block)] = total[: lag_grad.shape[0]]


def whole(shape):
    return pl.BlockSpec(shape, lambda *_: (0,) * len(shape))


def shaped(shape, dtype=BF16):
    return jax.ShapeDtypeStruct(shape, dtype)


def call(kernel, in_specs, out_specs, out_shape, scratch=(), flops=0, limit=None, scalars=0):
    return pl.pallas_call(
        kernel,
        grid_spec=pltpu.PrefetchScalarGridSpec(
            num_scalar_prefetch=scalars,
            grid=(1,),
            in_specs=in_specs,
            out_specs=out_specs,
            scratch_shapes=scratch,
        ),
        out_shape=out_shape,
        compiler_params=pltpu.CompilerParams(
            dimension_semantics=("arbitrary",), vmem_limit_bytes=limit or VMEM_LIMIT
        ),
        cost_estimate=pl.CostEstimate(flops=flops, bytes_accessed=0, transcendentals=0),
    )


VMEM_LIMIT = 52 * MIB
FINAL_LIMIT = 16 * MIB
PREP_LIMIT = 56 * MIB
CONV_FLOPS = 24_000_000_000
CROSS_FLOPS = 0
JOIN_FLOPS = 0
BACK_FLOPS = 35_000_000_000


def shift(value, steps):
    count = lax.axis_size(RUNS)
    first, last = max(0, -steps), min(count, count - steps)
    return lax.ppermute(value, RUNS, [(i, i + steps) for i in range(first, last)])


def swap(kept, near, far):
    def flip(value, axis):
        return lax.ppermute(value, axis, [(0, 1), (1, 0)])

    near = flip(near, "c")
    far = call(
        pick_kernel,
        [whole(far.shape), whole(near.shape)],
        whole(near.shape),
        shaped(near.shape),
    )(far, near)
    return kept, near, flip(far, "yl")


def exchange(value, axes):
    return lax.all_to_all(value, axes, split_axis=0, concat_axis=0, tiled=True)


def body(forward, inverse, gate_input, key_input, value_input, out_grad, filter_taps):
    lags = filter_taps.shape[0]
    held, channels = out_grad.shape
    share = lags // lax.axis_size(CTX)
    norm = 2.0 / PERIOD / lags**0.5
    local = (BLOCK, WIDE)
    ship = (2 * BLOCK, LANES)
    pieces = (channels // WIDE, held, WIDE)
    ships_pair = (2,) + ship
    flat = (TOKENS, LANES)
    reach = (lags, LANES)
    slots = (lags // share, SLOT, LANES)
    scalar = pl.BlockSpec(memory_space=pltpu.SMEM)
    place = lax.axis_index(GROUP).reshape(1)

    part = (BLOCK, LANES)
    by_block = (BLOCKS, BLOCK, LANES)
    pair = (2,) + part
    *ships, cotangent = call(
        prep_kernel,
        [scalar] + [whole(local)] * 2 + [whole(out_grad.shape)],
        [whole(part), whole(pair), whole(part), whole(pieces)],
        [shaped(part), shaped(pair), shaped(part), shaped(pieces)],
        limit=PREP_LIMIT,
    )(place, key_input, value_input, out_grad)
    cotangent = exchange(cotangent, CH).reshape(local)
    mixed, tail = call(
        join_kernel,
        [scalar, whole(part), whole(pair), whole(pair)],
        [whole(flat), whole(reach)],
        [shaped(flat), shaped(reach)],
        flops=JOIN_FLOPS,
    )(place, *swap(*ships))
    mixed_halo = shift(tail, 1)
    grad = (cotangent.astype(F32) * gate_input.astype(F32)).astype(BF16)
    grad = exchange(grad.reshape(BLOCK, BLOCKS, LANES).transpose(1, 0, 2), GROUP).reshape(flat)

    table = whole(forward.shape)
    by_bins = (STEPS, ROWS, WIDE)
    filt_bins = (STEPS, ROWS, LANES)
    seven = pltpu.VMEM((BLOCK, WIDE + lags // BLOCK * LANES), BF16)
    conv, spectrum, response = call(
        functools.partial(conv_kernel, norm),
        [
            table,
            table,
            whole(reach),
            whole(flat),
            pl.BlockSpec(reach, lambda step, place: (0, place[0])),
        ],
        [whole(flat), whole(by_bins), whole(filt_bins)],
        [shaped(flat), shaped(by_bins), shaped(filt_bins)],
        [seven, pltpu.VMEM((BLOCK, lags // BLOCK * LANES), BF16)],
        CONV_FLOPS,
        scalars=1,
    )(place, forward, inverse, mixed_halo, mixed, filter_taps)
    head, lag_grad = call(
        functools.partial(cross_kernel, norm),
        [table, table, whole(flat), whole(by_bins)],
        [whole(reach), whole(slots)],
        [shaped(reach), shaped(slots)],
        [pltpu.VMEM(local, BF16), pltpu.VMEM((lags + SLOT, LANES), F32)],
        CROSS_FLOPS,
    )(forward, inverse, grad, spectrum)
    grad_halo = shift(head, -1)
    lag_parts = exchange(lag_grad, CTX)

    ships = call(
        functools.partial(back_kernel, norm),
        [
            scalar,
            table,
            table,
            whole(flat),
            whole(reach),
            whole(filt_bins),
            whole(flat),
        ],
        [whole(ship), whole(ships_pair), whole(ship)],
        [shaped(ship), shaped(ships_pair), shaped(ship)],
        [seven],
        BACK_FLOPS,
    )(place, forward, inverse, grad, grad_halo, response, conv)
    gate_grad, key_grad, value_grad, filter_grad = call(
        final_kernel,
        [scalar, whole(ship), whole(ships_pair), whole(ships_pair)]
        + [whole(local)] * 3
        + [whole(slots)],
        [whole(local)] * 3 + [whole((share, WIDE))],
        [shaped(local)] * 3 + [shaped((share, WIDE), F32)],
        limit=FINAL_LIMIT,
    )(place, *swap(*ships), cotangent, key_input, value_input, lag_parts)
    return gate_grad, key_grad, value_grad, filter_grad


def solution(mesh):
    split = Mesh(mesh.devices.reshape(SIZES), AXES)
    spans = P(CTX, CH)
    mapped = jax.shard_map(
        body,
        mesh=split,
        in_specs=(P(), P(), spans, spans, spans, P(CTX + CH, None), P(None, CH)),
        out_specs=(spans, spans, spans, spans),
        check_vma=False,
    )

    def run(gate_input, key_input, value_input, out_grad, filter_taps):
        return mapped(*make_tables(), gate_input, key_input, value_input, out_grad, filter_taps)

    return run
```

```python
import functools
import math

import jax
import jax.numpy as jnp
import ml_dtypes
import numpy as np
from jax import lax
from jax.experimental import pallas as pl
from jax.experimental.pallas import tpu as pltpu
from jax.sharding import Mesh, PartitionSpec as P

BF16 = jnp.bfloat16
F32 = jnp.float32
AXES = ("z", "yh", "yl", "c", "x", "zh")
SIZES = (8, 2, 2, 2, 4, 2)
CTX = ("z", "yh", "yl", "c")
GROUP = ("yl", "c")
RUNS = ("z", "yh")
CH = ("x", "zh")

BLOCK = 256
PERIOD = 1024
LANES = 128
BLOCKS = 4
TOKENS = BLOCKS * BLOCK
WIDE = BLOCKS * LANES
BINS = 128
STEPS = 4
ROWS = 2 * BINS
SLOT = 16
MIB = 1024 * 1024


def make_tables():
    freq = np.arange(PERIOD // 2)[:, None]
    place = np.arange(BLOCK)[None, :]
    angle = math.pi / PERIOD * ((2 * freq + 1) * place % (2 * PERIOD)).astype(np.float64)
    both = np.stack([np.cos(angle), -np.sin(angle)]).reshape(2, BINS, STEPS, BLOCK)
    both = both.transpose(2, 0, 1, 3).reshape(STEPS, ROWS, BLOCK)
    tables = both, both.transpose(0, 2, 1)
    return tuple(np.ascontiguousarray(t).astype(ml_dtypes.bfloat16) for t in tables)


def turn(spec, chunk, block):
    re, im = spec
    eighths = (2 * chunk + 1) * block % 8
    half = math.sqrt(0.5)
    if eighths == 0:
        return re, im
    if eighths == 1:
        return (re + im) * half, (im - re) * half
    if eighths == 2:
        return im, -re
    if eighths == 3:
        return (im - re) * half, (re + im) * -half
    if eighths == 4:
        return -re, -im
    if eighths == 5:
        return (re + im) * -half, (re - im) * half
    if eighths == 6:
        return -im, re
    return (re - im) * half, (re + im) * half


def add(specs):
    return sum(re for re, _ in specs), sum(im for _, im in specs)


def times(a, b):
    return a[0] * b[0] - a[1] * b[1], a[0] * b[1] + a[1] * b[0]


def times_conj(a, b):
    return a[0] * b[0] + a[1] * b[1], a[1] * b[0] - a[0] * b[1]


def transform(table, blocks, chunk, first=0):
    flat = dot(table, blocks)
    count = blocks.shape[1] // LANES
    parts = [flat[:, lane_block(i)] for i in range(count)]
    return [turn((p[:BINS], p[BINS:]), chunk, first + i) for i, p in enumerate(parts)]


def stacked(specs):
    return jnp.concatenate([jnp.concatenate(spec, axis=0) for spec in specs], axis=1).astype(BF16)


def fill(blocks, *sources):
    at = 0
    for source in sources:
        for block in range(source.shape[0] // BLOCK):
            blocks[:, lane_block(at)] = source[token_block(block), :]
            at += 1


def dot(a, b):
    return jnp.dot(a, b, preferred_element_type=F32)


def lane_block(index):
    return slice(index * LANES, (index + 1) * LANES)


def lanes_at(index):
    return pl.ds(pl.multiple_of(index * LANES, LANES), LANES)


def rows_at(index):
    return pl.ds(pl.multiple_of(index * BLOCK, BLOCK), BLOCK)


def token_block(index):
    return slice(index * BLOCK, (index + 1) * BLOCK)


def at_hops(kept, near, far):
    return [kept, near.at[0], far.at[0], far.at[1]]


def out_hops(kept, near, far):
    return [kept, near.at[0], far, near.at[1]]


def prep_kernel(place, key, value, out_grad, kept, near, far, pieces):
    for hop, ship in enumerate(out_hops(kept, near, far)):
        at = (slice(None), lanes_at(place[0] ^ hop))
        ship[...] = (key[at].astype(F32) * value[at].astype(F32)).astype(BF16)
    for piece in range(pieces.shape[0]):
        pieces[piece] = out_grad[:, piece * WIDE : (piece + 1) * WIDE]


def pick_kernel(far, near, out):
    out[0] = far[...]
    out[1] = near[1]


def join_kernel(place, kept, near, far, mixed, tail):
    for hop, ship in enumerate(at_hops(kept, near, far)):
        mixed[rows_at(place[0] ^ hop), :] = ship[...]
    tail[...] = mixed[TOKENS - tail.shape[0] :, :]


def conv_kernel(
    scale, place, table, back, halo, mixed, taps, conv, spectrum, response, blocks, filt, held, sems
):
    lags = halo.shape[0]
    reach = lags // BLOCK
    taps_copies = [
        pltpu.make_async_copy(
            taps.at[token_block(j), lanes_at(place[0])],
            filt.at[:, lane_block(j)],
            sems.at[STEPS + j],
        )
        for j in range(reach)
    ]
    for copy in taps_copies:
        copy.start()
    fill(blocks, halo, mixed)
    copies = []
    for chunk in range(STEPS):
        specs = transform(table[chunk], blocks[...], chunk)
        specs = [add(specs[b : b + reach + 1]) for b in range(BLOCKS)]
        held[chunk] = stacked(specs)
        copy = pltpu.make_async_copy(held.at[chunk], spectrum.at[chunk], sems.at[chunk])
        copy.start()
        copies.append(copy)
        if chunk == 0:
            for copy in taps_copies:
                copy.wait()
        resp = add(transform(table[chunk], filt[...], chunk))
        response[chunk] = stacked([resp])
        y = [turn(times(resp, spec), chunk, -(b + reach)) for b, spec in enumerate(specs)]
        part = dot(back[chunk], stacked(y))
        total = total + part if chunk else part
    for block in range(BLOCKS):
        conv[token_block(block), :] = (total[:, lane_block(block)] * scale).astype(BF16)
    for copy in copies:
        copy.wait()


def cross_kernel(
    scale, table, back, grad, spectrum, head, lag_grad, blocks, total, arrived, sems
):
    copies = [
        pltpu.make_async_copy(spectrum.at[chunk], arrived.at[chunk], sems.at[chunk])
        for chunk in range(STEPS)
    ]
    for copy in copies:
        copy.start()
    lags = head.shape[0]
    reach = lags // BLOCK
    head[...] = grad[:lags, :]
    fill(blocks, grad)
    for chunk in range(STEPS):
        specs = transform(table[chunk], blocks[...], chunk, reach)
        copies[chunk].wait()
        terms = []
        for block, spec in enumerate(specs):
            held = arrived[chunk, :, lane_block(block)].astype(F32)
            terms.append(times_conj(spec, (held[:BINS], held[BINS:])))
        term = add(terms)
        part = dot(back[chunk], stacked([turn(term, chunk, -j) for j in range(reach)]))
        summed = summed + part if chunk else part
    for j in range(reach):
        total[token_block(j), :] = summed[:, lane_block(j)] * scale
    total[lags:, :] = jnp.zeros_like(total[lags:, :])
    count = lag_grad.shape[0]
    share = lags // count
    for slot in range(count):
        lag_grad[slot] = total[slot * share : slot * share + SLOT, :].astype(BF16)


def back_kernel(scale, place, table, back, grad, halo, response, conv, *refs):
    outs, (blocks,) = refs[:BLOCKS], refs[BLOCKS:]
    reach = halo.shape[0] // BLOCK
    fill(blocks, grad, halo)
    for chunk in range(STEPS):
        held = response[chunk].astype(F32)
        resp = held[:BINS], held[BINS:]
        specs = transform(table[chunk], blocks[...], chunk)
        specs = [add(specs[b : b + reach + 1]) for b in range(BLOCKS)]
        y = [turn(times_conj(spec, resp), chunk, -b) for b, spec in enumerate(specs)]
        part = dot(back[chunk], stacked(y))
        total = total + part if chunk else part
    blocks[:, :WIDE] = (total * scale).astype(BF16)
    for hop, out in enumerate(outs):
        out[:BLOCK, :] = conv[rows_at(place[0] ^ hop), :]
        out[BLOCK:, :] = blocks[:, lanes_at(place[0] ^ hop)]


def final_kernel(place, *refs):
    ships, refs = refs[:BLOCKS], refs[BLOCKS:]
    cotangent, key, value, parts, gate_grad, key_grad, value_grad, lag_grad = refs
    for hop, ship in enumerate(ships):
        at = (slice(None), lanes_at(place[0] ^ hop))
        conv, back = ship[:BLOCK, :].astype(F32), ship[BLOCK:, :].astype(F32)
        gate_grad[at] = (cotangent[at].astype(F32) * conv).astype(BF16)
        key_grad[at] = (back * value[at].astype(F32)).astype(BF16)
        value_grad[at] = (back * key[at].astype(F32)).astype(BF16)
    for block in range(BLOCKS):
        total = parts[block].astype(F32)
        for source in range(1, parts.shape[0] // BLOCKS):
            total += parts[source * BLOCKS + block].astype(F32)
        lag_grad[:, lane_block(block)] = total[: lag_grad.shape[0]]


def whole(shape):
    return pl.BlockSpec(shape, lambda *_: (0,) * len(shape))


def shaped(shape, dtype=BF16):
    return jax.ShapeDtypeStruct(shape, dtype)


def call(kernel, in_specs, out_specs, out_shape, scratch=(), flops=0, limit=None, scalars=0):
    return pl.pallas_call(
        kernel,
        grid_spec=pltpu.PrefetchScalarGridSpec(
            num_scalar_prefetch=scalars,
            grid=(1,),
            in_specs=in_specs,
            out_specs=out_specs,
            scratch_shapes=scratch,
        ),
        out_shape=out_shape,
        compiler_params=pltpu.CompilerParams(
            dimension_semantics=("arbitrary",), vmem_limit_bytes=limit or VMEM_LIMIT
        ),
        cost_estimate=pl.CostEstimate(flops=flops, bytes_accessed=0, transcendentals=0),
    )


VMEM_LIMIT = 103 * MIB // 2
FINAL_LIMIT = 16 * MIB
PREP_LIMIT = 56 * MIB
CONV_FLOPS = 24_000_000_000
CROSS_FLOPS = 0
JOIN_FLOPS = 0
BACK_FLOPS = 35_000_000_000


def shift(value, steps):
    count = lax.axis_size(RUNS)
    first, last = max(0, -steps), min(count, count - steps)
    return lax.ppermute(value, RUNS, [(i, i + steps) for i in range(first, last)])


def swap(kept, near, far):
    def flip(value, axis):
        return lax.ppermute(value, axis, [(0, 1), (1, 0)])

    near = flip(near, "c")
    far = call(
        pick_kernel,
        [whole(far.shape), whole(near.shape)],
        whole(near.shape),
        shaped(near.shape),
    )(far, near)
    return kept, near, flip(far, "yl")


def swap_direct(ships):
    return [ships[0]] + [
        lax.ppermute(ships[hop], GROUP, [(i, i ^ hop) for i in range(BLOCKS)])
        for hop in range(1, BLOCKS)
    ]


def exchange(value, axes):
    return lax.all_to_all(value, axes, split_axis=0, concat_axis=0, tiled=True)


def body(forward, inverse, gate_input, key_input, value_input, out_grad, filter_taps):
    lags = filter_taps.shape[0]
    held, channels = out_grad.shape
    share = lags // lax.axis_size(CTX)
    norm = 2.0 / PERIOD / lags**0.5
    local = (BLOCK, WIDE)
    ship = (2 * BLOCK, LANES)
    pieces = (channels // WIDE, held, WIDE)
    flat = (TOKENS, LANES)
    reach = (lags, LANES)
    slots = (lags // share, SLOT, LANES)
    scalar = pl.BlockSpec(memory_space=pltpu.SMEM)
    anywhere = pl.BlockSpec(memory_space=pl.ANY)
    place = lax.axis_index(GROUP).reshape(1)

    part = (BLOCK, LANES)
    by_block = (BLOCKS, BLOCK, LANES)
    pair = (2,) + part
    *ships, cotangent = call(
        prep_kernel,
        [scalar] + [whole(local)] * 2 + [whole(out_grad.shape)],
        [whole(part), whole(pair), whole(part), whole(pieces)],
        [shaped(part), shaped(pair), shaped(part), shaped(pieces)],
        limit=PREP_LIMIT,
    )(place, key_input, value_input, out_grad)
    cotangent = exchange(cotangent, CH).reshape(local)
    mixed, tail = call(
        join_kernel,
        [scalar, whole(part), whole(pair), whole(pair)],
        [whole(flat), whole(reach)],
        [shaped(flat), shaped(reach)],
        flops=JOIN_FLOPS,
    )(place, *swap(*ships))
    mixed_halo = shift(tail, 1)
    grad = (cotangent.astype(F32) * gate_input.astype(F32)).astype(BF16)
    grad = exchange(grad.reshape(BLOCK, BLOCKS, LANES).transpose(1, 0, 2), GROUP).reshape(flat)

    table = whole(forward.shape)
    by_bins = (STEPS, ROWS, WIDE)
    filt_bins = (STEPS, ROWS, LANES)
    seven = pltpu.VMEM((BLOCK, WIDE + lags // BLOCK * LANES), BF16)
    conv, spectrum, response = call(
        functools.partial(conv_kernel, norm),
        [
            table,
            table,
            whole(reach),
            whole(flat),
            anywhere,
        ],
        [whole(flat), anywhere, whole(filt_bins)],
        [shaped(flat), shaped(by_bins), shaped(filt_bins)],
        [
            seven,
            pltpu.VMEM((BLOCK, lags // BLOCK * LANES), BF16),
            pltpu.VMEM(by_bins, BF16),
            pltpu.SemaphoreType.DMA((STEPS + lags // BLOCK,)),
        ],
        CONV_FLOPS,
        scalars=1,
    )(place, forward, inverse, mixed_halo, mixed, filter_taps)
    head, lag_grad = call(
        functools.partial(cross_kernel, norm),
        [table, table, whole(flat), anywhere],
        [whole(reach), whole(slots)],
        [shaped(reach), shaped(slots)],
        [
            pltpu.VMEM(local, BF16),
            pltpu.VMEM((lags + SLOT, LANES), F32),
            pltpu.VMEM(by_bins, BF16),
            pltpu.SemaphoreType.DMA((STEPS,)),
        ],
        CROSS_FLOPS,
    )(forward, inverse, grad, spectrum)
    grad_halo = shift(head, -1)
    lag_parts = exchange(lag_grad, CTX)

    ships = call(
        functools.partial(back_kernel, norm),
        [
            scalar,
            table,
            table,
            whole(flat),
            whole(reach),
            whole(filt_bins),
            whole(flat),
        ],
        [whole(ship)] * BLOCKS,
        [shaped(ship)] * BLOCKS,
        [seven],
        BACK_FLOPS,
    )(place, forward, inverse, grad, grad_halo, response, conv)
    gate_grad, key_grad, value_grad, filter_grad = call(
        final_kernel,
        [scalar] + [whole(ship)] * BLOCKS + [whole(local)] * 3 + [whole(slots)],
        [whole(local)] * 3 + [whole((share, WIDE))],
        [shaped(local)] * 3 + [shaped((share, WIDE), F32)],
        limit=FINAL_LIMIT,
    )(place, *swap_direct(ships), cotangent, key_input, value_input, lag_parts)
    return gate_grad, key_grad, value_grad, filter_grad


def solution(mesh):
    split = Mesh(mesh.devices.reshape(SIZES), AXES)
    spans = P(CTX, CH)
    mapped = jax.shard_map(
        body,
        mesh=split,
        in_specs=(P(), P(), spans, spans, spans, P(CTX + CH, None), P(None, CH)),
        out_specs=(spans, spans, spans, spans),
        check_vma=False,
    )

    def run(gate_input, key_input, value_input, out_grad, filter_taps):
        return mapped(*make_tables(), gate_input, key_input, value_input, out_grad, filter_taps)

    return run
```

```python
import functools
import math

import jax
import jax.numpy as jnp
import ml_dtypes
import numpy as np
from jax import lax
from jax.experimental import pallas as pl
from jax.experimental.pallas import tpu as pltpu
from jax.sharding import Mesh, PartitionSpec as P

BF16 = jnp.bfloat16
F32 = jnp.float32
AXES = ("z", "yh", "yl", "c", "x", "zh")
SIZES = (8, 2, 2, 2, 4, 2)
CTX = ("z", "yh", "yl", "c")
GROUP = ("yl", "c")
RUNS = ("z", "yh")
CH = ("x", "zh")

BLOCK = 256
PERIOD = 1024
LANES = 128
BLOCKS = 4
TOKENS = BLOCKS * BLOCK
WIDE = BLOCKS * LANES
BINS = 128
STEPS = 4
ROWS = 2 * BINS
SLOT = 4
MIB = 1024 * 1024


def make_tables():
    freq = np.arange(PERIOD // 2)[:, None]
    place = np.arange(BLOCK)[None, :]
    angle = math.pi / PERIOD * ((2 * freq + 1) * place % (2 * PERIOD)).astype(np.float64)
    both = np.stack([np.cos(angle), -np.sin(angle)]).reshape(2, BINS, STEPS, BLOCK)
    both = both.transpose(2, 0, 1, 3).reshape(STEPS, ROWS, BLOCK)
    tables = both, both.transpose(0, 2, 1)
    return tuple(np.ascontiguousarray(t).astype(ml_dtypes.bfloat16) for t in tables)


def turn(spec, chunk, block):
    re, im = spec
    eighths = (2 * chunk + 1) * block % 8
    half = math.sqrt(0.5)
    if eighths == 0:
        return re, im
    if eighths == 1:
        return (re + im) * half, (im - re) * half
    if eighths == 2:
        return im, -re
    if eighths == 3:
        return (im - re) * half, (re + im) * -half
    if eighths == 4:
        return -re, -im
    if eighths == 5:
        return (re + im) * -half, (re - im) * half
    if eighths == 6:
        return -im, re
    return (re - im) * half, (re + im) * half


def add(specs):
    return sum(re for re, _ in specs), sum(im for _, im in specs)


def times(a, b):
    return a[0] * b[0] - a[1] * b[1], a[0] * b[1] + a[1] * b[0]


def times_conj(a, b):
    return a[0] * b[0] + a[1] * b[1], a[1] * b[0] - a[0] * b[1]


def transform(table, blocks, chunk, first=0):
    flat = dot(table, blocks)
    count = blocks.shape[1] // LANES
    parts = [flat[:, lane_block(i)] for i in range(count)]
    return [turn((p[:BINS], p[BINS:]), chunk, first + i) for i, p in enumerate(parts)]


def stacked(specs):
    return jnp.concatenate([jnp.concatenate(spec, axis=0) for spec in specs], axis=1).astype(BF16)


def fill(blocks, *sources):
    at = 0
    for source in sources:
        for block in range(source.shape[0] // BLOCK):
            blocks[:, lane_block(at)] = source[token_block(block), :]
            at += 1


def dot(a, b):
    return jnp.dot(a, b, preferred_element_type=F32)


def lane_block(index):
    return slice(index * LANES, (index + 1) * LANES)


def lanes_at(index):
    return pl.ds(pl.multiple_of(index * LANES, LANES), LANES)


def rows_at(index):
    return pl.ds(pl.multiple_of(index * BLOCK, BLOCK), BLOCK)


def token_block(index):
    return slice(index * BLOCK, (index + 1) * BLOCK)


def at_hops(kept, near, far):
    return [kept, near.at[0], far.at[0], far.at[1]]


def out_hops(kept, near, far):
    return [kept, near.at[0], far, near.at[1]]


def pieces_kernel(out_grad, pieces, sems):
    copies = []
    for piece in range(pieces.shape[0]):
        source = out_grad.at[:, piece * WIDE : (piece + 1) * WIDE]
        copies.append(pltpu.make_async_copy(source, pieces.at[piece], sems.at[piece]))
        copies[-1].start()
    for copy in copies:
        copy.wait()


def mixed_kernel(place, key, value, kept, near, far):
    for hop, ship in enumerate(out_hops(kept, near, far)):
        at = (slice(None), lanes_at(place[0] ^ hop))
        ship[...] = (key[at].astype(F32) * value[at].astype(F32)).astype(BF16)


def pick_kernel(far, near, out):
    out[0] = far[...]
    out[1] = near[1]


def join_kernel(place, kept, near, far, mixed, tail):
    for hop, ship in enumerate(at_hops(kept, near, far)):
        mixed[rows_at(place[0] ^ hop), :] = ship[...]
    tail[...] = mixed[TOKENS - tail.shape[0] :, :]


def conv_kernel(
    scale, place, table, back, halo, mixed, taps, conv, spectrum, response, blocks, filt, held, sems
):
    lags = halo.shape[0]
    reach = lags // BLOCK
    taps_copies = [
        pltpu.make_async_copy(
            taps.at[token_block(j), lanes_at(place[0])],
            filt.at[:, lane_block(j)],
            sems.at[STEPS + j],
        )
        for j in range(reach)
    ]
    for copy in taps_copies:
        copy.start()
    fill(blocks, halo, mixed)
    copies = []
    for chunk in range(STEPS):
        specs = transform(table[chunk], blocks[...], chunk)
        specs = [add(specs[b : b + reach + 1]) for b in range(BLOCKS)]
        held[chunk] = stacked(specs)
        copy = pltpu.make_async_copy(held.at[chunk], spectrum.at[chunk], sems.at[chunk])
        copy.start()
        copies.append(copy)
        if chunk == 0:
            for copy in taps_copies:
                copy.wait()
        resp = add(transform(table[chunk], filt[...], chunk))
        response[chunk] = stacked([resp])
        y = [turn(times(resp, spec), chunk, -(b + reach)) for b, spec in enumerate(specs)]
        part = dot(back[chunk], stacked(y))
        total = total + part if chunk else part
    for block in range(BLOCKS):
        conv[token_block(block), :] = (total[:, lane_block(block)] * scale).astype(BF16)
    for copy in copies:
        copy.wait()


def cross_kernel(
    scale, table, back, grad, spectrum, head, lag_grad, blocks, total, arrived, sems
):
    copies = [
        pltpu.make_async_copy(spectrum.at[chunk], arrived.at[chunk], sems.at[chunk])
        for chunk in range(STEPS)
    ]
    for copy in copies:
        copy.start()
    lags = head.shape[0]
    reach = lags // BLOCK
    head[...] = grad[:lags, :]
    fill(blocks, grad)
    for chunk in range(STEPS):
        specs = transform(table[chunk], blocks[...], chunk, reach)
        copies[chunk].wait()
        terms = []
        for block, spec in enumerate(specs):
            held = arrived[chunk, :, lane_block(block)].astype(F32)
            terms.append(times_conj(spec, (held[:BINS], held[BINS:])))
        term = add(terms)
        part = dot(back[chunk], stacked([turn(term, chunk, -j) for j in range(reach)]))
        summed = summed + part if chunk else part
    for j in range(reach):
        total[token_block(j), :] = summed[:, lane_block(j)] * scale
    for rows in range(lag_grad.shape[0]):
        lag_grad[rows] = total[rows * SLOT : (rows + 1) * SLOT, :].astype(BF16)


def back_kernel(scale, place, table, back, grad, halo, response, conv, *refs):
    outs, (blocks,) = refs[:BLOCKS], refs[BLOCKS:]
    reach = halo.shape[0] // BLOCK
    fill(blocks, grad, halo)
    for chunk in range(STEPS):
        held = response[chunk].astype(F32)
        resp = held[:BINS], held[BINS:]
        specs = transform(table[chunk], blocks[...], chunk)
        specs = [add(specs[b : b + reach + 1]) for b in range(BLOCKS)]
        y = [turn(times_conj(spec, resp), chunk, -b) for b, spec in enumerate(specs)]
        part = dot(back[chunk], stacked(y))
        total = total + part if chunk else part
    blocks[:, :WIDE] = (total * scale).astype(BF16)
    for hop, out in enumerate(outs):
        out[:BLOCK, :] = conv[rows_at(place[0] ^ hop), :]
        out[BLOCK:, :] = blocks[:, lanes_at(place[0] ^ hop)]


def final_kernel(place, *refs):
    ships, refs = refs[:BLOCKS], refs[BLOCKS:]
    cotangent, key, value, parts, gate_grad, key_grad, value_grad, lag_grad = refs
    for hop, ship in enumerate(ships):
        at = (slice(None), lanes_at(place[0] ^ hop))
        conv, back = ship[:BLOCK, :].astype(F32), ship[BLOCK:, :].astype(F32)
        gate_grad[at] = (cotangent[at].astype(F32) * conv).astype(BF16)
        key_grad[at] = (back * value[at].astype(F32)).astype(BF16)
        value_grad[at] = (back * key[at].astype(F32)).astype(BF16)
    units = lag_grad.shape[0] // SLOT
    for block in range(BLOCKS):
        for unit in range(units):
            at = [source * units + unit for source in range(block, parts.shape[0] // units, BLOCKS)]
            total = sum(parts[i].astype(F32) for i in at)
            lag_grad[unit * SLOT : (unit + 1) * SLOT, lane_block(block)] = total


def whole(shape):
    return pl.BlockSpec(shape, lambda *_: (0,) * len(shape))


def shaped(shape, dtype=BF16):
    return jax.ShapeDtypeStruct(shape, dtype)


def call(kernel, in_specs, out_specs, out_shape, scratch=(), flops=0, limit=None, scalars=0):
    return pl.pallas_call(
        kernel,
        grid_spec=pltpu.PrefetchScalarGridSpec(
            num_scalar_prefetch=scalars,
            grid=(1,),
            in_specs=in_specs,
            out_specs=out_specs,
            scratch_shapes=scratch,
        ),
        out_shape=out_shape,
        compiler_params=pltpu.CompilerParams(
            dimension_semantics=("arbitrary",), vmem_limit_bytes=limit or VMEM_LIMIT
        ),
        cost_estimate=pl.CostEstimate(flops=flops, bytes_accessed=0, transcendentals=0),
    )


VMEM_LIMIT = 103 * MIB // 2
FINAL_LIMIT = 16 * MIB
PREP_LIMIT = 56 * MIB
CONV_FLOPS = 24_000_000_000
CROSS_FLOPS = 0
JOIN_FLOPS = 0
BACK_FLOPS = 35_000_000_000


def shift(value, steps):
    count = lax.axis_size(RUNS)
    first, last = max(0, -steps), min(count, count - steps)
    return lax.ppermute(value, RUNS, [(i, i + steps) for i in range(first, last)])


def swap(kept, near, far):
    def flip(value, axis):
        return lax.ppermute(value, axis, [(0, 1), (1, 0)])

    near = flip(near, "c")
    far = call(
        pick_kernel,
        [whole(far.shape), whole(near.shape)],
        whole(near.shape),
        shaped(near.shape),
    )(far, near)
    return kept, near, flip(far, "yl")


def swap_direct(ships):
    return [ships[0]] + [
        lax.ppermute(ships[hop], GROUP, [(i, i ^ hop) for i in range(BLOCKS)])
        for hop in range(1, BLOCKS)
    ]


def exchange(value, axes):
    return lax.all_to_all(value, axes, split_axis=0, concat_axis=0, tiled=True)


def body(forward, inverse, gate_input, key_input, value_input, out_grad, filter_taps):
    lags = filter_taps.shape[0]
    held, channels = out_grad.shape
    share = lags // lax.axis_size(CTX)
    norm = 2.0 / PERIOD / lags**0.5
    local = (BLOCK, WIDE)
    ship = (2 * BLOCK, LANES)
    pieces = (channels // WIDE, held, WIDE)
    flat = (TOKENS, LANES)
    reach = (lags, LANES)
    slots = (lags // SLOT, SLOT, LANES)
    scalar = pl.BlockSpec(memory_space=pltpu.SMEM)
    anywhere = pl.BlockSpec(memory_space=pl.ANY)
    place = lax.axis_index(GROUP).reshape(1)

    part = (BLOCK, LANES)
    by_block = (BLOCKS, BLOCK, LANES)
    pair = (2,) + part
    cotangent = call(
        pieces_kernel,
        [anywhere],
        anywhere,
        shaped(pieces),
        [pltpu.SemaphoreType.DMA((pieces[0],))],
        limit=PREP_LIMIT,
    )(out_grad)
    ships = call(
        mixed_kernel,
        [scalar] + [whole(local)] * 2,
        [whole(part), whole(pair), whole(part)],
        [shaped(part), shaped(pair), shaped(part)],
    )(place, key_input, value_input)
    cotangent = exchange(cotangent, CH).reshape(local)
    mixed, tail = call(
        join_kernel,
        [scalar, whole(part), whole(pair), whole(pair)],
        [whole(flat), whole(reach)],
        [shaped(flat), shaped(reach)],
        flops=JOIN_FLOPS,
    )(place, *swap(*ships))
    mixed_halo = shift(tail, 1)
    grad = (cotangent.astype(F32) * gate_input.astype(F32)).astype(BF16)
    grad = exchange(grad.reshape(BLOCK, BLOCKS, LANES).transpose(1, 0, 2), GROUP).reshape(flat)

    table = whole(forward.shape)
    by_bins = (STEPS, ROWS, WIDE)
    filt_bins = (STEPS, ROWS, LANES)
    seven = pltpu.VMEM((BLOCK, WIDE + lags // BLOCK * LANES), BF16)
    conv, spectrum, response = call(
        functools.partial(conv_kernel, norm),
        [
            table,
            table,
            whole(reach),
            whole(flat),
            anywhere,
        ],
        [whole(flat), anywhere, whole(filt_bins)],
        [shaped(flat), shaped(by_bins), shaped(filt_bins)],
        [
            seven,
            pltpu.VMEM((BLOCK, lags // BLOCK * LANES), BF16),
            pltpu.VMEM(by_bins, BF16),
            pltpu.SemaphoreType.DMA((STEPS + lags // BLOCK,)),
        ],
        CONV_FLOPS,
        scalars=1,
    )(place, forward, inverse, mixed_halo, mixed, filter_taps)
    head, lag_grad = call(
        functools.partial(cross_kernel, norm),
        [table, table, whole(flat), anywhere],
        [whole(reach), whole(slots)],
        [shaped(reach), shaped(slots)],
        [
            pltpu.VMEM(local, BF16),
            pltpu.VMEM(reach, F32),
            pltpu.VMEM(by_bins, BF16),
            pltpu.SemaphoreType.DMA((STEPS,)),
        ],
        CROSS_FLOPS,
    )(forward, inverse, grad, spectrum)
    grad_halo = shift(head, -1)
    lag_parts = exchange(lag_grad, CTX)

    ships = call(
        functools.partial(back_kernel, norm),
        [
            scalar,
            table,
            table,
            whole(flat),
            whole(reach),
            whole(filt_bins),
            whole(flat),
        ],
        [whole(ship)] * BLOCKS,
        [shaped(ship)] * BLOCKS,
        [seven],
        BACK_FLOPS,
    )(place, forward, inverse, grad, grad_halo, response, conv)
    gate_grad, key_grad, value_grad, filter_grad = call(
        final_kernel,
        [scalar] + [whole(ship)] * BLOCKS + [whole(local)] * 3 + [whole(slots)],
        [whole(local)] * 3 + [whole((share, WIDE))],
        [shaped(local)] * 3 + [shaped((share, WIDE), F32)],
        limit=FINAL_LIMIT,
    )(place, *swap_direct(ships), cotangent, key_input, value_input, lag_parts)
    return gate_grad, key_grad, value_grad, filter_grad


def solution(mesh):
    split = Mesh(mesh.devices.reshape(SIZES), AXES)
    spans = P(CTX, CH)
    mapped = jax.shard_map(
        body,
        mesh=split,
        in_specs=(P(), P(), spans, spans, spans, P(CTX + CH, None), P(None, CH)),
        out_specs=(spans, spans, spans, spans),
        check_vma=False,
    )

    def run(gate_input, key_input, value_input, out_grad, filter_taps):
        return mapped(*make_tables(), gate_input, key_input, value_input, out_grad, filter_taps)

    return run
```

```python
import functools
import math

import jax
import jax.numpy as jnp
import ml_dtypes
import numpy as np
from jax import lax
from jax.experimental import pallas as pl
from jax.experimental.pallas import tpu as pltpu
from jax.sharding import Mesh, PartitionSpec as P

BF16 = jnp.bfloat16
F32 = jnp.float32
AXES = ("z", "yh", "yl", "c", "x", "zh")
SIZES = (8, 2, 2, 2, 4, 2)
CTX = ("z", "yh", "yl", "c")
GROUP = ("yl", "c")
RUNS = ("z", "yh")
CH = ("x", "zh")

BLOCK = 256
PERIOD = 1024
LANES = 128
BLOCKS = 4
TOKENS = BLOCKS * BLOCK
WIDE = BLOCKS * LANES
BINS = 128
STEPS = 4
ROWS = 2 * BINS
SLOT = 4
MIB = 1024 * 1024


def make_tables():
    freq = np.arange(PERIOD // 2)[:, None]
    place = np.arange(BLOCK)[None, :]
    angle = math.pi / PERIOD * ((2 * freq + 1) * place % (2 * PERIOD)).astype(np.float64)
    both = np.stack([np.cos(angle), -np.sin(angle)]).reshape(2, BINS, STEPS, BLOCK)
    both = both.transpose(2, 0, 1, 3).reshape(STEPS, ROWS, BLOCK)
    tables = both, both.transpose(0, 2, 1)
    return tuple(np.ascontiguousarray(t).astype(ml_dtypes.bfloat16) for t in tables)


def turn(spec, chunk, block):
    re, im = spec
    eighths = (2 * chunk + 1) * block % 8
    half = math.sqrt(0.5)
    if eighths == 0:
        return re, im
    if eighths == 1:
        return (re + im) * half, (im - re) * half
    if eighths == 2:
        return im, -re
    if eighths == 3:
        return (im - re) * half, (re + im) * -half
    if eighths == 4:
        return -re, -im
    if eighths == 5:
        return (re + im) * -half, (re - im) * half
    if eighths == 6:
        return -im, re
    return (re - im) * half, (re + im) * half


def add(specs):
    return sum(re for re, _ in specs), sum(im for _, im in specs)


def times(a, b):
    return a[0] * b[0] - a[1] * b[1], a[0] * b[1] + a[1] * b[0]


def times_conj(a, b):
    return a[0] * b[0] + a[1] * b[1], a[1] * b[0] - a[0] * b[1]


def transform(table, blocks, chunk, first=0):
    flat = dot(table, blocks)
    count = blocks.shape[1] // LANES
    parts = [flat[:, lane_block(i)] for i in range(count)]
    return [turn((p[:BINS], p[BINS:]), chunk, first + i) for i, p in enumerate(parts)]


def stacked(specs):
    return jnp.concatenate([jnp.concatenate(spec, axis=0) for spec in specs], axis=1).astype(BF16)


def fill(blocks, *sources):
    at = 0
    for source in sources:
        for block in range(source.shape[0] // BLOCK):
            blocks[:, lane_block(at)] = source[token_block(block), :]
            at += 1


def dot(a, b):
    return jnp.dot(a, b, preferred_element_type=F32)


def lane_block(index):
    return slice(index * LANES, (index + 1) * LANES)


def lanes_at(index):
    return pl.ds(pl.multiple_of(index * LANES, LANES), LANES)


def rows_at(index):
    return pl.ds(pl.multiple_of(index * BLOCK, BLOCK), BLOCK)


def token_block(index):
    return slice(index * BLOCK, (index + 1) * BLOCK)


def at_hops(kept, near, far):
    return [kept, near.at[0], far.at[0], far.at[1]]


def out_hops(kept, near, far):
    return [kept, near.at[0], far, near.at[1]]


def pieces_kernel(out_grad, pieces):
    for piece in range(pieces.shape[0]):
        pieces[piece] = out_grad[:, piece * WIDE : (piece + 1) * WIDE]


def mixed_kernel(place, key, value, kept, near, far):
    for hop, ship in enumerate(out_hops(kept, near, far)):
        at = (slice(None), lanes_at(place[0] ^ hop))
        ship[...] = (key[at].astype(F32) * value[at].astype(F32)).astype(BF16)


def pick_kernel(far, near, out):
    out[0] = far[...]
    out[1] = near[1]


def join_kernel(place, kept, near, far, mixed, tail):
    for hop, ship in enumerate(at_hops(kept, near, far)):
        mixed[rows_at(place[0] ^ hop), :] = ship[...]
    tail[...] = mixed[TOKENS - tail.shape[0] :, :]


def conv_kernel(
    scale, place, table, back, halo, mixed, taps, conv, spectrum, response, blocks, filt, held, sems
):
    lags = halo.shape[0]
    reach = lags // BLOCK
    taps_copies = [
        pltpu.make_async_copy(
            taps.at[token_block(j), lanes_at(place[0])],
            filt.at[:, lane_block(j)],
            sems.at[STEPS + j],
        )
        for j in range(reach)
    ]
    for copy in taps_copies:
        copy.start()
    fill(blocks, halo, mixed)
    copies = []
    for chunk in range(STEPS):
        specs = transform(table[chunk], blocks[...], chunk)
        specs = [add(specs[b : b + reach + 1]) for b in range(BLOCKS)]
        held[chunk] = stacked(specs)
        copy = pltpu.make_async_copy(held.at[chunk], spectrum.at[chunk], sems.at[chunk])
        copy.start()
        copies.append(copy)
        if chunk == 0:
            for copy in taps_copies:
                copy.wait()
        resp = add(transform(table[chunk], filt[...], chunk))
        response[chunk] = stacked([resp])
        y = [turn(times(resp, spec), chunk, -(b + reach)) for b, spec in enumerate(specs)]
        part = dot(back[chunk], stacked(y))
        total = total + part if chunk else part
    for block in range(BLOCKS):
        conv[token_block(block), :] = (total[:, lane_block(block)] * scale).astype(BF16)
    for copy in copies:
        copy.wait()


def cross_kernel(
    scale, table, back, grad, spectrum, head, lag_grad, blocks, total, arrived, sems
):
    copies = [
        pltpu.make_async_copy(spectrum.at[chunk], arrived.at[chunk], sems.at[chunk])
        for chunk in range(STEPS)
    ]
    for copy in copies:
        copy.start()
    lags = head.shape[0]
    reach = lags // BLOCK
    head[...] = grad[:lags, :]
    fill(blocks, grad)
    for chunk in range(STEPS):
        specs = transform(table[chunk], blocks[...], chunk, reach)
        copies[chunk].wait()
        terms = []
        for block, spec in enumerate(specs):
            held = arrived[chunk, :, lane_block(block)].astype(F32)
            terms.append(times_conj(spec, (held[:BINS], held[BINS:])))
        term = add(terms)
        part = dot(back[chunk], stacked([turn(term, chunk, -j) for j in range(reach)]))
        summed = summed + part if chunk else part
    for j in range(reach):
        total[token_block(j), :] = summed[:, lane_block(j)] * scale
    for rows in range(lag_grad.shape[0]):
        lag_grad[rows] = total[rows * SLOT : (rows + 1) * SLOT, :].astype(BF16)


def back_kernel(scale, place, table, back, grad, halo, response, conv, *refs):
    outs, (blocks,) = refs[:BLOCKS], refs[BLOCKS:]
    reach = halo.shape[0] // BLOCK
    fill(blocks, grad, halo)
    for chunk in range(STEPS):
        held = response[chunk].astype(F32)
        resp = held[:BINS], held[BINS:]
        specs = transform(table[chunk], blocks[...], chunk)
        specs = [add(specs[b : b + reach + 1]) for b in range(BLOCKS)]
        y = [turn(times_conj(spec, resp), chunk, -b) for b, spec in enumerate(specs)]
        part = dot(back[chunk], stacked(y))
        total = total + part if chunk else part
    blocks[:, :WIDE] = (total * scale).astype(BF16)
    for hop, out in enumerate(outs):
        out[:BLOCK, :] = conv[rows_at(place[0] ^ hop), :]
        out[BLOCK:, :] = blocks[:, lanes_at(place[0] ^ hop)]


def final_kernel(place, *refs):
    ships, refs = refs[:BLOCKS], refs[BLOCKS:]
    cotangent, key, value, parts, gate_grad, key_grad, value_grad, lag_grad = refs
    for hop, ship in enumerate(ships):
        at = (slice(None), lanes_at(place[0] ^ hop))
        conv, back = ship[:BLOCK, :].astype(F32), ship[BLOCK:, :].astype(F32)
        gate_grad[at] = (cotangent[at].astype(F32) * conv).astype(BF16)
        key_grad[at] = (back * value[at].astype(F32)).astype(BF16)
        value_grad[at] = (back * key[at].astype(F32)).astype(BF16)
    units = lag_grad.shape[0] // SLOT
    for block in range(BLOCKS):
        for unit in range(units):
            at = [source * units + unit for source in range(block, parts.shape[0] // units, BLOCKS)]
            total = sum(parts[i].astype(F32) for i in at)
            lag_grad[unit * SLOT : (unit + 1) * SLOT, lane_block(block)] = total


def whole(shape):
    return pl.BlockSpec(shape, lambda *_: (0,) * len(shape))


def shaped(shape, dtype=BF16):
    return jax.ShapeDtypeStruct(shape, dtype)


def call(kernel, in_specs, out_specs, out_shape, scratch=(), flops=0, limit=None, scalars=0):
    return pl.pallas_call(
        kernel,
        grid_spec=pltpu.PrefetchScalarGridSpec(
            num_scalar_prefetch=scalars,
            grid=(1,),
            in_specs=in_specs,
            out_specs=out_specs,
            scratch_shapes=scratch,
        ),
        out_shape=out_shape,
        compiler_params=pltpu.CompilerParams(
            dimension_semantics=("arbitrary",), vmem_limit_bytes=limit or VMEM_LIMIT
        ),
        cost_estimate=pl.CostEstimate(flops=flops, bytes_accessed=0, transcendentals=0),
    )


VMEM_LIMIT = 103 * MIB // 2
FINAL_LIMIT = 16 * MIB
PREP_LIMIT = 56 * MIB
CONV_FLOPS = 24_000_000_000
CROSS_FLOPS = 0
JOIN_FLOPS = 0
BACK_FLOPS = 35_000_000_000


def shift(value, steps):
    count = lax.axis_size(RUNS)
    first, last = max(0, -steps), min(count, count - steps)
    return lax.ppermute(value, RUNS, [(i, i + steps) for i in range(first, last)])


def swap(kept, near, far):
    def flip(value, axis):
        return lax.ppermute(value, axis, [(0, 1), (1, 0)])

    near = flip(near, "c")
    far = call(
        pick_kernel,
        [whole(far.shape), whole(near.shape)],
        whole(near.shape),
        shaped(near.shape),
    )(far, near)
    return kept, near, flip(far, "yl")


def swap_direct(ships):
    return [ships[0]] + [
        lax.ppermute(ships[hop], GROUP, [(i, i ^ hop) for i in range(BLOCKS)])
        for hop in range(1, BLOCKS)
    ]


def exchange(value, axes):
    return lax.all_to_all(value, axes, split_axis=0, concat_axis=0, tiled=True)


def body(forward, inverse, gate_input, key_input, value_input, out_grad, filter_taps):
    lags = filter_taps.shape[0]
    held, channels = out_grad.shape
    share = lags // lax.axis_size(CTX)
    norm = 2.0 / PERIOD / lags**0.5
    local = (BLOCK, WIDE)
    ship = (2 * BLOCK, LANES)
    pieces = (channels // WIDE, held, WIDE)
    flat = (TOKENS, LANES)
    reach = (lags, LANES)
    slots = (lags // SLOT, SLOT, LANES)
    scalar = pl.BlockSpec(memory_space=pltpu.SMEM)
    anywhere = pl.BlockSpec(memory_space=pl.ANY)
    place = lax.axis_index(GROUP).reshape(1)

    part = (BLOCK, LANES)
    by_block = (BLOCKS, BLOCK, LANES)
    pair = (2,) + part
    cotangent = call(
        pieces_kernel,
        [whole(out_grad.shape)],
        whole(pieces),
        shaped(pieces),
        limit=PREP_LIMIT,
    )(out_grad)
    ships = call(
        mixed_kernel,
        [scalar] + [whole(local)] * 2,
        [whole(part), whole(pair), whole(part)],
        [shaped(part), shaped(pair), shaped(part)],
    )(place, key_input, value_input)
    cotangent = exchange(cotangent, CH).reshape(local)
    mixed, tail = call(
        join_kernel,
        [scalar, whole(part), whole(pair), whole(pair)],
        [whole(flat), whole(reach)],
        [shaped(flat), shaped(reach)],
        flops=JOIN_FLOPS,
    )(place, *swap(*ships))
    mixed_halo = shift(tail, 1)
    grad = (cotangent.astype(F32) * gate_input.astype(F32)).astype(BF16)
    grad = exchange(grad.reshape(BLOCK, BLOCKS, LANES).transpose(1, 0, 2), GROUP).reshape(flat)

    table = whole(forward.shape)
    by_bins = (STEPS, ROWS, WIDE)
    filt_bins = (STEPS, ROWS, LANES)
    seven = pltpu.VMEM((BLOCK, WIDE + lags // BLOCK * LANES), BF16)
    conv, spectrum, response = call(
        functools.partial(conv_kernel, norm),
        [
            table,
            table,
            whole(reach),
            whole(flat),
            anywhere,
        ],
        [whole(flat), anywhere, whole(filt_bins)],
        [shaped(flat), shaped(by_bins), shaped(filt_bins)],
        [
            seven,
            pltpu.VMEM((BLOCK, lags // BLOCK * LANES), BF16),
            pltpu.VMEM(by_bins, BF16),
            pltpu.SemaphoreType.DMA((STEPS + lags // BLOCK,)),
        ],
        CONV_FLOPS,
        scalars=1,
    )(place, forward, inverse, mixed_halo, mixed, filter_taps)
    head, lag_grad = call(
        functools.partial(cross_kernel, norm),
        [table, table, whole(flat), anywhere],
        [whole(reach), whole(slots)],
        [shaped(reach), shaped(slots)],
        [
            pltpu.VMEM(local, BF16),
            pltpu.VMEM(reach, F32),
            pltpu.VMEM(by_bins, BF16),
            pltpu.SemaphoreType.DMA((STEPS,)),
        ],
        CROSS_FLOPS,
    )(forward, inverse, grad, spectrum)
    grad_halo = shift(head, -1)
    lag_parts = exchange(lag_grad, CTX)

    ships = call(
        functools.partial(back_kernel, norm),
        [
            scalar,
            table,
            table,
            whole(flat),
            whole(reach),
            whole(filt_bins),
            whole(flat),
        ],
        [whole(ship)] * BLOCKS,
        [shaped(ship)] * BLOCKS,
        [seven],
        BACK_FLOPS,
    )(place, forward, inverse, grad, grad_halo, response, conv)
    gate_grad, key_grad, value_grad, filter_grad = call(
        final_kernel,
        [scalar] + [whole(ship)] * BLOCKS + [whole(local)] * 3 + [whole(slots)],
        [whole(local)] * 3 + [whole((share, WIDE))],
        [shaped(local)] * 3 + [shaped((share, WIDE), F32)],
        limit=FINAL_LIMIT,
    )(place, *swap_direct(ships), cotangent, key_input, value_input, lag_parts)
    return gate_grad, key_grad, value_grad, filter_grad


def solution(mesh):
    split = Mesh(mesh.devices.reshape(SIZES), AXES)
    spans = P(CTX, CH)
    mapped = jax.shard_map(
        body,
        mesh=split,
        in_specs=(P(), P(), spans, spans, spans, P(CTX + CH, None), P(None, CH)),
        out_specs=(spans, spans, spans, spans),
        check_vma=False,
    )

    def run(gate_input, key_input, value_input, out_grad, filter_taps):
        return mapped(*make_tables(), gate_input, key_input, value_input, out_grad, filter_taps)

    return run
```

```python
import functools
import math

import jax
import jax.numpy as jnp
import ml_dtypes
import numpy as np
from jax import lax
from jax.experimental import pallas as pl
from jax.experimental.pallas import tpu as pltpu
from jax.sharding import Mesh, PartitionSpec as P

BF16 = jnp.bfloat16
F32 = jnp.float32
AXES = ("z", "yh", "yl", "c", "x", "zh")
SIZES = (8, 2, 2, 2, 4, 2)
CTX = ("z", "yh", "yl", "c")
GROUP = ("yl", "c")
RUNS = ("z", "yh")
CH = ("x", "zh")

BLOCK = 256
PERIOD = 1024
LANES = 128
BLOCKS = 4
TOKENS = BLOCKS * BLOCK
WIDE = BLOCKS * LANES
BINS = 128
STEPS = 4
ROWS = 2 * BINS
SLOT = 4
MIB = 1024 * 1024


def make_tables():
    freq = np.arange(PERIOD // 2)[:, None]
    place = np.arange(BLOCK)[None, :]
    angle = math.pi / PERIOD * ((2 * freq + 1) * place % (2 * PERIOD)).astype(np.float64)
    both = np.stack([np.cos(angle), -np.sin(angle)]).reshape(2, BINS, STEPS, BLOCK)
    both = both.transpose(2, 0, 1, 3).reshape(STEPS, ROWS, BLOCK)
    tables = both, both.transpose(0, 2, 1)
    return tuple(np.ascontiguousarray(t).astype(ml_dtypes.bfloat16) for t in tables)


def turn(spec, chunk, block):
    re, im = spec
    eighths = (2 * chunk + 1) * block % 8
    half = math.sqrt(0.5)
    if eighths == 0:
        return re, im
    if eighths == 1:
        return (re + im) * half, (im - re) * half
    if eighths == 2:
        return im, -re
    if eighths == 3:
        return (im - re) * half, (re + im) * -half
    if eighths == 4:
        return -re, -im
    if eighths == 5:
        return (re + im) * -half, (re - im) * half
    if eighths == 6:
        return -im, re
    return (re - im) * half, (re + im) * half


def add(specs):
    return sum(re for re, _ in specs), sum(im for _, im in specs)


def times(a, b):
    return a[0] * b[0] - a[1] * b[1], a[0] * b[1] + a[1] * b[0]


def times_conj(a, b):
    return a[0] * b[0] + a[1] * b[1], a[1] * b[0] - a[0] * b[1]


def transform(table, blocks, chunk, first=0):
    flat = dot(table, blocks)
    count = blocks.shape[1] // LANES
    parts = [flat[:, lane_block(i)] for i in range(count)]
    return [turn((p[:BINS], p[BINS:]), chunk, first + i) for i, p in enumerate(parts)]


def stacked(specs):
    return jnp.concatenate([jnp.concatenate(spec, axis=0) for spec in specs], axis=1).astype(BF16)


def fill(blocks, *sources):
    at = 0
    for source in sources:
        for block in range(source.shape[0] // BLOCK):
            blocks[:, lane_block(at)] = source[token_block(block), :]
            at += 1


def dot(a, b):
    return jnp.dot(a, b, preferred_element_type=F32)


def lane_block(index):
    return slice(index * LANES, (index + 1) * LANES)


def lanes_at(index):
    return pl.ds(pl.multiple_of(index * LANES, LANES), LANES)


def rows_at(index):
    return pl.ds(pl.multiple_of(index * BLOCK, BLOCK), BLOCK)


def token_block(index):
    return slice(index * BLOCK, (index + 1) * BLOCK)


def at_hops(kept, near, far):
    return [kept, near.at[0], far.at[0], far.at[1]]


def out_hops(kept, near, far):
    return [kept, near.at[0], far, near.at[1]]


def pieces_kernel(out_grad, pieces):
    for piece in range(pieces.shape[0]):
        pieces[piece] = out_grad[:, piece * WIDE : (piece + 1) * WIDE]


def mixed_kernel(place, key, value, kept, near, far):
    for hop, ship in enumerate(out_hops(kept, near, far)):
        at = (slice(None), lanes_at(place[0] ^ hop))
        ship[...] = (key[at].astype(F32) * value[at].astype(F32)).astype(BF16)


def pick_kernel(far, near, out):
    out[0] = far[...]
    out[1] = near[1]


def join_kernel(place, kept, near, far, mixed, tail):
    for hop, ship in enumerate(at_hops(kept, near, far)):
        mixed[rows_at(place[0] ^ hop), :] = ship[...]
    tail[...] = mixed[TOKENS - tail.shape[0] :, :]


def conv_kernel(
    scale, place, table, back, halo, mixed, taps, conv, spectrum, response, blocks, filt, held, sems
):
    lags = halo.shape[0]
    reach = lags // BLOCK
    taps_copies = [
        pltpu.make_async_copy(
            taps.at[token_block(j), lanes_at(place[0])],
            filt.at[:, lane_block(j)],
            sems.at[STEPS + j],
        )
        for j in range(reach)
    ]
    for copy in taps_copies:
        copy.start()
    fill(blocks, halo, mixed)
    copies = []
    for chunk in range(STEPS):
        specs = transform(table[chunk], blocks[...], chunk)
        specs = [add(specs[b : b + reach + 1]) for b in range(BLOCKS)]
        held[chunk] = stacked(specs)
        copy = pltpu.make_async_copy(held.at[chunk], spectrum.at[chunk], sems.at[chunk])
        copy.start()
        copies.append(copy)
        if chunk == 0:
            for copy in taps_copies:
                copy.wait()
        resp = add(transform(table[chunk], filt[...], chunk))
        response[chunk] = stacked([resp])
        y = [turn(times(resp, spec), chunk, -(b + reach)) for b, spec in enumerate(specs)]
        part = dot(back[chunk], stacked(y))
        total = total + part if chunk else part
    for block in range(BLOCKS):
        conv[token_block(block), :] = (total[:, lane_block(block)] * scale).astype(BF16)
    for copy in copies:
        copy.wait()


def cross_kernel(
    scale, table, back, grad, spectrum, head, lag_grad, blocks, total, arrived, sems
):
    copies = [
        pltpu.make_async_copy(spectrum.at[chunk], arrived.at[chunk], sems.at[chunk])
        for chunk in range(STEPS)
    ]
    for copy in copies:
        copy.start()
    lags = head.shape[0]
    reach = lags // BLOCK
    head[...] = grad[:lags, :]
    fill(blocks, grad)
    for chunk in range(STEPS):
        specs = transform(table[chunk], blocks[...], chunk, reach)
        copies[chunk].wait()
        terms = []
        for block, spec in enumerate(specs):
            held = arrived[chunk, :, lane_block(block)].astype(F32)
            terms.append(times_conj(spec, (held[:BINS], held[BINS:])))
        term = add(terms)
        part = dot(back[chunk], stacked([turn(term, chunk, -j) for j in range(reach)]))
        summed = summed + part if chunk else part
    for j in range(reach):
        total[token_block(j), :] = summed[:, lane_block(j)] * scale
    for rows in range(lag_grad.shape[0]):
        lag_grad[rows] = total[rows * SLOT : (rows + 1) * SLOT, :].astype(BF16)


def back_kernel(scale, place, table, back, grad, halo, response, conv, *refs):
    outs, (blocks,) = refs[:BLOCKS], refs[BLOCKS:]
    reach = halo.shape[0] // BLOCK
    fill(blocks, grad, halo)
    for chunk in range(STEPS):
        held = response[chunk].astype(F32)
        resp = held[:BINS], held[BINS:]
        specs = transform(table[chunk], blocks[...], chunk)
        specs = [add(specs[b : b + reach + 1]) for b in range(BLOCKS)]
        y = [turn(times_conj(spec, resp), chunk, -b) for b, spec in enumerate(specs)]
        part = dot(back[chunk], stacked(y))
        total = total + part if chunk else part
    blocks[:, :WIDE] = (total * scale).astype(BF16)
    for hop, out in enumerate(outs):
        out[:BLOCK, :] = conv[rows_at(place[0] ^ hop), :]
        out[BLOCK:, :] = blocks[:, lanes_at(place[0] ^ hop)]


def final_kernel(place, *refs):
    ships, refs = refs[:BLOCKS], refs[BLOCKS:]
    cotangent, key, value, parts, gate_grad, key_grad, value_grad, lag_grad = refs
    for hop, ship in enumerate(ships):
        at = (slice(None), lanes_at(place[0] ^ hop))
        conv, back = ship[:BLOCK, :].astype(F32), ship[BLOCK:, :].astype(F32)
        gate_grad[at] = (cotangent[at].astype(F32) * conv).astype(BF16)
        key_grad[at] = (back * value[at].astype(F32)).astype(BF16)
        value_grad[at] = (back * key[at].astype(F32)).astype(BF16)
    units = lag_grad.shape[0] // SLOT
    for block in range(BLOCKS):
        for unit in range(units):
            at = [source * units + unit for source in range(block, parts.shape[0] // units, BLOCKS)]
            total = sum(parts[i].astype(F32) for i in at)
            lag_grad[unit * SLOT : (unit + 1) * SLOT, lane_block(block)] = total


def whole(shape):
    return pl.BlockSpec(shape, lambda *_: (0,) * len(shape))


def shaped(shape, dtype=BF16):
    return jax.ShapeDtypeStruct(shape, dtype)


def call(kernel, in_specs, out_specs, out_shape, scratch=(), flops=0, limit=None, scalars=0, steps=1):
    return pl.pallas_call(
        kernel,
        grid_spec=pltpu.PrefetchScalarGridSpec(
            num_scalar_prefetch=scalars,
            grid=(steps,),
            in_specs=in_specs,
            out_specs=out_specs,
            scratch_shapes=scratch,
        ),
        out_shape=out_shape,
        compiler_params=pltpu.CompilerParams(
            dimension_semantics=("arbitrary",), vmem_limit_bytes=limit or VMEM_LIMIT
        ),
        cost_estimate=pl.CostEstimate(flops=flops, bytes_accessed=0, transcendentals=0),
    )


VMEM_LIMIT = 103 * MIB // 2
FINAL_LIMIT = 16 * MIB
PREP_LIMIT = 56 * MIB
CONV_FLOPS = 24_000_000_000
CROSS_FLOPS = 0
JOIN_FLOPS = 0
BACK_FLOPS = 35_000_000_000


def shift(value, steps):
    count = lax.axis_size(RUNS)
    first, last = max(0, -steps), min(count, count - steps)
    return lax.ppermute(value, RUNS, [(i, i + steps) for i in range(first, last)])


def swap(kept, near, far):
    def flip(value, axis):
        return lax.ppermute(value, axis, [(0, 1), (1, 0)])

    near = flip(near, "c")
    far = call(
        pick_kernel,
        [whole(far.shape), whole(near.shape)],
        whole(near.shape),
        shaped(near.shape),
    )(far, near)
    return kept, near, flip(far, "yl")


def swap_direct(ships):
    return [ships[0]] + [
        lax.ppermute(ships[hop], GROUP, [(i, i ^ hop) for i in range(BLOCKS)])
        for hop in range(1, BLOCKS)
    ]


def exchange(value, axes):
    return lax.all_to_all(value, axes, split_axis=0, concat_axis=0, tiled=True)


def body(forward, inverse, gate_input, key_input, value_input, out_grad, filter_taps):
    lags = filter_taps.shape[0]
    held, channels = out_grad.shape
    share = lags // lax.axis_size(CTX)
    norm = 2.0 / PERIOD / lags**0.5
    local = (BLOCK, WIDE)
    ship = (2 * BLOCK, LANES)
    pieces = (channels // WIDE, held, WIDE)
    flat = (TOKENS, LANES)
    reach = (lags, LANES)
    slots = (lags // SLOT, SLOT, LANES)
    scalar = pl.BlockSpec(memory_space=pltpu.SMEM)
    anywhere = pl.BlockSpec(memory_space=pl.ANY)
    place = lax.axis_index(GROUP).reshape(1)

    part = (BLOCK, LANES)
    by_block = (BLOCKS, BLOCK, LANES)
    pair = (2,) + part
    cotangent = call(
        pieces_kernel,
        [pl.BlockSpec((held, channels // 2), lambda step: (0, step))],
        pl.BlockSpec((pieces[0] // 2,) + pieces[1:], lambda step: (step, 0, 0)),
        shaped(pieces),
        limit=PREP_LIMIT,
        steps=2,
    )(out_grad)
    ships = call(
        mixed_kernel,
        [scalar] + [whole(local)] * 2,
        [whole(part), whole(pair), whole(part)],
        [shaped(part), shaped(pair), shaped(part)],
    )(place, key_input, value_input)
    cotangent = exchange(cotangent, CH).reshape(local)
    mixed, tail = call(
        join_kernel,
        [scalar, whole(part), whole(pair), whole(pair)],
        [whole(flat), whole(reach)],
        [shaped(flat), shaped(reach)],
        flops=JOIN_FLOPS,
    )(place, *swap(*ships))
    mixed_halo = shift(tail, 1)
    grad = (cotangent.astype(F32) * gate_input.astype(F32)).astype(BF16)
    grad = exchange(grad.reshape(BLOCK, BLOCKS, LANES).transpose(1, 0, 2), GROUP).reshape(flat)

    table = whole(forward.shape)
    by_bins = (STEPS, ROWS, WIDE)
    filt_bins = (STEPS, ROWS, LANES)
    seven = pltpu.VMEM((BLOCK, WIDE + lags // BLOCK * LANES), BF16)
    conv, spectrum, response = call(
        functools.partial(conv_kernel, norm),
        [
            table,
            table,
            whole(reach),
            whole(flat),
            anywhere,
        ],
        [whole(flat), anywhere, whole(filt_bins)],
        [shaped(flat), shaped(by_bins), shaped(filt_bins)],
        [
            seven,
            pltpu.VMEM((BLOCK, lags // BLOCK * LANES), BF16),
            pltpu.VMEM(by_bins, BF16),
            pltpu.SemaphoreType.DMA((STEPS + lags // BLOCK,)),
        ],
        CONV_FLOPS,
        scalars=1,
    )(place, forward, inverse, mixed_halo, mixed, filter_taps)
    head, lag_grad = call(
        functools.partial(cross_kernel, norm),
        [table, table, whole(flat), anywhere],
        [whole(reach), whole(slots)],
        [shaped(reach), shaped(slots)],
        [
            pltpu.VMEM(local, BF16),
            pltpu.VMEM(reach, F32),
            pltpu.VMEM(by_bins, BF16),
            pltpu.SemaphoreType.DMA((STEPS,)),
        ],
        CROSS_FLOPS,
    )(forward, inverse, grad, spectrum)
    grad_halo = shift(head, -1)
    lag_parts = exchange(lag_grad, CTX)

    ships = call(
        functools.partial(back_kernel, norm),
        [
            scalar,
            table,
            table,
            whole(flat),
            whole(reach),
            whole(filt_bins),
            whole(flat),
        ],
        [whole(ship)] * BLOCKS,
        [shaped(ship)] * BLOCKS,
        [seven],
        BACK_FLOPS,
    )(place, forward, inverse, grad, grad_halo, response, conv)
    gate_grad, key_grad, value_grad, filter_grad = call(
        final_kernel,
        [scalar] + [whole(ship)] * BLOCKS + [whole(local)] * 3 + [whole(slots)],
        [whole(local)] * 3 + [whole((share, WIDE))],
        [shaped(local)] * 3 + [shaped((share, WIDE), F32)],
        limit=FINAL_LIMIT,
    )(place, *swap_direct(ships), cotangent, key_input, value_input, lag_parts)
    return gate_grad, key_grad, value_grad, filter_grad


def solution(mesh):
    split = Mesh(mesh.devices.reshape(SIZES), AXES)
    spans = P(CTX, CH)
    mapped = jax.shard_map(
        body,
        mesh=split,
        in_specs=(P(), P(), spans, spans, spans, P(CTX + CH, None), P(None, CH)),
        out_specs=(spans, spans, spans, spans),
        check_vma=False,
    )

    def run(gate_input, key_input, value_input, out_grad, filter_taps):
        return mapped(*make_tables(), gate_input, key_input, value_input, out_grad, filter_taps)

    return run
```
